32 devices in a mesh: dp: 8 (over z, y), blk: 4 (over x, core).
Axes of the slice: x: 2, y: 2, z: 4, core: 2. Of those that a mesh axis runs over, the one named last changes fastest.
Arguments:
- features: bfloat16 [174080, 256], P('dp'), may hold values from -6 to 6
- roi_table: int32 [8, 8192], P(None, ('dp', 'blk')), may hold values from 0 to 192, as said below
- offsets: int32 [2, 32], P(None, 'dp'), may hold values from 0 to 320, as said below
- box_targets: float32 [4, 8192], P(None, ('dp', 'blk')), may hold values from -6 to 6
- first_weight: float32 [12544, 1024], P('dp', 'blk'), may hold values from -0.0546875 to 0.0546875
- first_mean: float32 [12544, 1024], P('dp', 'blk'), may hold values from -0.00048828125 to 0.00048828125
- first_square: float32 [12544, 1024], P('dp', 'blk'), may hold values from 7.6904295e-11 to 3.0517577e-10
- second_weight: float32 [1024, 1024], P('dp', 'blk'), may hold values from -0.1875 to 0.1875
- second_mean: float32 [1024, 1024], P('dp', 'blk'), may hold values from -0.00048828125 to 0.00048828125
- second_square: float32 [1024, 1024], P('dp', 'blk'), may hold values from 1.0986328e-10 to 4.394531e-10
- out_weight: float32 [1024, 85], replicated, may hold values from -0.5 to 0.5
- out_mean: float32 [1024, 85], replicated, may hold values from -0.0029296875 to 0.0029296875
- out_square: float32 [1024, 85], replicated, may hold values from 3.5400392e-09 to 1.4160157e-08
- biases: float32 [2133], replicated, may hold values from -1.5 to 1.5
- bias_mean: float32 [2133], replicated, may hold values from -0.0017089844 to 0.0017089844
- bias_square: float32 [2133], replicated, may hold values from 1.2207031e-09 to 4.8828124e-09
Outputs:
- feature_grads: float32 [174080, 256], P(('dp', 'blk'))
- total_loss: float32 [], replicated
- first_new: float32 [12544, 1024], P('dp', 'blk')
- first_mean_new: float32 [12544, 1024], P('dp', 'blk')
- first_square_new: float32 [12544, 1024], P('dp', 'blk')
- second_new: float32 [1024, 1024], P('dp', 'blk')
- second_mean_new: float32 [1024, 1024], P('dp', 'blk')
- second_square_new: float32 [1024, 1024], P('dp', 'blk')
- out_new: float32 [1024, 85], replicated
- out_mean_new: float32 [1024, 85], replicated
- out_square_new: float32 [1024, 85], replicated
- bias_new: float32 [2133], replicated
- bias_mean_new: float32 [2133], replicated
- bias_square_new: float32 [2133], replicated
The draws below stay inside these ranges and needn't reach their ends.
Inputs may be any that keep to these rules, and one draw needn't show every extreme that they name: Rows of roi_table: left, top, right, bottom pixel edges of a box inside its image of 192 pixels a side, right > left and bottom > top; image 0 to 3 within the RoI's canvas; level 0 to 3; label 0 to 80 with 0 background; valid flag 0 or 1. `offsets`: each image of 192 pixels a side lies wholly inside its canvas, images of one canvas do not intersect.
All inputs are finite; a program needn't handle non-finite values.
Results may differ from the reference program's by a relative error of at most 0.018.
Values may be sent and summed in bfloat16 or wider, within the bound.
A program may use at most 320 MiB of HBM per device.

```python
import math
import jax
import jax.numpy as jnp
from jax import lax

C = 256
H = 1024
CLASSES = 81
ROI_DEV = 256
CANVAS = 512
IMAGES = 4
STEP = 10
ROIS = 8192
IMG = 192
CELLS = 21760
ALL_CELLS = 174080
ALL_IMAGES = 32
K1 = 12544
OUTW = 85
NB = 2133
N_DP = 8
N_BLK = 4


def draw_roi_table(key, part):
    key = jax.random.fold_in(key, 11)
    subkeys = jax.random.split(key, 8)
    left_edge = jax.random.randint(subkeys[0], (ROIS,), 0, IMG - 16)
    top_edge = jax.random.randint(subkeys[1], (ROIS,), 0, IMG - 16)
    box_width = jax.random.randint(subkeys[2], (ROIS,), 16, IMG + 1)
    box_height = jax.random.randint(subkeys[3], (ROIS,), 16, IMG + 1)
    right_edge = jnp.minimum(left_edge + box_width, IMG).at[0].set(IMG)
    bottom_edge = jnp.minimum(top_edge + box_height, IMG)
    image_of = jax.random.randint(subkeys[4], (ROIS,), 0, IMAGES)
    level_of = jax.random.randint(subkeys[5], (ROIS,), 0, 4)
    label_of = jax.random.randint(subkeys[6], (ROIS,), 0, CLASSES).at[0].set(CLASSES - 1)
    device = jnp.arange(ROIS, dtype=jnp.int32) // ROI_DEV
    blk_pos = device % N_BLK
    dp_pos = device // N_BLK
    thresh = 200 + 400 * blk_pos // max(N_BLK - 1, 1) + 400 * dp_pos // max(N_DP - 1, 1)
    valid_of = (jax.random.randint(subkeys[7], (ROIS,), 0, 1000) < thresh).astype(jnp.int32)
    return jnp.stack((left_edge, top_edge, right_edge, bottom_edge, image_of, level_of, label_of, valid_of)).astype(jnp.int32)


def draw_offsets(key, part):
    key = jax.random.fold_in(key, 23)
    slack = jax.random.randint(key, (2, ALL_IMAGES), 0, CANVAS // 8 + 1)
    slot_of = jnp.arange(ALL_IMAGES, dtype=jnp.int32) % IMAGES
    quad_row = slot_of // 2 % 2 * (CANVAS // 2)
    quad_col = slot_of % 2 * (CANVAS // 2)
    placed = jnp.stack((quad_row, quad_col)) + slack
    placed = placed.at[:, 0].set(0).at[:, -1].set(CANVAS - IMG)
    return placed.astype(jnp.int32)


def steps_of(stream_key, shape, pieces, least, high):
    loudness, own = 1.0, jax.random.fold_in(stream_key, 6)
    for dim, parts in pieces:
        steps = jnp.exp(jax.random.uniform(jax.random.fold_in(own, dim), (parts,), jnp.float32, least / len(pieces), high / len(pieces)))
        loudness = loudness * jnp.repeat(steps, shape[dim] // parts).reshape([-1 if axis == dim else 1 for axis in range(len(shape))])
    return loudness


def centred(key, shape, width, reach, cuts=(), held_as=jnp.bfloat16):
    level = steps_of(key, shape, cuts, -0.22, 0.18) if cuts else 1.0
    entries = jax.random.normal(key, shape, jnp.float32) * width * level
    return jnp.minimum(jnp.maximum(entries, -reach), reach).astype(held_as)


def setup_inputs(seed: int = 0) -> dict:
    key_list = jax.random.split(jax.random.key(seed), 17)
    features = centred(key_list[0], (ALL_CELLS, C), 1.0, 6.0, ((0, 8),))
    roi_table = draw_roi_table(jax.random.fold_in(key_list[16], 71), 0)
    offsets = draw_offsets(jax.random.fold_in(key_list[16], 71), 0)
    box_targets = centred(key_list[3], (4, ROIS), 1.0, 6.0, ((1, 32),), jnp.float32)
    first_weight = centred(key_list[4], (K1, H), K1 ** -0.5, 0.0546875, ((0, 8), (1, 4)), jnp.float32)
    first_mean = centred(key_list[5], (K1, H), (0.0028 / ROIS ** 0.5), 0.00048828125, ((0, 8), (1, 4)), jnp.float32)
    first_square = jnp.clip(jnp.exp(math.log(3.051757735406113e-10) - 1.3783262 * jax.random.uniform(key_list[6], (K1, H), jnp.float32) ** steps_of(key_list[6], (K1, H), ((0, 8), (1, 4)), -0.2, 0.2)), 7.690429543183441e-11, 3.051757735406113e-10)
    second_weight = centred(key_list[7], (H, H), H ** -0.5, 0.1875, ((0, 8), (1, 4)), jnp.float32)
    second_mean = centred(key_list[8], (H, H), (0.0033 / ROIS ** 0.5), 0.00048828125, ((0, 8), (1, 4)), jnp.float32)
    second_square = jnp.clip(jnp.exp(math.log(4.3945311278825727e-10) - 1.3862944 * jax.random.uniform(key_list[9], (H, H), jnp.float32) ** steps_of(key_list[9], (H, H), ((0, 8), (1, 4)), -0.2, 0.2)), 1.0986327819706432e-10, 4.3945311278825727e-10)
    out_weight = centred(key_list[10], (H, OUTW), (H // 8) ** -0.5, 0.5, (), jnp.float32)
    out_mean = centred(key_list[11], (H, OUTW), (0.019 / ROIS ** 0.5), 0.0029296875, (), jnp.float32)
    out_square = jnp.clip(jnp.exp(jax.random.uniform(key_list[12], (H, OUTW), jnp.float32, math.log(3.5400391507067752e-09), math.log(1.4160156602827101e-08))), 3.5400391507067752e-09, 1.4160156602827101e-08)
    biases = centred(key_list[13], (NB,), 0.1, 1.5, (), jnp.float32)
    bias_mean = centred(key_list[14], (NB,), (0.011 / ROIS ** 0.5), 0.0017089844, (), jnp.float32)
    bias_square = jnp.clip(jnp.exp(jax.random.uniform(key_list[15], (NB,), jnp.float32, math.log(1.2207030941624453e-09), math.log(4.882812376649781e-09))), 1.2207030941624453e-09, 4.882812376649781e-09)
    return dict(features=features, roi_table=roi_table, offsets=offsets, box_targets=box_targets, first_weight=first_weight, first_mean=first_mean, first_square=first_square, second_weight=second_weight, second_mean=second_mean, second_square=second_square, out_weight=out_weight, out_mean=out_mean, out_square=out_square, biases=biases, bias_mean=bias_mean, bias_square=bias_square)


@jax.custom_vjp
def low(v):
    return lax.optimization_barrier(v.astype(jnp.bfloat16)).astype(jnp.float32)

@jax.custom_vjp
def low_back(v):
    return v

def low_keep(v):
    return (low(v), None)

def low_pass(kept, grad):
    return (grad,)

def back_keep(v):
    return (v, None)

def back_low(kept, grad):
    return (low(grad),)
low.defvjp(low_keep, low_pass)
low_back.defvjp(back_keep, back_low)
third = 1.0 / 3.0
rate_first = 0.018
rate_second = 0.06
rate_out = 0.18
rate_bias = 0.2

def product(left_side, right_side):
    return jnp.dot(left_side, right_side, precision=lax.Precision.HIGHEST, preferred_element_type=jnp.float32)

def smooth_unit(values):
    return jax.nn.gelu(values, approximate=False)

def sample_table(roi_table, offsets):
    level_of = roi_table[5]
    image_of = roi_table[4]
    choose = (image_of[:, None] == jnp.arange(IMAGES, dtype=jnp.int32)[None, :]).astype(jnp.int32)
    shift_y = lax.optimization_barrier(jnp.sum(choose * offsets[0][None, :], axis=1))
    shift_x = lax.optimization_barrier(jnp.sum(choose * offsets[1][None, :], axis=1))
    grid_side = jnp.right_shift(jnp.full_like(level_of, CANVAS // 4), level_of)
    cell_base = jnp.zeros_like(level_of)
    for finer in range(1, 4):
        prior_side = CANVAS // 4 >> finer - 1
        cell_base = cell_base + jnp.where(level_of >= finer, prior_side * prior_side, 0).astype(jnp.int32)
    stride_px = (4 * jnp.left_shift(jnp.ones_like(level_of), level_of)).astype(jnp.float32)
    centres = (jnp.arange(7, dtype=jnp.float32) + 0.5) / 7.0

    def axis_points(low_edge, high_edge, shift_by):
        start_px = (low_edge + shift_by).astype(jnp.float32)
        extent = (high_edge - low_edge).astype(jnp.float32)
        points = start_px[:, None] + centres[None, :] * extent[:, None]
        limit_max = (grid_side - 1).astype(jnp.float32)[:, None]
        scaled = jnp.clip(points / stride_px[:, None] - 0.5, 0.0, limit_max)
        floor_idx = jnp.minimum(jnp.floor(scaled).astype(jnp.int32), grid_side[:, None] - 2)
        return (floor_idx, scaled - floor_idx.astype(jnp.float32))
    row_low, row_frac = axis_points(roi_table[1], roi_table[3], shift_y)
    col_low, col_frac = axis_points(roi_table[0], roi_table[2], shift_x)
    index_list = []
    weight_list = []
    for corner_row in (0, 1):
        for corner_col in (0, 1):
            cells = cell_base[:, None, None] + (row_low[:, :, None] + corner_row) * grid_side[:, None, None] + col_low[:, None, :] + corner_col
            row_part = row_frac if corner_row == 1 else 1.0 - row_frac
            col_part = col_frac if corner_col == 1 else 1.0 - col_frac
            index_list.append(cells.reshape(-1).astype(jnp.int32))
            weight_list.append((row_part[:, :, None] * col_part[:, None, :]).reshape(-1))
    return (jnp.stack(index_list), jnp.stack(weight_list))

def pool_rows(feature_rows, indices, weights, roi_count):
    pooled_sum = weights[0][:, None] * feature_rows[indices[0]]
    for corner in range(1, 4):
        pooled_sum = pooled_sum + weights[corner][:, None] * feature_rows[indices[corner]]
    return pooled_sum.reshape(roi_count, -1)

def head_loss(head_out, roi_table, box_targets, valid_total):
    logits = head_out[:, :CLASSES]
    deltas = head_out[:, CLASSES:]
    labels = roi_table[6]
    valid_f = roi_table[7].astype(jnp.float32)
    onehot = (labels[:, None] == jnp.arange(CLASSES, dtype=jnp.int32)[None, :]).astype(jnp.float32)
    cross_ent = jax.nn.logsumexp(logits, axis=1) - lax.optimization_barrier(jnp.sum(onehot * logits, axis=1))
    delta_err = deltas - box_targets.T
    absolute = jnp.abs(delta_err)
    huber = jnp.where(absolute < 1.0, 0.5 * delta_err * delta_err, absolute - 0.5)
    foreground = (labels > 0).astype(jnp.float32)
    return jnp.sum(valid_f * (cross_ent + foreground * lax.optimization_barrier(jnp.sum(huber, axis=1)))) / valid_total

def group_loss(params, feature_rows, roi_table, offsets, box_targets, valid_total):
    first_weight, second_weight, out_weight, biases = params
    indices, weights = sample_table(roi_table, offsets)
    pooled = low(pool_rows(feature_rows, indices, weights, roi_table.shape[1]))
    first_pre = low_back(product(pooled, low(first_weight)) + biases[:H])
    first_act = low(smooth_unit(first_pre))
    second_pre = low_back(product(first_act, low(second_weight)) + biases[H:2 * H])
    second_act = low(smooth_unit(second_pre))
    head_out = low_back(product(second_act, low(out_weight)) + biases[2 * H:])
    return head_loss(head_out, roi_table, box_targets, valid_total)

def adamw(weight, gradient, moment, square, step_rate):
    new_mean = 0.9 * moment + 0.1 * gradient
    new_square = 0.999 * square + 0.001 * gradient * gradient
    mean_hat = new_mean / (1.0 - 0.9 ** STEP)
    square_hat = new_square / (1.0 - 0.999 ** STEP)
    new_weight = weight - step_rate * (mean_hat / (jnp.sqrt(square_hat) + 1e-08) + 0.0001 * weight)
    return (new_weight, new_mean, new_square)

def reference(features, roi_table, offsets, box_targets, first_weight, first_mean, first_square, second_weight, second_mean, second_square, out_weight, out_mean, out_square, biases, bias_mean, bias_square):
    valid_total = jnp.maximum(jnp.sum(roi_table[7].astype(jnp.float32)), 1.0)
    params = (first_weight, second_weight, out_weight, biases)
    group_rows = ROIS // N_DP
    feature_all = features.astype(jnp.float32).reshape(N_DP, CELLS, C)
    tables = roi_table.reshape(8, N_DP, group_rows).transpose(1, 0, 2)
    shifts = offsets.reshape(2, N_DP, IMAGES).transpose(1, 0, 2)
    targets = box_targets.reshape(4, N_DP, group_rows).transpose(1, 0, 2)

    def visit(running, slices):
        feature_rows, table_rows, shift_rows, target_rows = slices

        def local_loss(param_set, feature_set):
            return group_loss(param_set, feature_set, table_rows, shift_rows, target_rows, valid_total)
        loss_value, pull_back = jax.vjp(local_loss, params, feature_rows)
        param_grads, feature_grad = pull_back(jnp.ones_like(loss_value))
        updated = jax.tree.map(jnp.add, running, (loss_value, param_grads))
        return (updated, feature_grad)
    start_state = (jnp.zeros((), jnp.float32), jax.tree.map(jnp.zeros_like, params))
    (total_loss, gradients), feature_grads = lax.scan(visit, start_state, (feature_all, tables, shifts, targets))
    feature_grads = feature_grads.reshape(ALL_CELLS, C) * third
    first_grad, second_grad, out_grad, bias_grad = gradients
    first_new, first_mean_new, first_square_new = adamw(first_weight, first_grad, first_mean, first_square, rate_first)
    second_new, second_mean_new, second_square_new = adamw(second_weight, second_grad, second_mean, second_square, rate_second)
    out_new, out_mean_new, out_square_new = adamw(out_weight, out_grad, out_mean, out_square, rate_out)
    bias_new, bias_mean_new, bias_square_new = adamw(biases, bias_grad, bias_mean, bias_square, rate_bias)
    return (feature_grads, total_loss, first_new, first_mean_new, first_square_new, second_new, second_mean_new, second_square_new, out_new, out_mean_new, out_square_new, bias_new, bias_mean_new, bias_square_new)
```

```python
import functools

import jax
import jax.numpy as jnp
import numpy as np
from jax import lax
from jax.experimental import pallas as pl
from jax.experimental.pallas import tpu as pltpu
from jax.sharding import PartitionSpec as P

C = 256
H = 1024
CLASSES = 81
CANVAS = 512
IMAGES = 4
LEVELS = 4
STEP = 10
K1 = 12544
BINS = 49

HALF = 128
SLOTS = 26
KQ = SLOTS * HALF
FAR = -1.0e6
BATCH = 16
LANES = 512
SIDES = (128, 64, 32, 16)
BASES = (0, 16384, 20480, 21504)
WIN_ROWS = (52, 28, 16, 16)
WIN_COLS = (64, 32, 16, 16)
BACK_COLS = (56, 32, 16, 16)
VMEM_LIMIT = 60 * 1024 * 1024
GROUP = 32
OWNED = 13
SHARD = OWNED + 1
AHEAD = H // 2
SWAPPED = 9
LATER = OWNED - SWAPPED
AHEAD_ROWS = (OWNED + 2) * GROUP
MESH = pl.DeviceIdType.MESH

third = 1.0 / 3.0
rate_first = 0.018
rate_second = 0.06
rate_out = 0.18
rate_bias = 0.2


def contract_rows(left_side, right_side):
    return lax.dot_general(
        left_side, right_side, (((0,), (0,)), ((), ())), preferred_element_type=jnp.float32
    )


def contract_cols(left_side, right_side):
    return lax.dot_general(
        left_side, right_side, (((1,), (1,)), ((), ())), preferred_element_type=jnp.float32
    )


def sort_rois(roi_table, box_targets):
    count = roi_table.shape[1]
    key = roi_table[5] * IMAGES + roi_table[4]
    place = jnp.arange(count, dtype=jnp.int32)
    before = (key[None, :] < key[:, None]) | (
        (key[None, :] == key[:, None]) & (place[None, :] < place[:, None])
    )
    rank = jnp.sum(before.astype(jnp.int32), axis=1)
    segments = jnp.arange(LEVELS * IMAGES + 1, dtype=jnp.int32)
    starts = jnp.sum((key[None, :] < segments[:, None]).astype(jnp.int32), axis=1)
    rows = jnp.concatenate((roi_table.astype(jnp.float32), box_targets), axis=0)
    pick = (rank[None, :] == place[:, None]).astype(jnp.float32)
    ordered = lax.dot_general(
        pick, rows, (((1,), (1,)), ((), ())), precision=lax.Precision.HIGHEST
    )
    return ordered[:, :8].astype(jnp.int32).T, ordered[:, 8:], starts


def sample_points(table, offsets, parity):
    level_of = table[5]
    image_of = table[4]
    choose = (image_of[:, None] == jnp.arange(IMAGES, dtype=jnp.int32)[None, :]).astype(jnp.int32)
    shift_y = jnp.sum(choose * offsets[0][None, :], axis=1)
    shift_x = jnp.sum(choose * offsets[1][None, :], axis=1)
    grid_side = jnp.right_shift(jnp.full_like(level_of, CANVAS // 4), level_of)
    stride_px = (4 * jnp.left_shift(jnp.ones_like(level_of), level_of)).astype(jnp.float32)
    bins = 2 * jnp.arange(SLOTS, dtype=jnp.int32) + parity
    inside = bins < BINS
    every = jnp.arange(7, dtype=jnp.int32)

    def axis_points(low_edge, high_edge, shift_by, which, keep):
        centres = (which.astype(jnp.float32) + 0.5) / 7.0
        start_px = (low_edge + shift_by).astype(jnp.float32)
        extent = (high_edge - low_edge).astype(jnp.float32)
        points = start_px[:, None] + centres[None, :] * extent[:, None]
        limit_max = (grid_side - 1).astype(jnp.float32)[:, None]
        scaled = jnp.clip(points / stride_px[:, None] - 0.5, 0.0, limit_max)
        return jnp.where(keep[None, :], scaled, FAR)

    rows = (table[1], table[3], shift_y)
    cols = (table[0], table[2], shift_x)
    return (
        axis_points(*rows, every, every >= 0),
        axis_points(*cols, every, every >= 0),
        axis_points(*rows, bins // 7, inside),
        axis_points(*cols, bins % 7, inside),
    )


def window_lows(offsets):
    lows = []
    for level in range(LEVELS - 1):
        half_stride = 2 << level
        lows.append(jnp.maximum(jnp.right_shift(offsets - half_stride, 2 + level), 0))
    lows.append(jnp.zeros_like(offsets))
    return jnp.stack(lows, axis=1).reshape(-1)


def segment_loop(starts, lows, visit):
    for level in range(LEVELS):

        def image_step(image, carry, level=level):
            segment = level * IMAGES + image
            begin = starts[segment]
            end = starts[segment + 1]
            row_low = lows[level * IMAGES + image]
            col_low = lows[(LEVELS + level) * IMAGES + image]

            @pl.when(end > begin)
            def _():
                visit(level, begin, end, row_low, col_low)

            return carry

        lax.fori_loop(0, IMAGES, image_step, 0)


def hat(distance):
    return jnp.maximum(1.0 - jnp.abs(distance), 0.0)


def pool_kernel(starts, lows, meta, feat_hbm, uv_ref, out_ref, raw, cells, win, acc, sem):
    total = raw.shape[0]
    lane0 = pl.multiple_of(meta[0] * HALF, HALF)
    fetch = pltpu.make_async_copy(feat_hbm.at[:, pl.ds(lane0, HALF)], raw, sem)
    fetch.start()
    count = acc.shape[0]

    def clear(step, carry):
        acc[pl.ds(pl.multiple_of(step * 8, 8), 8), :] = jnp.zeros((8, KQ), jnp.float32)
        return carry

    lax.fori_loop(0, count // 8, clear, 0)
    fetch.wait()

    def widen(step, carry):
        rows = pl.ds(pl.multiple_of(step * 128, 128), 128)
        cells[rows, :] = raw[rows, :].astype(jnp.float32)
        return carry

    lax.fori_loop(0, total // 128, widen, 0)

    def visit(level, begin, end, row_low, col_low):
        side, base = SIDES[level], BASES[level]
        height, width = WIN_ROWS[level], WIN_COLS[level]
        shift = width.bit_length() - 1
        per_tile = HALF // width
        tiles = height // per_tile
        depth = tiles * HALF

        def take(row, carry):
            source = pl.ds(base + (row_low + row) * side + col_low, width)
            target = pl.ds(pl.multiple_of(row * width, width), width)
            win[target, :] = cells[source, :].astype(jnp.bfloat16)
            return carry

        lax.fori_loop(0, height, take, 0)
        row_shift = row_low.astype(jnp.float32)
        col_shift = col_low.astype(jnp.float32)

        def group(parity, step, carry):
            first = pl.multiple_of(step * BATCH, BATCH)
            lane = lax.broadcasted_iota(jnp.int32, (BATCH, HALF), 1)
            lane_row = jnp.right_shift(lane, shift).astype(jnp.float32) + row_shift
            lane_col = jnp.bitwise_and(lane, width - 1).astype(jnp.float32) + col_shift
            roi = first + lax.broadcasted_iota(jnp.int32, (BATCH, HALF), 0)
            mine = (roi >= begin) & (roi < end)
            points = jnp.where(mine, uv_ref[pl.ds(first, BATCH), :], FAR)
            row_at = [points[:, a : a + 1] - lane_row for a in range(7)]
            col_hats = [hat(points[:, 64 + b : 65 + b] - lane_col) for b in range(7)]
            bins = [2 * slot + parity for slot in range(SLOTS)]
            pooled = None
            for begin_tile in range(0, tiles, 4):
                columns = []
                for tile in range(begin_tile, min(begin_tile + 4, tiles)):
                    row_hats = [hat(at - float(tile * per_tile)) for at in row_at]
                    weights = [
                        (row_hats[one // 7] * col_hats[one % 7]).astype(jnp.bfloat16)
                        if one < BINS
                        else jnp.zeros((BATCH, HALF), jnp.bfloat16)
                        for one in bins
                    ]
                    columns.append(jnp.concatenate(weights, axis=0))
                part = jnp.dot(
                    jnp.concatenate(columns, axis=1),
                    win[begin_tile * HALF : (begin_tile + len(columns)) * HALF, :],
                    preferred_element_type=jnp.float32,
                )
                pooled = part if pooled is None else pooled + part
            for slot in range(SLOTS):
                where = (pl.ds(first, BATCH), slice(slot * HALF, (slot + 1) * HALF))
                acc[where] = acc[where] + pooled[slot * BATCH : (slot + 1) * BATCH, :]
            return carry

        for parity in (0, 1):

            @pl.when(meta[1] == parity)
            def _(parity=parity):
                lax.fori_loop(
                    begin // BATCH, (end + BATCH - 1) // BATCH, functools.partial(group, parity), 0
                )

    segment_loop(starts, lows, visit)

    def narrow(step, carry):
        rows = pl.ds(pl.multiple_of(step * 16, 16), 16)
        out_ref[rows, :] = acc[rows, :].astype(jnp.bfloat16)
        return carry

    lax.fori_loop(0, count // 16, narrow, 0)


def pool(features, meta, starts, lows, points):
    count = points.shape[0]
    cells = features.shape[0]
    return pl.pallas_call(
        pool_kernel,
        out_shape=jax.ShapeDtypeStruct((count, KQ), jnp.bfloat16),
        in_specs=[
            pl.BlockSpec(memory_space=pltpu.SMEM),
            pl.BlockSpec(memory_space=pltpu.SMEM),
            pl.BlockSpec(memory_space=pltpu.SMEM),
            pl.BlockSpec(memory_space=pl.ANY),
            pl.BlockSpec(memory_space=pltpu.VMEM),
        ],
        out_specs=pl.BlockSpec(memory_space=pltpu.VMEM),
        scratch_shapes=[
            pltpu.VMEM((cells, HALF), jnp.bfloat16),
            pltpu.VMEM((cells, HALF), jnp.float32),
            pltpu.VMEM((KQ, HALF), jnp.bfloat16),
            pltpu.VMEM((count, KQ), jnp.float32),
            pltpu.SemaphoreType.DMA,
        ],
        compiler_params=pltpu.CompilerParams(vmem_limit_bytes=VMEM_LIMIT),
        cost_estimate=pl.CostEstimate(
            flops=40_000_000_000, bytes_accessed=13_000_000, transcendentals=0
        ),
        name="pool_bins",
    )(starts, lows, meta, features, points)


def spread_kernel(
    starts,
    lows,
    grad_ref,
    weight_hbm,
    row_ref,
    col_ref,
    out_ref,
    weight_ref,
    pooled,
    cells,
    part,
    row_hat,
    right,
    weight_sem,
):
    total = cells.shape[0]
    fetch = pltpu.make_async_copy(weight_hbm, weight_ref, weight_sem)
    fetch.start()

    def clear(step, carry):
        rows = pl.ds(pl.multiple_of(step * 128, 128), 128)
        cells[rows, :] = jnp.zeros((128, HALF), jnp.float32)
        return carry

    lax.fori_loop(0, total // 128, clear, 0)
    fetch.wait()

    def back_dot(step, carry):
        cols = pl.ds(pl.multiple_of(step * 256, 256), 256)
        pooled[:, cols] = contract_cols(grad_ref[...], weight_ref[cols, :]).astype(jnp.bfloat16)
        return carry

    lax.fori_loop(0, KQ // 256, back_dot, 0)
    right[SLOTS * BATCH :, :] = jnp.zeros((LANES - SLOTS * BATCH, HALF), jnp.bfloat16)

    def visit(level, begin, end, row_low, col_low):
        side, base = SIDES[level], BASES[level]
        height, width = WIN_ROWS[level], BACK_COLS[level]
        chunk = (26, 28, 16, 16)[level]
        row_shift = row_low.astype(jnp.float32)
        col_shift = col_low.astype(jnp.float32)

        def wipe(row, carry):
            rows = pl.ds(pl.multiple_of(row * width, 8), width)
            part[rows, :] = jnp.zeros((width, HALF), jnp.float32)
            return carry

        lax.fori_loop(0, height, wipe, 0)

        def group(step, carry):
            first = pl.multiple_of(step * BATCH, BATCH)
            for slot in range(SLOTS):
                right[slot * BATCH : (slot + 1) * BATCH, :] = pooled[
                    pl.ds(first, BATCH), slot * HALF : (slot + 1) * HALF
                ]
            lane = lax.broadcasted_iota(jnp.int32, (1, LANES), 1)
            roi = first + jnp.bitwise_and(lane, BATCH - 1)
            mine = (roi >= begin) & (roi < end)
            row_at = jnp.where(mine, row_ref[pl.ds(step, 1), :], FAR) - row_shift
            col_at = jnp.where(mine, col_ref[pl.ds(step, 1), :], FAR) - col_shift
            row_hat[...] = hat(
                row_at - lax.broadcasted_iota(jnp.int32, (56, LANES), 0).astype(jnp.float32)
            )
            col_hat = hat(
                col_at - lax.broadcasted_iota(jnp.int32, (width, LANES), 0).astype(jnp.float32)
            )
            for row in range(0, height, chunk):
                left = jnp.concatenate(
                    [col_hat * row_hat[row + one : row + one + 1, :] for one in range(chunk)], axis=0
                ).astype(jnp.bfloat16)
                rows = slice(row * width, (row + chunk) * width)
                part[rows, :] += jnp.dot(left, right[...], preferred_element_type=jnp.float32)
            return carry

        lax.fori_loop(begin // BATCH, (end + BATCH - 1) // BATCH, group, 0)

        def flush(row, carry):
            target = pl.ds(base + (row_low + row) * side + col_low, width)
            source = pl.ds(pl.multiple_of(row * width, 8), width)
            cells[target, :] = cells[target, :] + part[source, :]
            return carry

        lax.fori_loop(0, height, flush, 0)

    segment_loop(starts, lows, visit)

    def narrow(step, carry):
        rows = pl.ds(pl.multiple_of(step * 128, 128), 128)
        out_ref[rows, :] = (cells[rows, :] * third).astype(jnp.bfloat16)
        return carry

    lax.fori_loop(0, total // 128, narrow, 0)


def spread(first_grad, weight, starts, lows, rows_at, cols_at, cells):
    count = first_grad.shape[0]
    return pl.pallas_call(
        spread_kernel,
        out_shape=jax.ShapeDtypeStruct((cells, HALF), jnp.bfloat16),
        in_specs=[
            pl.BlockSpec(memory_space=pltpu.SMEM),
            pl.BlockSpec(memory_space=pltpu.SMEM),
            pl.BlockSpec(memory_space=pltpu.VMEM),
            pl.BlockSpec(memory_space=pl.ANY),
            pl.BlockSpec(memory_space=pltpu.VMEM),
            pl.BlockSpec(memory_space=pltpu.VMEM),
        ],
        out_specs=pl.BlockSpec(memory_space=pltpu.VMEM),
        scratch_shapes=[
            pltpu.VMEM((KQ, H), jnp.bfloat16),
            pltpu.VMEM((count, KQ), jnp.bfloat16),
            pltpu.VMEM((cells, HALF), jnp.float32),
            pltpu.VMEM((WIN_ROWS[0] * BACK_COLS[0], HALF), jnp.float32),
            pltpu.VMEM((56, LANES), jnp.float32),
            pltpu.VMEM((LANES, HALF), jnp.bfloat16),
            pltpu.SemaphoreType.DMA,
        ],
        compiler_params=pltpu.CompilerParams(vmem_limit_bytes=VMEM_LIMIT),
        cost_estimate=pl.CostEstimate(
            flops=40_000_000_000, bytes_accessed=15_000_000, transcendentals=0
        ),
        name="spread_bins",
    )(starts, lows, first_grad, weight, rows_at, cols_at)


def adamw(weight, gradient, moment, square, step_rate):
    new_mean = 0.9 * moment + 0.1 * gradient
    new_square = 0.999 * square + 0.001 * gradient * gradient
    mean_hat = new_mean / (1.0 - 0.9**STEP)
    square_hat = new_square / (1.0 - 0.999**STEP)
    new_weight = weight - step_rate * (mean_hat / (jnp.sqrt(square_hat) + 1e-08) + 0.0001 * weight)
    return (new_weight, new_mean, new_square)


def groups_before(half, parity, index):
    inside = index % 16 - (8 * parity + 4 * half)
    return index // 16 * 4 + jnp.minimum(jnp.maximum(inside, 0), 4)


def group_place(half, parity, slot, part, n_dp):
    span = K1 // GROUP // n_dp

    def earlier(index):
        inside = jnp.bitwise_and(index, 15) - (8 * parity + 4 * half)
        return jnp.right_shift(index, 4) * 4 + jnp.minimum(jnp.maximum(inside, 0), 4)

    group = 8 * (2 * slot + parity) + 4 * half + part
    owner = sum((group >= span * other).astype(jnp.int32) for other in range(1, n_dp))
    return owner, earlier(group) - earlier(owner * span)


def owned_groups(n_dp):
    span = K1 // GROUP // n_dp
    table = np.zeros((n_dp, 4, OWNED), np.int32)
    for owner in range(n_dp):
        for quarter in range(4):
            found = [
                local
                for local in range(span)
                if (owner * span + local) // 8 % 2 == quarter % 2
                and (owner * span + local) % 8 // 4 == quarter // 2
            ]
            table[owner, quarter] = (found + [0] * OWNED)[:OWNED]
    return table


def group_sources(n_dp):
    span = K1 // GROUP // n_dp
    table = np.zeros((n_dp, span), np.int32)
    for owner in range(n_dp):
        met = [0] * 4
        for local in range(span):
            group = owner * span + local
            quarter = group % 8 // 4 * 2 + group // 8 % 2
            table[owner, local] = quarter * OWNED + met[quarter]
            met[quarter] += 1
    return table


def by_groups(n_dp):
    return n_dp == 8


def deal_kernel(table, weight_ref, rois_ref, out_ref):
    base = lax.axis_index("dp") * 4 * OWNED
    for quarter in range(4):

        def step(index, carry, quarter=quarter):
            source = pl.ds(
                pl.multiple_of(table[base + quarter * OWNED + index] * GROUP, GROUP), GROUP
            )
            target = pl.ds(pl.multiple_of(index * GROUP, GROUP), GROUP)
            out_ref[quarter, target, :] = weight_ref[source, :].astype(jnp.bfloat16)
            return carry

        lax.fori_loop(0, OWNED, step, 0)
        out_ref[quarter, OWNED * GROUP :, :] = rois_ref[...]


def gather_quarter(first_weight, second_weight, rois, n_dp):
    cols = first_weight.shape[1]
    second = second_weight.astype(jnp.bfloat16)
    if by_groups(n_dp):
        table = jnp.asarray(owned_groups(n_dp).reshape(-1))
        top = lax.optimization_barrier(rois[8:].astype(jnp.bfloat16))
        rest = rois[8:] - top.astype(jnp.float32)
        middle_term = lax.optimization_barrier(rest.astype(jnp.bfloat16))
        last = (rest - middle_term.astype(jnp.float32)).astype(jnp.bfloat16)
        riders = jnp.concatenate((rois[:8].astype(jnp.bfloat16), top, middle_term, last), axis=0)
        riders = jnp.pad(riders, ((0, GROUP - riders.shape[0]), (0, 0)))
        dealt = pl.pallas_call(
            deal_kernel,
            out_shape=jax.ShapeDtypeStruct((4, SHARD * GROUP, cols), jnp.bfloat16),
            in_specs=[
                pl.BlockSpec(memory_space=pltpu.SMEM),
                pl.BlockSpec(memory_space=pltpu.VMEM),
                pl.BlockSpec(memory_space=pltpu.VMEM),
            ],
            out_specs=pl.BlockSpec(memory_space=pltpu.VMEM),
            name="deal_rows",
        )(table, first_weight, riders)
        swapped = lax.all_to_all(dealt, "blk", split_axis=0, concat_axis=0, tiled=True)
        ridden = swapped[:, OWNED * GROUP :].astype(jnp.float32).transpose(1, 0, 2)
        ridden = ridden.reshape(GROUP, -1)
        all_rois = jnp.concatenate(
            (ridden[:8], (ridden[8:12] + ridden[12:16]) + ridden[16:20]), axis=0
        )
        rows = swapped[:, : OWNED * GROUP].transpose(1, 0, 2).reshape(OWNED * GROUP, -1)
        block = second.reshape(2, 2, GROUP, cols).transpose(0, 2, 1, 3).reshape(2 * GROUP, -1)
        ahead = jnp.concatenate((rows[:, :AHEAD], block), axis=0)
        gathered = lax.all_gather(ahead, "dp", axis=0, tiled=True)
        behind = rows[:, AHEAD:]
        swapped = lax.ppermute(behind, "dp", [(spot, spot ^ 1) for spot in range(n_dp)])
        return (gathered, behind, swapped), all_rois
    all_rois = lax.all_gather(rois, "blk", axis=1, tiled=True)
    rows = lax.all_gather(first_weight.astype(jnp.bfloat16), "dp", axis=0, tiled=True)
    split = jnp.pad(rows.reshape(BINS, C, cols), ((0, 2 * SLOTS - BINS), (0, 0), (0, 0)))
    split = split.reshape(SLOTS, 2, 2, HALF, cols).transpose(2, 1, 0, 3, 4)
    split = split.reshape(4, KQ, cols)
    mine = lax.all_to_all(split, "blk", split_axis=0, concat_axis=0, tiled=True)
    mine = mine.transpose(1, 0, 2).reshape(KQ, -1)
    second = lax.all_gather(second, "dp", axis=0, tiled=True)
    block = second.reshape(4, -1, cols).transpose(1, 0, 2).reshape(-1, 4 * cols)
    rows = jnp.concatenate((mine, block), axis=0)
    return (rows, rows, rows), all_rois


def second_blocks(source, target, column, sem, n_dp):
    owners, rows = (n_dp, GROUP) if by_groups(n_dp) else (1, H // 4)
    copies = []
    for owner in range(owners):
        for part in range(4):
            if by_groups(n_dp):
                first = owner * AHEAD_ROWS + (OWNED + part // 2) * GROUP
                lane = part % 2 * 256
            else:
                first, lane = KQ, part * 256
            copies.append(
                pltpu.make_async_copy(
                    source.at[pl.ds(first, rows), pl.ds(lane, 256)],
                    target.at[pl.ds((owner * 4 + part) * rows, rows), column],
                    sem.at[owner * 4 + part],
                )
            )
    return copies


def owner_rows(half, parity, owner, n_dp):
    span = K1 // GROUP // n_dp
    begin = groups_before(half, parity, owner * span)
    end = groups_before(half, parity, (owner + 1) * span)
    many = pl.ds(pl.multiple_of(begin * GROUP, GROUP), (OWNED - 1) * GROUP)
    last = pl.ds(pl.multiple_of((end - 1) * GROUP, GROUP), GROUP)
    return many, last, end - begin == OWNED


def ahead_copies(source, target, sems, half, parity, n_dp):
    copies = []
    for owner in range(n_dp):
        many, last, full = owner_rows(half, parity, owner, n_dp)
        first, rows = owner * AHEAD_ROWS, (OWNED - 1) * GROUP
        copies.append(
            (
                None,
                pltpu.make_async_copy(
                    source.at[pl.ds(first, rows), :], target.at[many, :], sems.at[2 * owner]
                ),
            )
        )
        copies.append(
            (
                full,
                pltpu.make_async_copy(
                    source.at[pl.ds(first + rows, GROUP), :],
                    target.at[last, :],
                    sems.at[2 * owner + 1],
                ),
            )
        )
    return copies


def whole_copies(source, targets, sems):
    return [
        (
            None,
            pltpu.make_async_copy(
                source.at[pl.ds(0, KQ), pl.ds(half * AHEAD, AHEAD)], target, sems.at[half]
            ),
        )
        for half, target in enumerate(targets)
    ]


def each_copy(copies, action):
    for condition, copy in copies:
        if condition is None:
            action(copy)
        else:

            @pl.when(condition)
            def _(copy=copy):
                action(copy)


def wipe_slots(target, parity):
    target[KQ - HALF :, :] = jnp.zeros((HALF, AHEAD), jnp.bfloat16)

    @pl.when(parity == 1)
    def _():
        target[KQ - 2 * HALF : KQ - HALF, :] = jnp.zeros((HALF, AHEAD), jnp.bfloat16)


def gelu_parts(values):
    cdf = 0.5 * (1.0 + lax.erf(values * np.float32(np.sqrt(0.5))))
    density = jnp.exp(-0.5 * values * values) * np.float32(1.0 / np.sqrt(2.0 * np.pi))
    return values * cdf, cdf + values * density


def middle_kernel(
    n_dp,
    pooled_hbm,
    ahead_hbm,
    behind_hbm,
    swapped_hbm,
    predict_ref,
    bias_ref,
    aux_ref,
    valid_ref,
    all_grad,
    second_out,
    tail_ref,
    ordered_hbm,
    pooled,
    ahead,
    behind,
    second_ref,
    part,
    sent,
    came,
    first_pre,
    second_pre,
    first_act,
    second_act,
    first_grad,
    second_grad,
    valid_came,
    pooled_sem,
    weight_sem,
    own_sem,
    second_sem,
    out_sem,
    up_send,
    up_recv,
    down_send,
    down_recv,
    y_send,
    y_recv,
    valid_send,
    valid_recv,
    send_sem,
    recv_sem,
):
    me = lax.axis_index("blk")
    dp = lax.axis_index("dp")
    peers = [(dp + step) % n_dp for step in range(1, n_dp)] if by_groups(n_dp) else []
    high, low = me // 2, me % 2
    sibling = high * 2 + (1 - low)
    across = (1 - high) * 2 + low
    corner = (1 - high) * 2 + (1 - low)
    rows = part.shape[0]
    quarter = H // 4

    barrier = pltpu.get_barrier_semaphore()
    for other in (sibling, across, corner):
        pl.semaphore_signal(barrier, inc=1, device_id={"blk": other}, device_id_type=MESH)
    for peer in peers:
        pl.semaphore_signal(barrier, inc=1, device_id={"dp": peer}, device_id_type=MESH)

    def hidden_cols(which):
        return pl.ds(pl.multiple_of(which * quarter, quarter), quarter)

    z, y = dp // 2, dp % 2
    partner = 2 * z + 1 - y
    shard = (OWNED - 1) * GROUP

    def shard_pieces(owner):
        many, last, full = owner_rows(high, low, owner, n_dp)
        first = many.start
        return (
            (None, pl.ds(pl.multiple_of(first, GROUP), shard // 2), pl.ds(0, shard // 2)),
            (
                None,
                pl.ds(pl.multiple_of(first + shard // 2, GROUP), shard // 2),
                pl.ds(shard // 2, shard // 2),
            ),
            (full, last, pl.ds(shard, GROUP)),
        )

    def shard_copies(owner, send, recv, index, target, own=False):
        copies = []
        for piece, (condition, place, source) in enumerate(shard_pieces(owner)):
            copies.append(
                (
                    condition,
                    pltpu.make_async_remote_copy(
                        src_ref=behind_hbm.at[source, :] if own else behind.at[place, :],
                        dst_ref=behind.at[place, :],
                        send_sem=send.at[3 * index + piece],
                        recv_sem=recv.at[3 * index + piece],
                        device_id={"dp": target},
                        device_id_type=MESH,
                    ),
                )
            )
        return copies

    def own_shard(action):
        @pl.when(z < 3)
        def _():
            each_copy(shard_copies(dp, up_send, up_recv, 0, dp + 2, True), action)

        @pl.when(z > 0)
        def _():
            each_copy(shard_copies(dp, down_send, down_recv, 0, dp - 2, True), action)

    def relay_shards(distance, took, action):
        def pass_on(owner, send, recv, neighbour, goes_on, place):
            coming = shard_copies(owner, send, recv, distance - 1, neighbour)
            aside = shard_copies(owner, y_send, y_recv, place, partner)
            onward = [None] * len(coming)
            if distance < 3:
                onward = shard_copies(owner, send, recv, distance, neighbour)
            for came_in, on, over in zip(coming, onward, aside):
                each_copy([came_in], took)
                if on is not None:

                    @pl.when(goes_on)
                    def _(on=on):
                        each_copy([on], action)

                each_copy([over], action)

        @pl.when(z >= distance)
        def _():
            pass_on(dp - 2 * distance, up_send, up_recv, dp + 2, z < 3, z - distance)

        @pl.when(z + distance <= 3)
        def _():
            pass_on(dp + 2 * distance, down_send, down_recv, dp - 2, z > 0, z + distance)

    def serve(distance):
        if by_groups(n_dp):
            relay_shards(distance, lambda copy: copy.wait_recv(), lambda copy: copy.start())

    blocks = second_blocks(ahead_hbm, second_ref, hidden_cols(me), second_sem, n_dp)
    for copy in blocks:
        copy.start()
    if by_groups(n_dp):
        early = ahead_copies(ahead_hbm, ahead, weight_sem, high, low, n_dp)
        late = []
        for which, (source_hbm, owner) in enumerate(((behind_hbm, dp), (swapped_hbm, partner))):
            for piece, (condition, place, source) in enumerate(shard_pieces(owner)):
                late.append(
                    (
                        condition,
                        pltpu.make_async_copy(
                            source_hbm.at[source, :],
                            behind.at[place, :],
                            out_sem.at[2 + 3 * which + piece],
                        ),
                    )
                )
        wipe_slots(ahead, low)
        wipe_slots(behind, low)
    else:
        early, late = whole_copies(ahead_hbm, (ahead, behind), weight_sem), []
    each_copy((*early, *late), lambda copy: copy.start())

    def chunk_rows(which):
        return pl.ds(pl.multiple_of(which * rows, 16), rows)

    order = (corner, across, sibling, me)
    chunks = [
        pltpu.make_async_copy(
            pooled_hbm.at[chunk_rows(which), :], pooled.at[chunk_rows(which), :], pooled_sem.at[i]
        )
        for i, which in enumerate(order)
    ]
    for chunk in chunks:
        chunk.start()
    pl.semaphore_wait(barrier, 3 + len(peers))
    counts = [
        pltpu.make_async_remote_copy(
            src_ref=valid_ref,
            dst_ref=valid_came.at[index],
            send_sem=valid_send.at[index],
            recv_sem=valid_recv.at[index],
            device_id={"dp": peer},
            device_id_type=MESH,
        )
        for index, peer in enumerate(peers)
    ]
    if by_groups(n_dp):
        own_shard(lambda copy: copy.start())
    for copy in counts:
        copy.start()

    def remote(source, target, index, other):
        return pltpu.make_async_remote_copy(
            src_ref=source,
            dst_ref=target,
            send_sem=send_sem.at[index],
            recv_sem=recv_sem.at[index],
            device_id={"blk": other},
            device_id_type=MESH,
        )

    for copy in blocks:
        copy.wait()
    mine, theirs = second_ref.at[:, hidden_cols(me)], second_ref.at[:, hidden_cols(across)]
    second_sibling = remote(mine, mine, 3, sibling)
    second_across = remote(mine, mine, 4, across)
    second_forward = remote(theirs, theirs, 5, sibling)
    second_across.start()
    second_sibling.start()

    def in_blocks(count, body):
        def step(index, carry):
            body(index)
            return carry

        lax.fori_loop(0, count, step, 0)

    def block32(step):
        return pl.ds(pl.multiple_of(step * 32, 32), 32)

    def first_half_product(which):
        cols = slice(which * AHEAD, (which + 1) * AHEAD)
        weight = (ahead, behind)[which]
        base = 18 * which
        to_sibling = remote(sent.at[0, :, cols], came.at[0, :, cols], base, sibling)
        to_across = remote(sent.at[1, :, cols], came.at[1, :, cols], base + 1, across)
        to_sibling_last = remote(sent.at[2, :, cols], came.at[2, :, cols], base + 2, sibling)

        def chunk_dot(i):
            if which == 0:
                chunks[i].wait()

            def cols_dot(step):
                lanes = pl.ds(pl.multiple_of(step * 256, 256), 256)
                target = pl.ds(pl.multiple_of(which * AHEAD + step * 256, 256), 256)
                part[:, target] = jnp.dot(
                    pooled[chunk_rows(order[i]), :],
                    weight[:, lanes],
                    preferred_element_type=jnp.float32,
                )

            in_blocks(AHEAD // 256, cols_dot)

        def hand_on(slot, came_slot=None):
            def store(step):
                block = block32(step)
                value = part[block, cols]
                if came_slot is not None:
                    value = value + came[came_slot, block, cols].astype(jnp.float32)
                sent[slot, block, cols] = value.astype(jnp.bfloat16)

            in_blocks(rows // 32, store)

        def step0():
            chunk_dot(0)
            hand_on(0)
            to_sibling.start()

        def step1():
            chunk_dot(1)
            to_sibling.wait_recv()
            hand_on(1, 0)
            to_across.start()

        def step2():
            chunk_dot(2)
            hand_on(2)
            to_sibling_last.start()

        def step3():
            chunk_dot(3)
            to_sibling_last.wait_recv()
            to_across.wait_recv()

            def activate(step):
                block = block32(step)
                value = (
                    part[block, cols]
                    + came[1, block, cols].astype(jnp.float32)
                    + came[2, block, cols].astype(jnp.float32)
                    + bias_ref[0:1, cols]
                )
                first_pre[block, cols] = value
                first_act[block, cols] = gelu_parts(value)[0].astype(jnp.bfloat16)

            in_blocks(rows // 32, activate)

        return (step0, step1, step2, step3), (to_sibling, to_across, to_sibling_last)

    steps, sums = first_half_product(0)
    each_copy(early, lambda copy: copy.wait())
    steps[0]()
    steps[1]()
    serve(1)
    second_across.wait_recv()
    second_forward.start()
    steps[2]()
    serve(2)
    steps[3]()
    serve(3)
    each_copy(late, lambda copy: copy.wait())
    if by_groups(n_dp):
        for place in range(4):

            @pl.when(z != place)
            def _(place=place):
                each_copy(
                    shard_copies(2 * place + 1 - y, y_send, y_recv, place, partner),
                    lambda copy: copy.wait_recv(),
                )
    ordered_copies = [
        pltpu.make_async_copy(
            source, ordered_hbm.at[:, pl.ds(which * AHEAD, AHEAD)], out_sem.at[which]
        )
        for which, source in enumerate((ahead, behind))
    ]
    for copy in ordered_copies:
        copy.start()
    steps, more_sums = first_half_product(1)
    for step in steps:
        step()
    my_rows = chunk_rows(me)
    across_rows = chunk_rows(across)
    second_sibling.wait_recv()
    second_forward.wait_recv()

    def second_dot(step):
        cols = pl.ds(pl.multiple_of(step * 256, 256), 256)
        second_pre[:, cols] = (
            jnp.dot(first_act[...], second_ref[:, cols], preferred_element_type=jnp.float32)
            + bias_ref[1:2, cols]
        )

    in_blocks(H // 256, second_dot)

    def activate_second(step):
        block = block32(step)
        second_act[block, :] = gelu_parts(second_pre[block, :])[0].astype(jnp.bfloat16)

    in_blocks(rows // 32, activate_second)
    head_out = (
        jnp.dot(second_act[...], predict_ref[...], preferred_element_type=jnp.float32)
        + bias_ref[2:3, :HALF]
    )
    lane = lax.broadcasted_iota(jnp.int32, (rows, HALF), 1)
    is_logit = lane < CLASSES
    is_delta = (lane >= CLASSES) & (lane < CLASSES + 4)
    label = aux_ref[:, 0:1]
    valid_total = valid_ref[0:1, 0:1]
    for index, copy in enumerate(counts):
        copy.wait_recv()
        valid_total = valid_total + valid_came[index, 0:1, 0:1]
    share = aux_ref[:, 1:2] / jnp.maximum(valid_total, 1.0)
    foreground = (label > 0.5).astype(jnp.float32)
    onehot = (lane.astype(jnp.float32) == label).astype(jnp.float32)
    top = jnp.max(jnp.where(is_logit, head_out, -jnp.inf), axis=1, keepdims=True)
    exped = jnp.where(is_logit, jnp.exp(jnp.minimum(head_out - top, 0.0)), 0.0)
    exp_sum = jnp.sum(exped, axis=1, keepdims=True)
    chosen = jnp.sum(onehot * head_out, axis=1, keepdims=True)
    error = jnp.where(is_delta, head_out - aux_ref[...], 0.0)
    absolute = jnp.abs(error)
    huber = jnp.where(absolute < 1.0, 0.5 * error * error, absolute - 0.5)
    huber_sum = jnp.sum(jnp.where(is_delta, huber, 0.0), axis=1, keepdims=True)
    loss_rows = share * (jnp.log(exp_sum) + top - chosen + foreground * huber_sum)
    delta_slope = foreground * jnp.minimum(jnp.maximum(error, -1.0), 1.0)
    head_grad = (share * (exped / exp_sum - jnp.where(is_logit, onehot, 0.0) + delta_slope)).astype(
        jnp.bfloat16
    )
    wide = head_grad.astype(jnp.float32)
    lane1 = lax.broadcasted_iota(jnp.int32, (1, HALF), 1)
    head_bias = jnp.sum(wide, axis=0, keepdims=True) + jnp.where(
        lane1 == CLASSES + 4, jnp.sum(loss_rows, axis=0, keepdims=True), 0.0
    )

    def second_back(step):
        cols = pl.ds(pl.multiple_of(step * 256, 256), 256)
        back = contract_cols(head_grad, predict_ref[cols, :])
        second_grad[:, cols] = (back * gelu_parts(second_pre[:, cols])[1]).astype(jnp.bfloat16)

    in_blocks(H // 256, second_back)
    def first_back(step):
        cols = slice(step * quarter, (step + 1) * quarter)
        back = contract_cols(second_grad[...], second_ref[cols, :])
        first_grad[:, cols] = (back * gelu_parts(first_pre[:, cols])[1]).astype(jnp.bfloat16)
        source, target = first_grad.at[:, cols], all_grad.at[my_rows, cols]
        to_other = remote(source, target, 6 + step, across)
        to_twin = remote(source, target, 10 + step, sibling)
        to_other.start()
        to_twin.start()
        relayed = all_grad.at[across_rows, cols]
        return to_other, to_twin, remote(relayed, relayed, 14 + step, sibling)

    grad_copies = [first_back(step) for step in range(4)]
    grad_own = pltpu.make_async_copy(first_grad, all_grad.at[my_rows, :], own_sem.at[2])
    grad_own.start()

    def bias_rows(grads):
        total = jnp.sum(grads[...].astype(jnp.float32), axis=0, keepdims=True)
        return [total[:, i * HALF : (i + 1) * HALF] for i in range(H // HALF)]

    nothing = jnp.zeros((1, HALF), jnp.float32)
    bias_sums = (
        bias_rows(first_grad),
        bias_rows(second_grad),
        [head_bias] + [nothing] * 7,
        [nothing] * 8,
    )
    for step in range(4):
        piece = contract_rows(second_act[:, step * quarter : (step + 1) * quarter], head_grad)
        if by_groups(n_dp):
            for owner in range(n_dp):
                tail_ref[step, owner, :32, :] = piece[owner * 32 : owner * 32 + 32, :]
                tail_ref[step, owner, 32:, :] = jnp.concatenate(
                    [bias_sums[step][owner]] + [nothing] * 7, axis=0
                )
        else:
            tail_ref[step, :quarter, :] = piece
            tail_ref[step, quarter:, :] = jnp.concatenate(bias_sums[step], axis=0)

    for to_other, _, relay in grad_copies:
        to_other.wait_recv()
        relay.start()

    def second_block(step):
        cols = pl.ds(pl.multiple_of(step * 256, 256), 256)
        second_out[:, cols] = contract_rows(first_act[...], second_grad[:, cols]).astype(
            jnp.bfloat16
        )

    in_blocks(H // 256, second_block)
    grad_own.wait()
    for _, to_twin, relay in grad_copies:
        to_twin.wait_recv()
        relay.wait_recv()
    for copy in ordered_copies:
        copy.wait()
    if by_groups(n_dp):

        def sent_off(copy):
            copy.wait_send()

        own_shard(sent_off)
        for distance in (1, 2, 3):
            relay_shards(distance, lambda copy: None, sent_off)
    for copy in (
        *sums,
        *more_sums,
        second_sibling,
        second_across,
        second_forward,
        *(copy for three in grad_copies for copy in three),
        *counts,
    ):
        copy.wait_send()


def middle(pooled, ahead, behind, swapped, predict, bias, aux, valid_here, n_dp):
    count = pooled.shape[0]
    rows = aux.shape[0]
    tail = (4, n_dp, 40, HALF) if by_groups(n_dp) else (4, H // 4 + 8, HALF)
    any_spec = pl.BlockSpec(memory_space=pl.ANY)
    vmem_spec = pl.BlockSpec(memory_space=pltpu.VMEM)
    return pl.pallas_call(
        functools.partial(middle_kernel, n_dp),
        out_shape=(
            jax.ShapeDtypeStruct((count, H), jnp.bfloat16),
            jax.ShapeDtypeStruct((H, H), jnp.bfloat16),
            jax.ShapeDtypeStruct(tail, jnp.float32),
            jax.ShapeDtypeStruct((KQ, H), jnp.bfloat16),
        ),
        in_specs=[any_spec] * 4 + [vmem_spec] * 4,
        out_specs=(any_spec, vmem_spec, vmem_spec, any_spec),
        scratch_shapes=[
            pltpu.VMEM((count, KQ), jnp.bfloat16),
            pltpu.VMEM((KQ, AHEAD), jnp.bfloat16),
            pltpu.VMEM((KQ, AHEAD), jnp.bfloat16),
            pltpu.VMEM((H, H), jnp.bfloat16),
            pltpu.VMEM((rows, H), jnp.float32),
            pltpu.VMEM((3, rows, H), jnp.bfloat16),
            pltpu.VMEM((3, rows, H), jnp.bfloat16),
            pltpu.VMEM((rows, H), jnp.float32),
            pltpu.VMEM((rows, H), jnp.float32),
            pltpu.VMEM((rows, H), jnp.bfloat16),
            pltpu.VMEM((rows, H), jnp.bfloat16),
            pltpu.VMEM((rows, H), jnp.bfloat16),
            pltpu.VMEM((rows, H), jnp.bfloat16),
            pltpu.VMEM((7, 8, HALF), jnp.float32),
            pltpu.SemaphoreType.DMA((4,)),
            pltpu.SemaphoreType.DMA((SLOTS,)),
            pltpu.SemaphoreType.DMA((3,)),
            pltpu.SemaphoreType.DMA((4 * n_dp if by_groups(n_dp) else 4,)),
            pltpu.SemaphoreType.DMA((8,)),
            pltpu.SemaphoreType.DMA((9,)),
            pltpu.SemaphoreType.DMA((9,)),
            pltpu.SemaphoreType.DMA((9,)),
            pltpu.SemaphoreType.DMA((9,)),
            pltpu.SemaphoreType.DMA((12,)),
            pltpu.SemaphoreType.DMA((12,)),
            pltpu.SemaphoreType.DMA((7,)),
            pltpu.SemaphoreType.DMA((7,)),
            pltpu.SemaphoreType.DMA((21,)),
            pltpu.SemaphoreType.DMA((21,)),
        ],
        compiler_params=pltpu.CompilerParams(
            vmem_limit_bytes=VMEM_LIMIT, collective_id=0, has_side_effects=True
        ),
        cost_estimate=pl.CostEstimate(
            flops=9_000_000_000, bytes_accessed=25_000_000, transcendentals=1_500_000
        ),
        name="middle",
    )(pooled, ahead, behind, swapped, predict, bias, aux, valid_here)


def weight_grad_kernel(n_dp, meta, pooled_ref, grad_ref, here_hbm, there_hbm, later_hbm, stage, sems):
    half, parity, y = meta[0], meta[1], meta[2]
    step = pl.program_id(0)
    last = pl.num_programs(0) - 1

    def copies(which):
        buffer = which % 2
        for one in range(256 // GROUP):
            slot = 2 * which + one // 4
            owner, local = group_place(half, parity, slot, one % 4, n_dp)
            row = jnp.right_shift(owner, 1)
            inside = slot < SLOTS - 1 - parity
            here = jnp.bitwise_and(owner, 1) == y
            there = jnp.logical_not(here)
            for condition, target, place in (
                (here, here_hbm, row * OWNED + local),
                (there & (local < SWAPPED), there_hbm, row * SWAPPED + local),
                (there & (local >= SWAPPED), later_hbm, row * LATER + local - SWAPPED),
            ):

                @pl.when(inside & condition)
                def _(target=target, one=one, place=place):
                    rows = pl.ds(pl.multiple_of(place * GROUP, GROUP), GROUP)
                    pltpu.make_async_copy(
                        stage.at[buffer, pl.ds(one * GROUP, GROUP), :],
                        target.at[rows, :],
                        sems.at[buffer, one],
                    ).start()

    def waits(which):
        buffer = which % 2
        for one in range(256 // GROUP):

            @pl.when(2 * which + one // 4 < SLOTS - 1 - parity)
            def _(one=one):
                rows = pl.ds(one * GROUP, GROUP)
                pltpu.make_async_copy(
                    stage.at[buffer, rows, :], here_hbm.at[rows, :], sems.at[buffer, one]
                ).wait()

    @pl.when(step >= 2)
    def _():
        waits(step - 2)

    stage[step % 2] = contract_rows(pooled_ref[...], grad_ref[...]).astype(jnp.bfloat16)
    copies(step)

    @pl.when(step == last)
    def _():
        waits(step - 1)
        waits(step)


def weight_grad(pooled, all_grad, meta, n_dp):
    count = pooled.shape[0]
    shapes = tuple(
        jax.ShapeDtypeStruct((n_dp // 2 * groups * GROUP, H), jnp.bfloat16)
        for groups in (OWNED, SWAPPED, LATER)
    )
    any_spec = pl.BlockSpec(memory_space=pl.ANY)
    return pl.pallas_call(
        functools.partial(weight_grad_kernel, n_dp),
        grid=(SLOTS // 2,),
        out_shape=shapes,
        in_specs=[
            pl.BlockSpec(memory_space=pltpu.SMEM),
            pl.BlockSpec((count, 256), lambda i: (0, i)),
            pl.BlockSpec((count, H), lambda i: (0, 0)),
        ],
        out_specs=(any_spec, any_spec, any_spec),
        scratch_shapes=[
            pltpu.VMEM((2, 256, H), jnp.bfloat16),
            pltpu.SemaphoreType.DMA((2, 256 // GROUP)),
        ],
        compiler_params=pltpu.CompilerParams(vmem_limit_bytes=VMEM_LIMIT),
        cost_estimate=pl.CostEstimate(
            flops=7_000_000_000, bytes_accessed=16_000_000, transcendentals=0
        ),
        name="weight_grad",
    )(meta, pooled, all_grad)


def reduce_kernel(
    n_dp,
    here_hbm,
    swapped_hbm,
    later_hbm,
    tail_ref,
    second_ref,
    cells_hbm,
    home_ref,
    second_out,
    tails_ref,
    kept_hbm,
    far_hbm,
    cells_kept,
    cells_near,
    cells_own,
    cells_sum,
    mine,
    y_came,
    up_came,
    down_came,
    final,
    tail_near,
    tail_mine,
    tail_came,
    second_came,
    tail_send,
    tail_recv,
    second_send,
    second_recv,
    cells_load,
    cells_send,
    cells_recv,
    shard_load,
    y_send,
    y_recv,
    up_send,
    up_recv,
    down_send,
    down_recv,
    home_send,
    home_recv,
):
    dp = lax.axis_index("dp")
    me = lax.axis_index("blk")
    half, parity = me // 2, me % 2
    z, y = dp // 2, dp % 2
    home_rows = OWNED * GROUP
    quarter = H // 4
    sibling, across = me // 2 * 2 + 1 - me % 2, (me + 2) % 4
    others = ((me + 1) % 4, (me + 2) % 4, (me + 3) % 4)
    has_below, has_above = z > 0, z < 3

    barrier = pltpu.get_barrier_semaphore()

    def greet(**where):
        pl.semaphore_signal(barrier, inc=1, device_id=where, device_id_type=MESH)

    peers = tuple((dp + step) % n_dp for step in range(1, n_dp))
    for peer in peers:
        greet(dp=peer)
    for other in others:
        greet(blk=other)

    def order(k):
        near, far = ((3, 3), (2, 0), (1, 2), (0, 1))[k]
        low_side = jnp.where(z % 3 == 0, near, far)
        return jnp.where(z < 2, low_side, 3 - low_side)

    def shard_loads(k):
        target = order(k)
        rows = pl.ds(pl.multiple_of(target * home_rows, GROUP), home_rows)
        some = SWAPPED * GROUP
        swapped = pl.ds(pl.multiple_of(target * some, GROUP), some)
        return [
            pltpu.make_async_copy(here_hbm.at[rows, :], mine.at[target], shard_load.at[2 * k]),
            pltpu.make_async_copy(
                swapped_hbm.at[swapped, :],
                y_came.at[target, pl.ds(0, some)],
                shard_load.at[2 * k + 1],
            ),
        ]

    for k in range(4):
        for copy in shard_loads(k):
            copy.start()
    pl.semaphore_wait(barrier, n_dp + 2)

    def remote(source, target, send, recv, **where):
        return pltpu.make_async_remote_copy(
            src_ref=source,
            dst_ref=target,
            send_sem=send,
            recv_sem=recv,
            device_id=where,
            device_id_type=MESH,
        )

    piece = tail_ref.shape[2]
    nears, seconds = [], []
    for index, other in enumerate(others):
        nears.append(
            remote(
                tail_ref.at[other],
                tail_near.at[index],
                tail_send.at[index],
                tail_recv.at[index],
                blk=other,
            )
        )
        seconds.append(
            remote(
                second_ref.at[:, pl.ds(pl.multiple_of(other * quarter, quarter), quarter)],
                second_came.at[index],
                second_send.at[index],
                second_recv.at[index],
                blk=other,
            )
        )

    quarter_cells = cells_sum.shape[0]

    def cell_rows(which):
        return cells_hbm.at[pl.ds(pl.multiple_of(which * quarter_cells, 16), quarter_cells), :]

    loads, gives = [], []
    for index, chip in enumerate((1 - half, half)):
        loads.append(
            pltpu.make_async_copy(
                cell_rows(2 * chip + parity), cells_own.at[index], cells_load.at[index]
            )
        )
        gives.append(
            remote(
                cell_rows(2 * chip + 1 - parity),
                cells_near.at[index],
                cells_send.at[index],
                cells_recv.at[index],
                blk=sibling,
            )
        )
    kept_out = pltpu.make_async_copy(cells_kept, kept_hbm, cells_load.at[2])
    crossing = remote(cells_sum, far_hbm, cells_send.at[2], cells_recv.at[2], blk=across)
    parts = (pl.ds(0, SWAPPED * GROUP), pl.ds(SWAPPED * GROUP, LATER * GROUP))

    def y_copy(k):
        target = order(k)
        rows = pl.ds(pl.multiple_of(target * LATER * GROUP, GROUP), LATER * GROUP)
        return remote(
            later_hbm.at[rows, :],
            y_came.at[target, parts[1]],
            y_send.at[k],
            y_recv.at[k],
            dp=2 * z + 1 - y,
        )

    for k in range(4):
        y_copy(k).start()
    for copy in (*nears, *seconds, *gives, *loads):
        copy.start()

    def cell_blocks(body):
        def step(index, carry):
            body(pl.ds(pl.multiple_of(index * 160, 160), 160))
            return carry

        lax.fori_loop(0, quarter_cells // 160, step, 0)

    def give_across():
        loads[0].wait()
        gives[0].wait_recv()

        def add(rows):
            cells_sum[rows, :] = (
                cells_own[0, rows, :].astype(jnp.float32)
                + cells_near[0, rows, :].astype(jnp.float32)
            ).astype(jnp.bfloat16)

        cell_blocks(add)
        crossing.start()

    def keep_here():
        loads[1].wait()
        gives[1].wait_recv()

        def add(rows):
            cells_kept[rows, :] = cells_own[1, rows, :].astype(jnp.float32) + cells_near[
                1, rows, :
            ].astype(jnp.float32)

        cell_blocks(add)
        kept_out.start()

    def add_up(target, sources, part):
        first, groups = ((0, SWAPPED), (SWAPPED, LATER))[part]

        def step(index, carry):
            rows = pl.ds(pl.multiple_of((first + index) * GROUP, GROUP), GROUP)
            total = mine[target, rows, :].astype(jnp.float32)
            for ref in sources:
                total = total + ref[target, rows, :].astype(jnp.float32)
            mine[target, rows, :] = total.astype(jnp.bfloat16)
            return carry

        lax.fori_loop(0, groups, step, 0)

    def z_copy(target, part, came, send, recv, neighbour):
        sem = 2 * target + part
        return remote(
            mine.at[target, parts[part]],
            came.at[target, parts[part]],
            send.at[sem],
            recv.at[sem],
            dp=neighbour,
        )

    def up_copy(target, part):
        return z_copy(target, part, up_came, up_send, up_recv, dp + 2)

    def down_copy(target, part):
        return z_copy(target, part, down_came, down_send, down_recv, dp - 2)

    def arrive(k, part):
        if part == 0:
            for copy in shard_loads(k):
                copy.wait()
        else:
            y_copy(k).wait_recv()

    def chain(k, part):
        target = order(k)
        arrive(k, part)

        @pl.when(target > z)
        def _():
            @pl.when(has_below)
            def _():
                up_copy(target, part).wait_recv()
                add_up(target, (y_came, up_came), part)

            @pl.when(jnp.logical_not(has_below))
            def _():
                add_up(target, (y_came,), part)

            up_copy(target, part).start()

        @pl.when(target < z)
        def _():
            @pl.when(has_above)
            def _():
                down_copy(target, part).wait_recv()
                add_up(target, (y_came, down_came), part)

            @pl.when(jnp.logical_not(has_above))
            def _():
                add_up(target, (y_came,), part)

            down_copy(target, part).start()

    def last(part):
        arrive(3, part)
        add_up(z, (y_came,), part)

        @pl.when(has_below)
        def _():
            up_copy(z, part).wait_recv()
            add_up(z, (up_came,), part)

        @pl.when(has_above)
        def _():
            down_copy(z, part).wait_recv()
            add_up(z, (down_came,), part)

    def home_copies(part):
        copies = []
        for index, other in enumerate(others):
            cols = pl.ds(pl.multiple_of(other * quarter, quarter), quarter)
            copies.append(
                remote(
                    mine.at[z, parts[part], cols],
                    final.at[me, parts[part]],
                    home_send.at[3 * part + index],
                    home_recv.at[3 * part + index],
                    blk=other,
                )
            )
        return copies

    chain(0, 0)
    give_across()
    for copy in nears:
        copy.wait_recv()
    tail_mine[...] = tail_ref[me] + tail_near[0] + tail_near[1] + tail_near[2]
    tails = []
    for index, peer in enumerate(peers):
        sem = 3 + index
        tails.append(
            remote(
                tail_mine.at[peer],
                tail_came.at[index],
                tail_send.at[sem],
                tail_recv.at[sem],
                dp=peer,
            )
        )
    for copy in tails:
        copy.start()
    chain(1, 0)
    for copy in tails:
        copy.wait_recv()
    my_tail = pl.ds(pl.multiple_of((me * n_dp + dp) * piece, 8), piece)
    total = tail_mine[dp]
    for index in range(n_dp - 1):
        total = total + tail_came[index]
    tails_ref[my_tail, :] = total
    spreads = []
    for index, peer in enumerate(peers):
        spot = tails_ref.at[my_tail, :]
        sem = n_dp + 2 + index
        spreads.append(remote(spot, spot, tail_send.at[sem], tail_recv.at[sem], dp=peer))
    for copy in spreads:
        copy.start()
    keep_here()
    chain(2, 0)
    last(0)
    homes = home_copies(0)
    for copy in homes:
        copy.start()
    for k in range(3):
        chain(k, 1)
    block = tails_ref.at[pl.ds(pl.multiple_of(me * n_dp * piece, 8), n_dp * piece), :]
    shares = []
    for index, other in enumerate(others):
        sem = 2 * n_dp + 1 + index
        shares.append(remote(block, block, tail_send.at[sem], tail_recv.at[sem], blk=other))
    for copy in spreads:
        copy.wait_recv()
    for copy in shares:
        copy.start()
    own_cols = pl.ds(pl.multiple_of(me * quarter, quarter), quarter)
    second = second_ref[:, own_cols].astype(jnp.float32)
    for index, copy in enumerate(seconds):
        copy.wait_recv()
        second = second + second_came[index].astype(jnp.float32)
    second_out[...] = second
    last(1)
    homes_later = home_copies(1)
    for copy in homes_later:
        copy.start()
    home_ref[pl.ds(pl.multiple_of(me * home_rows, GROUP), home_rows), :] = mine[z, :, own_cols]
    for copy in shares:
        copy.wait_recv()
    for index in range(3):
        sender = (me + 3 - index) % 4
        homes[index].wait_recv()
        homes_later[index].wait_recv()
        rows = pl.ds(pl.multiple_of(sender * home_rows, GROUP), home_rows)
        home_ref[rows, :] = final[sender]
    for copy in (
        *homes,
        *homes_later,
        *nears,
        *tails,
        *spreads,
        *shares,
        *seconds,
        *gives,
        crossing,
        *(y_copy(k) for k in range(4)),
    ):
        copy.wait_send()
    kept_out.wait()
    crossing.wait_recv()
    for k in range(3):
        target = order(k)

        @pl.when(target > z)
        def _():
            up_copy(target, 0).wait_send()
            up_copy(target, 1).wait_send()

        @pl.when(target < z)
        def _():
            down_copy(target, 0).wait_send()
            down_copy(target, 1).wait_send()


def reduce_home(here, swapped, later, tail, second, cell_grads, n_dp):
    home = OWNED * GROUP
    piece = tail.shape[2]
    cells = cell_grads.shape[0] // 4
    vmem_spec = pl.BlockSpec(memory_space=pltpu.VMEM)
    any_spec = pl.BlockSpec(memory_space=pl.ANY)
    shards = pltpu.VMEM((4, home, H), jnp.bfloat16)

    def sems(number):
        return pltpu.SemaphoreType.DMA((number,))

    return pl.pallas_call(
        functools.partial(reduce_kernel, n_dp),
        out_shape=(
            jax.ShapeDtypeStruct((4 * home, H // 4), jnp.bfloat16),
            jax.ShapeDtypeStruct((H // n_dp, H // 4), jnp.float32),
            jax.ShapeDtypeStruct((4 * n_dp * piece, HALF), jnp.float32),
            jax.ShapeDtypeStruct((cells, HALF), jnp.float32),
            jax.ShapeDtypeStruct((cells, HALF), jnp.bfloat16),
        ),
        in_specs=[any_spec, any_spec, any_spec, vmem_spec, vmem_spec, any_spec],
        out_specs=(vmem_spec,) * 3 + (any_spec,) * 2,
        scratch_shapes=[
            pltpu.VMEM((cells, HALF), jnp.float32),
            pltpu.VMEM((2, cells, HALF), jnp.bfloat16),
            pltpu.VMEM((2, cells, HALF), jnp.bfloat16),
            pltpu.VMEM((cells, HALF), jnp.bfloat16),
            shards,
            shards,
            shards,
            shards,
            pltpu.VMEM((4, home, H // 4), jnp.bfloat16),
            pltpu.VMEM((3, n_dp, piece, HALF), jnp.float32),
            pltpu.VMEM((n_dp, piece, HALF), jnp.float32),
            pltpu.VMEM((n_dp - 1, piece, HALF), jnp.float32),
            pltpu.VMEM((3, H // n_dp, H // 4), jnp.bfloat16),
            sems(2 * n_dp + 4),
            sems(2 * n_dp + 4),
            sems(3),
            sems(3),
            sems(3),
            sems(3),
            sems(3),
            sems(8),
            sems(4),
            sems(4),
            sems(8),
            sems(8),
            sems(8),
            sems(8),
            sems(6),
            sems(6),
        ],
        compiler_params=pltpu.CompilerParams(
            vmem_limit_bytes=VMEM_LIMIT, collective_id=1, has_side_effects=True
        ),
        cost_estimate=pl.CostEstimate(
            flops=60_000_000_000, bytes_accessed=200_000_000, transcendentals=0
        ),
        name="reduce_home",
    )(here, swapped, later, tail, second, cell_grads)


def sum_apart(pooled, all_grad, n_blk):
    first_wgrad = contract_rows(pooled, all_grad).astype(jnp.bfloat16)
    split = first_wgrad.reshape(KQ, n_blk, -1).transpose(1, 0, 2)
    mine = lax.all_to_all(split, "blk", split_axis=0, concat_axis=0, tiled=True)
    cols = mine.shape[2]
    mine = mine.reshape(2, 2, SLOTS, HALF, cols).transpose(2, 1, 0, 3, 4)
    mine = mine.reshape(2 * SLOTS, C, cols)[:BINS].reshape(K1, cols)
    first_sum = lax.psum_scatter(mine, "dp", scatter_dimension=0, tiled=True).astype(jnp.float32)
    return first_sum


def finish_kernel(
    table,
    home_ref,
    weight_ref,
    mean_ref,
    square_ref,
    kept_ref,
    far_ref,
    new_ref,
    new_mean_ref,
    new_square_ref,
    features_ref,
):
    groups = weight_ref.shape[0] // GROUP
    span = K1 // GROUP // lax.axis_size("dp")
    base = lax.axis_index("dp") * span + pl.program_id(0) * groups
    my_half = lax.axis_index("blk") // 2
    for index in range(groups):
        source = pl.ds(pl.multiple_of(table[base + index] * GROUP, GROUP), GROUP)
        rows = slice(index * GROUP, (index + 1) * GROUP)
        updated = adamw(
            weight_ref[rows, :],
            home_ref[source, :].astype(jnp.float32),
            mean_ref[rows, :],
            square_ref[rows, :],
            rate_first,
        )
        new_ref[rows, :], new_mean_ref[rows, :], new_square_ref[rows, :] = updated
    for half in range(2):

        @pl.when(my_half == half)
        def _(half=half):
            features_ref[:, half * HALF : (half + 1) * HALF] = kept_ref[...]
            features_ref[:, (1 - half) * HALF : (2 - half) * HALF] = far_ref[...].astype(
                jnp.float32
            )


def finish(home, kept, far, first_weight, first_mean, first_square, n_dp):
    cols = first_weight.shape[1]
    steps = 7
    table = jnp.asarray(group_sources(n_dp).reshape(-1))
    block = pl.BlockSpec((first_weight.shape[0] // steps, cols), lambda i: (i, 0))
    shape = jax.ShapeDtypeStruct(first_weight.shape, jnp.float32)
    cells = kept.shape[0]
    some = -(-cells // steps // 16) * 16
    part = pl.BlockSpec((some, HALF), lambda i: (i, 0))
    return pl.pallas_call(
        finish_kernel,
        grid=(steps,),
        out_shape=(shape, shape, shape, jax.ShapeDtypeStruct((cells, C), jnp.float32)),
        in_specs=[
            pl.BlockSpec(memory_space=pltpu.SMEM),
            pl.BlockSpec(memory_space=pltpu.VMEM),
            block,
            block,
            block,
            part,
            part,
        ],
        out_specs=(block, block, block, pl.BlockSpec((some, C), lambda i: (i, 0))),
        compiler_params=pltpu.CompilerParams(vmem_limit_bytes=VMEM_LIMIT),
        name="finish",
    )(table, home, first_weight, first_mean, first_square, kept, far)


def on_device(
    features,
    roi_table,
    offsets,
    box_targets,
    first_weight,
    first_mean,
    first_square,
    second_weight,
    second_mean,
    second_square,
    out_weight,
    out_mean,
    out_square,
    biases,
    bias_mean,
    bias_square,
    n_dp,
    n_blk,
):
    place = lax.axis_index("blk")
    half = place // 2
    parity = place % 2
    roi_count = roi_table.shape[1]
    outw = out_weight.shape[1]
    rois = jnp.concatenate((roi_table.astype(jnp.float32), box_targets), axis=0)
    weight, all_rois = gather_quarter(first_weight, second_weight, rois, n_dp)
    valid_here = jnp.broadcast_to(jnp.sum(all_rois[7]), (8, HALF))
    if not by_groups(n_dp):
        valid_here = lax.psum(valid_here, "dp")
    predict = jnp.pad(out_weight.astype(jnp.bfloat16), ((0, 0), (0, HALF - outw)))
    bias = jnp.zeros((8, H), jnp.float32)
    bias = bias.at[0].set(biases[:H]).at[1].set(biases[H : 2 * H]).at[2, :outw].set(biases[2 * H :])

    table, targets, starts = sort_rois(all_rois[:8].astype(jnp.int32), all_rois[8:])
    lows = window_lows(offsets)
    row_sevens, col_sevens, rows_at, cols_at = sample_points(table, offsets, parity)
    apart = ((0, 0), (0, 64 - 7))
    points = jnp.concatenate((jnp.pad(row_sevens, apart), jnp.pad(col_sevens, apart)), axis=1)

    def by_group(values):
        grouped = values.reshape(-1, BATCH, SLOTS).transpose(0, 2, 1).reshape(-1, SLOTS * BATCH)
        return jnp.pad(grouped, ((0, 0), (0, LANES - SLOTS * BATCH)), constant_values=FAR)

    my_table = lax.dynamic_slice_in_dim(table, place * roi_count, roi_count, axis=1)
    my_targets = lax.dynamic_slice_in_dim(targets, place * roi_count, roi_count, axis=0)
    aux = jnp.concatenate(
        (
            my_table[6].astype(jnp.float32)[:, None],
            my_table[7].astype(jnp.float32)[:, None],
            jnp.zeros((roi_count, CLASSES - 2), jnp.float32),
            my_targets,
            jnp.zeros((roi_count, HALF - CLASSES - 4), jnp.float32),
        ),
        axis=1,
    )
    meta = jnp.stack((half, parity, lax.axis_index("dp") % 2))
    pooled = pool(features, meta, starts, lows, points)
    all_grad, second_wgrad, tail, ordered = middle(
        pooled, *weight, predict, bias, aux, valid_here, n_dp
    )
    second_part = lax.psum_scatter(second_wgrad, "dp", scatter_dimension=0, tiled=True)
    if by_groups(n_dp):
        here, there, later = weight_grad(pooled, all_grad, meta, n_dp)
        swapped = lax.ppermute(there, "dp", [(spot, spot ^ 1) for spot in range(n_dp)])
    cell_grads = spread(
        all_grad, ordered, starts, lows, by_group(rows_at), by_group(cols_at), features.shape[0]
    )
    if by_groups(n_dp):
        home, second_sum, tails, kept, far = reduce_home(
            here, swapped, later, tail, second_part, cell_grads, n_dp
        )
        first_new, first_mean_new, first_square_new, feature_grads = finish(
            home, kept, far, first_weight, first_mean, first_square, n_dp
        )
        tails = tails.reshape(n_blk, n_dp, -1, HALF)
        out_sum = tails[:, :, : -8].reshape(H, HALF)[:, :outw]
        bias_flat = tails[:, :, -8].reshape(-1)
    else:
        first_new, first_mean_new, first_square_new = adamw(
            first_weight, sum_apart(pooled, all_grad, n_blk), first_mean, first_square, rate_first
        )
        parts = lax.all_to_all(
            cell_grads.reshape(n_blk, -1, HALF), "blk", split_axis=0, concat_axis=0, tiled=True
        ).astype(jnp.float32)
        feature_grads = jnp.concatenate((parts[0] + parts[1], parts[2] + parts[3]), axis=1)
        second_sum = lax.psum_scatter(second_part, "blk", scatter_dimension=1, tiled=True)
        second_sum = second_sum.astype(jnp.float32)
        tails = lax.psum(tail, ("dp", "blk"))
        out_sum = tails[:, : H // n_blk].reshape(H, HALF)[:, :outw]
        bias_flat = tails[:, H // n_blk :].reshape(-1)
    bias_sum = bias_flat[: biases.shape[0]]
    total_loss = bias_flat[biases.shape[0]]

    second_new, second_mean_new, second_square_new = adamw(
        second_weight, second_sum, second_mean, second_square, rate_second
    )
    out_new, out_mean_new, out_square_new = adamw(
        out_weight, out_sum, out_mean, out_square, rate_out
    )
    bias_new, bias_mean_new, bias_square_new = adamw(
        biases, bias_sum, bias_mean, bias_square, rate_bias
    )
    return (
        feature_grads,
        total_loss,
        first_new,
        first_mean_new,
        first_square_new,
        second_new,
        second_mean_new,
        second_square_new,
        out_new,
        out_mean_new,
        out_square_new,
        bias_new,
        bias_mean_new,
        bias_square_new,
    )


def solution(mesh):
    in_specs = (
        P("dp", None),
        P(None, ("dp", "blk")),
        P(None, "dp"),
        P(None, ("dp", "blk")),
        P("dp", "blk"),
        P("dp", "blk"),
        P("dp", "blk"),
        P("dp", "blk"),
        P("dp", "blk"),
        P("dp", "blk"),
        P(),
        P(),
        P(),
        P(),
        P(),
        P(),
    )
    out_specs = (
        P(("dp", "blk"), None),
        P(),
        P("dp", "blk"),
        P("dp", "blk"),
        P("dp", "blk"),
        P("dp", "blk"),
        P("dp", "blk"),
        P("dp", "blk"),
        P(),
        P(),
        P(),
        P(),
        P(),
        P(),
    )
    return jax.shard_map(
        functools.partial(on_device, n_dp=mesh.shape["dp"], n_blk=mesh.shape["blk"]),
        mesh=mesh,
        in_specs=in_specs,
        out_specs=out_specs,
        check_vma=False,
    )
```

```python
import functools

import jax
import jax.numpy as jnp
import numpy as np
from jax import lax
from jax.experimental import pallas as pl
from jax.experimental.pallas import tpu as pltpu
from jax.sharding import PartitionSpec as P

C = 256
H = 1024
CLASSES = 81
CANVAS = 512
IMAGES = 4
LEVELS = 4
STEP = 10
K1 = 12544
BINS = 49

HALF = 128
SLOTS = 26
KQ = SLOTS * HALF
FAR = -1.0e6
BATCH = 16
MAIN = 24
LANES = MAIN * BATCH
SIDES = (128, 64, 32, 16)
BASES = (0, 16384, 20480, 21504)
WIN_ROWS = (52, 28, 16, 16)
WIN_COLS = (64, 32, 16, 16)
BACK_COLS = (56, 32, 16, 16)
VMEM_LIMIT = 60 * 1024 * 1024
GROUP = 32
OWNED = 13
SHARD = OWNED + 1
AHEAD = H // 2
SWAPPED = 8
LATER = OWNED - SWAPPED
AHEAD_ROWS = (OWNED + 2) * GROUP
MESH = pl.DeviceIdType.MESH

third = 1.0 / 3.0
rate_first = 0.018
rate_second = 0.06
rate_out = 0.18
rate_bias = 0.2


def contract_rows(left_side, right_side):
    return lax.dot_general(
        left_side, right_side, (((0,), (0,)), ((), ())), preferred_element_type=jnp.float32
    )


def contract_cols(left_side, right_side):
    return lax.dot_general(
        left_side, right_side, (((1,), (1,)), ((), ())), preferred_element_type=jnp.float32
    )


def sort_rois(roi_table, box_targets):
    count = roi_table.shape[1]
    key = roi_table[5] * IMAGES + roi_table[4]
    place = jnp.arange(count, dtype=jnp.int32)
    before = (key[None, :] < key[:, None]) | (
        (key[None, :] == key[:, None]) & (place[None, :] < place[:, None])
    )
    rank = jnp.sum(before.astype(jnp.int32), axis=1)
    segments = jnp.arange(LEVELS * IMAGES + 1, dtype=jnp.int32)
    starts = jnp.sum((key[None, :] < segments[:, None]).astype(jnp.int32), axis=1)
    rows = jnp.concatenate((roi_table.astype(jnp.float32), box_targets), axis=0)
    pick = (rank[None, :] == place[:, None]).astype(jnp.float32)
    ordered = lax.dot_general(
        pick, rows, (((1,), (1,)), ((), ())), precision=lax.Precision.HIGHEST
    )
    return ordered[:, :8].astype(jnp.int32).T, ordered[:, 8:], starts


def sample_points(table, offsets, parity):
    level_of = table[5]
    image_of = table[4]
    choose = (image_of[:, None] == jnp.arange(IMAGES, dtype=jnp.int32)[None, :]).astype(jnp.int32)
    shift_y = jnp.sum(choose * offsets[0][None, :], axis=1)
    shift_x = jnp.sum(choose * offsets[1][None, :], axis=1)
    grid_side = jnp.right_shift(jnp.full_like(level_of, CANVAS // 4), level_of)
    stride_px = (4 * jnp.left_shift(jnp.ones_like(level_of), level_of)).astype(jnp.float32)
    bins = 2 * jnp.arange(SLOTS, dtype=jnp.int32) + parity
    inside = bins < BINS
    every = jnp.arange(7, dtype=jnp.int32)

    def axis_points(low_edge, high_edge, shift_by, which, keep):
        centres = (which.astype(jnp.float32) + 0.5) / 7.0
        start_px = (low_edge + shift_by).astype(jnp.float32)
        extent = (high_edge - low_edge).astype(jnp.float32)
        points = start_px[:, None] + centres[None, :] * extent[:, None]
        limit_max = (grid_side - 1).astype(jnp.float32)[:, None]
        scaled = jnp.clip(points / stride_px[:, None] - 0.5, 0.0, limit_max)
        return jnp.where(keep[None, :], scaled, FAR)

    rows = (table[1], table[3], shift_y)
    cols = (table[0], table[2], shift_x)
    return (
        axis_points(*rows, every, every >= 0),
        axis_points(*cols, every, every >= 0),
        axis_points(*rows, bins // 7, inside),
        axis_points(*cols, bins % 7, inside),
    )


def window_lows(offsets):
    lows = []
    for level in range(LEVELS - 1):
        half_stride = 2 << level
        lows.append(jnp.maximum(jnp.right_shift(offsets - half_stride, 2 + level), 0))
    lows.append(jnp.zeros_like(offsets))
    return jnp.stack(lows, axis=1).reshape(-1)


def segment_loop(starts, lows, visit):
    for level in range(LEVELS):

        def image_step(image, carry, level=level):
            segment = level * IMAGES + image
            begin = starts[segment]
            end = starts[segment + 1]
            row_low = lows[level * IMAGES + image]
            col_low = lows[(LEVELS + level) * IMAGES + image]

            @pl.when(end > begin)
            def _():
                visit(level, begin, end, row_low, col_low)

            return carry

        lax.fori_loop(0, IMAGES, image_step, 0)


def hat(distance):
    return jnp.maximum(1.0 - jnp.abs(distance), 0.0)


def pool_kernel(starts, lows, meta, feat_hbm, uv_ref, out_ref, raw, cells, win, acc, sem):
    total = raw.shape[0]
    lane0 = pl.multiple_of(meta[0] * HALF, HALF)
    fetch = pltpu.make_async_copy(feat_hbm.at[:, pl.ds(lane0, HALF)], raw, sem)
    fetch.start()
    count = acc.shape[0]

    def clear(step, carry):
        acc[pl.ds(pl.multiple_of(step * 8, 8), 8), :] = jnp.zeros((8, KQ), jnp.float32)
        return carry

    lax.fori_loop(0, count // 8, clear, 0)
    fetch.wait()

    def widen(step, carry):
        rows = pl.ds(pl.multiple_of(step * 128, 128), 128)
        cells[rows, :] = raw[rows, :].astype(jnp.float32)
        return carry

    lax.fori_loop(0, total // 128, widen, 0)

    def visit(level, begin, end, row_low, col_low):
        side, base = SIDES[level], BASES[level]
        height, width = WIN_ROWS[level], WIN_COLS[level]
        shift = width.bit_length() - 1
        per_tile = HALF // width
        tiles = height // per_tile
        depth = tiles * HALF

        def take(row, carry):
            source = pl.ds(base + (row_low + row) * side + col_low, width)
            target = pl.ds(pl.multiple_of(row * width, width), width)
            win[target, :] = cells[source, :].astype(jnp.bfloat16)
            return carry

        lax.fori_loop(0, height, take, 0)
        row_shift = row_low.astype(jnp.float32)
        col_shift = col_low.astype(jnp.float32)

        def group(parity, step, carry):
            first = pl.multiple_of(step * BATCH, BATCH)
            lane = lax.broadcasted_iota(jnp.int32, (BATCH, HALF), 1)
            lane_row = jnp.right_shift(lane, shift).astype(jnp.float32) + row_shift
            lane_col = jnp.bitwise_and(lane, width - 1).astype(jnp.float32) + col_shift
            roi = first + lax.broadcasted_iota(jnp.int32, (BATCH, HALF), 0)
            mine = (roi >= begin) & (roi < end)
            points = jnp.where(mine, uv_ref[pl.ds(first, BATCH), :], FAR)
            row_at = [points[:, a : a + 1] - lane_row for a in range(7)]
            col_hats = [hat(points[:, 64 + b : 65 + b] - lane_col) for b in range(7)]
            bins = [2 * slot + parity for slot in range(SLOTS)]
            pooled = None
            for begin_tile in range(0, tiles, 4):
                columns = []
                for tile in range(begin_tile, min(begin_tile + 4, tiles)):
                    row_hats = [hat(at - float(tile * per_tile)) for at in row_at]
                    weights = [
                        (row_hats[one // 7] * col_hats[one % 7]).astype(jnp.bfloat16)
                        if one < BINS
                        else jnp.zeros((BATCH, HALF), jnp.bfloat16)
                        for one in bins
                    ]
                    columns.append(jnp.concatenate(weights, axis=0))
                part = jnp.dot(
                    jnp.concatenate(columns, axis=1),
                    win[begin_tile * HALF : (begin_tile + len(columns)) * HALF, :],
                    preferred_element_type=jnp.float32,
                )
                pooled = part if pooled is None else pooled + part
            for slot in range(SLOTS):
                where = (pl.ds(first, BATCH), slice(slot * HALF, (slot + 1) * HALF))
                acc[where] = acc[where] + pooled[slot * BATCH : (slot + 1) * BATCH, :]
            return carry

        for parity in (0, 1):

            @pl.when(meta[1] == parity)
            def _(parity=parity):
                lax.fori_loop(
                    begin // BATCH, (end + BATCH - 1) // BATCH, functools.partial(group, parity), 0
                )

    segment_loop(starts, lows, visit)

    def narrow(step, carry):
        rows = pl.ds(pl.multiple_of(step * 16, 16), 16)
        out_ref[rows, :] = acc[rows, :].astype(jnp.bfloat16)
        return carry

    lax.fori_loop(0, count // 16, narrow, 0)


def pool(features, meta, starts, lows, points):
    count = points.shape[0]
    cells = features.shape[0]
    return pl.pallas_call(
        pool_kernel,
        out_shape=jax.ShapeDtypeStruct((count, KQ), jnp.bfloat16),
        in_specs=[
            pl.BlockSpec(memory_space=pltpu.SMEM),
            pl.BlockSpec(memory_space=pltpu.SMEM),
            pl.BlockSpec(memory_space=pltpu.SMEM),
            pl.BlockSpec(memory_space=pl.ANY),
            pl.BlockSpec(memory_space=pltpu.VMEM),
        ],
        out_specs=pl.BlockSpec(memory_space=pltpu.VMEM),
        scratch_shapes=[
            pltpu.VMEM((cells, HALF), jnp.bfloat16),
            pltpu.VMEM((cells, HALF), jnp.float32),
            pltpu.VMEM((KQ, HALF), jnp.bfloat16),
            pltpu.VMEM((count, KQ), jnp.float32),
            pltpu.SemaphoreType.DMA,
        ],
        compiler_params=pltpu.CompilerParams(vmem_limit_bytes=VMEM_LIMIT),
        cost_estimate=pl.CostEstimate(
            flops=40_000_000_000, bytes_accessed=13_000_000, transcendentals=0
        ),
        name="pool_bins",
    )(starts, lows, meta, features, points)


def spread_kernel(
    starts,
    lows,
    grad_ref,
    weight_hbm,
    row_ref,
    col_ref,
    last_row_ref,
    last_col_ref,
    out_ref,
    weight_ref,
    pooled,
    cells,
    part,
    row_hat,
    right,
    weight_sem,
):
    total = cells.shape[0]
    fetch = pltpu.make_async_copy(weight_hbm, weight_ref, weight_sem)
    fetch.start()

    def clear(step, carry):
        rows = pl.ds(pl.multiple_of(step * 128, 128), 128)
        cells[rows, :] = jnp.zeros((128, HALF), jnp.float32)
        return carry

    lax.fori_loop(0, total // 128, clear, 0)
    fetch.wait()

    def back_dot(step, carry):
        cols = pl.ds(pl.multiple_of(step * 256, 256), 256)
        pooled[:, cols] = contract_cols(grad_ref[...], weight_ref[cols, :]).astype(jnp.bfloat16)
        return carry

    lax.fori_loop(0, KQ // 256, back_dot, 0)

    def visit(level, begin, end, row_low, col_low):
        side, base = SIDES[level], BASES[level]
        height, width = WIN_ROWS[level], BACK_COLS[level]
        chunk = (26, 28, 16, 16)[level]
        row_shift = row_low.astype(jnp.float32)
        col_shift = col_low.astype(jnp.float32)

        def wipe(row, carry):
            rows = pl.ds(pl.multiple_of(row * width, 8), width)
            part[rows, :] = jnp.zeros((width, HALF), jnp.float32)
            return carry

        lax.fori_loop(0, height, wipe, 0)

        def accumulate(row_at, col_at, lanes, samples):
            row_hat[:, :lanes] = hat(
                row_at - lax.broadcasted_iota(jnp.int32, (56, lanes), 0).astype(jnp.float32)
            )
            col_hat = hat(
                col_at - lax.broadcasted_iota(jnp.int32, (width, lanes), 0).astype(jnp.float32)
            )
            for row in range(0, height, chunk):
                left = jnp.concatenate(
                    [
                        col_hat * row_hat[row + one : row + one + 1, :lanes]
                        for one in range(chunk)
                    ],
                    axis=0,
                ).astype(jnp.bfloat16)
                rows = slice(row * width, (row + chunk) * width)
                part[rows, :] += jnp.dot(left, samples, preferred_element_type=jnp.float32)

        def placed(roi, row_line, col_line):
            mine = (roi >= begin) & (roi < end)
            return (
                jnp.where(mine, row_line, FAR) - row_shift,
                jnp.where(mine, col_line, FAR) - col_shift,
            )

        def group(step, carry):
            first = pl.multiple_of(step * BATCH, BATCH)
            for slot in range(MAIN):
                right[slot * BATCH : (slot + 1) * BATCH, :] = pooled[
                    pl.ds(first, BATCH), slot * HALF : (slot + 1) * HALF
                ]
            lane = lax.broadcasted_iota(jnp.int32, (1, LANES), 1)
            roi = first + jnp.bitwise_and(lane, BATCH - 1)
            line = pl.ds(step, 1)
            row_at, col_at = placed(roi, row_ref[line, :], col_ref[line, :])
            accumulate(row_at, col_at, LANES, right[...])
            return carry

        lax.fori_loop(begin // BATCH, (end + BATCH - 1) // BATCH, group, 0)

        def last_slot(step, carry):
            first = pl.multiple_of(step * HALF, HALF)
            roi = first + lax.broadcasted_iota(jnp.int32, (1, HALF), 1)
            line = pl.ds(step, 1)
            row_at, col_at = placed(roi, last_row_ref[line, :], last_col_ref[line, :])
            samples = pooled[pl.ds(first, HALF), MAIN * HALF : (MAIN + 1) * HALF]
            accumulate(row_at, col_at, HALF, samples)
            return carry

        lax.fori_loop(begin // HALF, (end + HALF - 1) // HALF, last_slot, 0)

        def flush(row, carry):
            target = pl.ds(base + (row_low + row) * side + col_low, width)
            source = pl.ds(pl.multiple_of(row * width, 8), width)
            cells[target, :] = cells[target, :] + part[source, :]
            return carry

        lax.fori_loop(0, height, flush, 0)

    segment_loop(starts, lows, visit)

    def narrow(step, carry):
        rows = pl.ds(pl.multiple_of(step * 128, 128), 128)
        out_ref[rows, :] = (cells[rows, :] * third).astype(jnp.bfloat16)
        return carry

    lax.fori_loop(0, total // 128, narrow, 0)


def spread(first_grad, weight, starts, lows, points, cells):
    count = first_grad.shape[0]
    return pl.pallas_call(
        spread_kernel,
        out_shape=jax.ShapeDtypeStruct((cells, HALF), jnp.bfloat16),
        in_specs=[
            pl.BlockSpec(memory_space=pltpu.SMEM),
            pl.BlockSpec(memory_space=pltpu.SMEM),
            pl.BlockSpec(memory_space=pltpu.VMEM),
            pl.BlockSpec(memory_space=pl.ANY),
            pl.BlockSpec(memory_space=pltpu.VMEM),
            pl.BlockSpec(memory_space=pltpu.VMEM),
            pl.BlockSpec(memory_space=pltpu.VMEM),
            pl.BlockSpec(memory_space=pltpu.VMEM),
        ],
        out_specs=pl.BlockSpec(memory_space=pltpu.VMEM),
        scratch_shapes=[
            pltpu.VMEM((KQ, H), jnp.bfloat16),
            pltpu.VMEM((count, KQ), jnp.bfloat16),
            pltpu.VMEM((cells, HALF), jnp.float32),
            pltpu.VMEM((WIN_ROWS[0] * BACK_COLS[0], HALF), jnp.float32),
            pltpu.VMEM((56, LANES), jnp.float32),
            pltpu.VMEM((LANES, HALF), jnp.bfloat16),
            pltpu.SemaphoreType.DMA,
        ],
        compiler_params=pltpu.CompilerParams(vmem_limit_bytes=VMEM_LIMIT),
        cost_estimate=pl.CostEstimate(
            flops=40_000_000_000, bytes_accessed=15_000_000, transcendentals=0
        ),
        name="spread_bins",
    )(starts, lows, first_grad, weight, *points)


def adamw(weight, gradient, moment, square, step_rate):
    new_mean = 0.9 * moment + 0.1 * gradient
    new_square = 0.999 * square + 0.001 * gradient * gradient
    mean_hat = new_mean / (1.0 - 0.9**STEP)
    square_hat = new_square / (1.0 - 0.999**STEP)
    new_weight = weight - step_rate * (mean_hat / (jnp.sqrt(square_hat) + 1e-08) + 0.0001 * weight)
    return (new_weight, new_mean, new_square)


def groups_before(half, parity, index):
    inside = index % 16 - (8 * parity + 4 * half)
    return index // 16 * 4 + jnp.minimum(jnp.maximum(inside, 0), 4)


def group_place(half, parity, slot, part, n_dp):
    span = K1 // GROUP // n_dp

    def earlier(index):
        inside = jnp.bitwise_and(index, 15) - (8 * parity + 4 * half)
        return jnp.right_shift(index, 4) * 4 + jnp.minimum(jnp.maximum(inside, 0), 4)

    group = 8 * (2 * slot + parity) + 4 * half + part
    owner = sum((group >= span * other).astype(jnp.int32) for other in range(1, n_dp))
    return owner, earlier(group) - earlier(owner * span)


def owned_groups(n_dp):
    span = K1 // GROUP // n_dp
    table = np.zeros((n_dp, 4, OWNED), np.int32)
    for owner in range(n_dp):
        for quarter in range(4):
            found = [
                local
                for local in range(span)
                if (owner * span + local) // 8 % 2 == quarter % 2
                and (owner * span + local) % 8 // 4 == quarter // 2
            ]
            table[owner, quarter] = (found + [0] * OWNED)[:OWNED]
    return table


def group_sources(n_dp):
    span = K1 // GROUP // n_dp
    table = np.zeros((n_dp, span), np.int32)
    for owner in range(n_dp):
        met = [0] * 4
        for local in range(span):
            group = owner * span + local
            quarter = group % 8 // 4 * 2 + group // 8 % 2
            table[owner, local] = quarter * OWNED + met[quarter]
            met[quarter] += 1
    return table


def by_groups(n_dp):
    return n_dp == 8


def deal_kernel(table, weight_ref, rois_ref, out_ref):
    base = lax.axis_index("dp") * 4 * OWNED
    for quarter in range(4):

        def step(index, carry, quarter=quarter):
            source = pl.ds(
                pl.multiple_of(table[base + quarter * OWNED + index] * GROUP, GROUP), GROUP
            )
            target = pl.ds(pl.multiple_of(index * GROUP, GROUP), GROUP)
            out_ref[quarter, target, :] = weight_ref[source, :].astype(jnp.bfloat16)
            return carry

        lax.fori_loop(0, OWNED, step, 0)
        out_ref[quarter, OWNED * GROUP :, :] = rois_ref[...]


def gather_quarter(first_weight, second_weight, rois, n_dp):
    cols = first_weight.shape[1]
    second = second_weight.astype(jnp.bfloat16)
    if by_groups(n_dp):
        table = jnp.asarray(owned_groups(n_dp).reshape(-1))
        top = lax.optimization_barrier(rois[8:].astype(jnp.bfloat16))
        rest = rois[8:] - top.astype(jnp.float32)
        middle_term = lax.optimization_barrier(rest.astype(jnp.bfloat16))
        last = (rest - middle_term.astype(jnp.float32)).astype(jnp.bfloat16)
        riders = jnp.concatenate((rois[:8].astype(jnp.bfloat16), top, middle_term, last), axis=0)
        riders = jnp.pad(riders, ((0, GROUP - riders.shape[0]), (0, 0)))
        dealt = pl.pallas_call(
            deal_kernel,
            out_shape=jax.ShapeDtypeStruct((4, SHARD * GROUP, cols), jnp.bfloat16),
            in_specs=[
                pl.BlockSpec(memory_space=pltpu.SMEM),
                pl.BlockSpec(memory_space=pltpu.VMEM),
                pl.BlockSpec(memory_space=pltpu.VMEM),
            ],
            out_specs=pl.BlockSpec(memory_space=pltpu.VMEM),
            name="deal_rows",
        )(table, first_weight, riders)
        swapped = lax.all_to_all(dealt, "blk", split_axis=0, concat_axis=0, tiled=True)
        ridden = swapped[:, OWNED * GROUP :].astype(jnp.float32).transpose(1, 0, 2)
        ridden = ridden.reshape(GROUP, -1)
        all_rois = jnp.concatenate(
            (ridden[:8], (ridden[8:12] + ridden[12:16]) + ridden[16:20]), axis=0
        )
        rows = swapped[:, : OWNED * GROUP].transpose(1, 0, 2).reshape(OWNED * GROUP, -1)
        block = second.reshape(2, 2, GROUP, cols).transpose(0, 2, 1, 3).reshape(2 * GROUP, -1)
        ahead = jnp.concatenate((rows[:, :AHEAD], block), axis=0)
        gathered = lax.all_gather(ahead, "dp", axis=0, tiled=True)
        behind = rows[:, AHEAD:]
        swapped = lax.ppermute(behind, "dp", [(spot, spot ^ 1) for spot in range(n_dp)])
        return (gathered, behind, swapped), all_rois
    all_rois = lax.all_gather(rois, "blk", axis=1, tiled=True)
    rows = lax.all_gather(first_weight.astype(jnp.bfloat16), "dp", axis=0, tiled=True)
    split = jnp.pad(rows.reshape(BINS, C, cols), ((0, 2 * SLOTS - BINS), (0, 0), (0, 0)))
    split = split.reshape(SLOTS, 2, 2, HALF, cols).transpose(2, 1, 0, 3, 4)
    split = split.reshape(4, KQ, cols)
    mine = lax.all_to_all(split, "blk", split_axis=0, concat_axis=0, tiled=True)
    mine = mine.transpose(1, 0, 2).reshape(KQ, -1)
    second = lax.all_gather(second, "dp", axis=0, tiled=True)
    block = second.reshape(4, -1, cols).transpose(1, 0, 2).reshape(-1, 4 * cols)
    rows = jnp.concatenate((mine, block), axis=0)
    return (rows, rows, rows), all_rois


def second_blocks(source, target, column, sem, n_dp):
    owners, rows = (n_dp, GROUP) if by_groups(n_dp) else (1, H // 4)
    copies = []
    for owner in range(owners):
        for part in range(4):
            if by_groups(n_dp):
                first = owner * AHEAD_ROWS + (OWNED + part // 2) * GROUP
                lane = part % 2 * 256
            else:
                first, lane = KQ, part * 256
            copies.append(
                pltpu.make_async_copy(
                    source.at[pl.ds(first, rows), pl.ds(lane, 256)],
                    target.at[pl.ds((owner * 4 + part) * rows, rows), column],
                    sem.at[owner * 4 + part],
                )
            )
    return copies


def owner_rows(half, parity, owner, n_dp):
    span = K1 // GROUP // n_dp
    begin = groups_before(half, parity, owner * span)
    end = groups_before(half, parity, (owner + 1) * span)
    many = pl.ds(pl.multiple_of(begin * GROUP, GROUP), (OWNED - 1) * GROUP)
    last = pl.ds(pl.multiple_of((end - 1) * GROUP, GROUP), GROUP)
    return many, last, end - begin == OWNED


def ahead_copies(source, target, sems, half, parity, n_dp):
    copies = []
    for owner in range(n_dp):
        many, last, full = owner_rows(half, parity, owner, n_dp)
        first, rows = owner * AHEAD_ROWS, (OWNED - 1) * GROUP
        copies.append(
            (
                None,
                pltpu.make_async_copy(
                    source.at[pl.ds(first, rows), :], target.at[many, :], sems.at[2 * owner]
                ),
            )
        )
        copies.append(
            (
                full,
                pltpu.make_async_copy(
                    source.at[pl.ds(first + rows, GROUP), :],
                    target.at[last, :],
                    sems.at[2 * owner + 1],
                ),
            )
        )
    return copies


def whole_copies(source, targets, sems):
    return [
        (
            None,
            pltpu.make_async_copy(
                source.at[pl.ds(0, KQ), pl.ds(half * AHEAD, AHEAD)], target, sems.at[half]
            ),
        )
        for half, target in enumerate(targets)
    ]


def each_copy(copies, action):
    for condition, copy in copies:
        if condition is None:
            action(copy)
        else:

            @pl.when(condition)
            def _(copy=copy):
                action(copy)


def wipe_slots(target, parity):
    target[KQ - HALF :, :] = jnp.zeros((HALF, AHEAD), jnp.bfloat16)

    @pl.when(parity == 1)
    def _():
        target[KQ - 2 * HALF : KQ - HALF, :] = jnp.zeros((HALF, AHEAD), jnp.bfloat16)


def gelu_parts(values):
    cdf = 0.5 * (1.0 + lax.erf(values * np.float32(np.sqrt(0.5))))
    density = jnp.exp(-0.5 * values * values) * np.float32(1.0 / np.sqrt(2.0 * np.pi))
    return values * cdf, cdf + values * density


def middle_kernel(
    n_dp,
    pooled_hbm,
    ahead_hbm,
    behind_hbm,
    swapped_hbm,
    predict_ref,
    bias_ref,
    aux_ref,
    all_grad,
    second_out,
    tail_ref,
    ordered_hbm,
    pooled,
    ahead,
    behind,
    second_ref,
    part,
    sent,
    came,
    first_pre,
    second_pre,
    first_act,
    second_act,
    first_grad,
    second_grad,
    valid_came,
    pooled_sem,
    weight_sem,
    own_sem,
    second_sem,
    out_sem,
    up_send,
    up_recv,
    down_send,
    down_recv,
    y_send,
    y_recv,
    valid_send,
    valid_recv,
    send_sem,
    recv_sem,
):
    me = lax.axis_index("blk")
    dp = lax.axis_index("dp")
    peers = [(dp + step) % n_dp for step in range(1, n_dp)] if by_groups(n_dp) else []
    high, low = me // 2, me % 2
    sibling = high * 2 + (1 - low)
    across = (1 - high) * 2 + low
    corner = (1 - high) * 2 + (1 - low)
    rows = part.shape[0]
    quarter = H // 4

    barrier = pltpu.get_barrier_semaphore()
    for other in (sibling, across, corner):
        pl.semaphore_signal(barrier, inc=1, device_id={"blk": other}, device_id_type=MESH)
    for peer in peers:
        pl.semaphore_signal(barrier, inc=1, device_id={"dp": peer}, device_id_type=MESH)

    def hidden_cols(which):
        return pl.ds(pl.multiple_of(which * quarter, quarter), quarter)

    z, y = dp // 2, dp % 2
    partner = 2 * z + 1 - y
    shard = (OWNED - 1) * GROUP

    def shard_pieces(owner):
        many, last, full = owner_rows(high, low, owner, n_dp)
        first = many.start
        return (
            (None, pl.ds(pl.multiple_of(first, GROUP), shard // 2), pl.ds(0, shard // 2)),
            (
                None,
                pl.ds(pl.multiple_of(first + shard // 2, GROUP), shard // 2),
                pl.ds(shard // 2, shard // 2),
            ),
            (full, last, pl.ds(shard, GROUP)),
        )

    def shard_copies(owner, send, recv, index, target, own=False):
        copies = []
        for piece, (condition, place, source) in enumerate(shard_pieces(owner)):
            copies.append(
                (
                    condition,
                    pltpu.make_async_remote_copy(
                        src_ref=behind_hbm.at[source, :] if own else behind.at[place, :],
                        dst_ref=behind.at[place, :],
                        send_sem=send.at[3 * index + piece],
                        recv_sem=recv.at[3 * index + piece],
                        device_id={"dp": target},
                        device_id_type=MESH,
                    ),
                )
            )
        return copies

    def own_shard(action):
        @pl.when(z < 3)
        def _():
            each_copy(shard_copies(dp, up_send, up_recv, 0, dp + 2, True), action)

        @pl.when(z > 0)
        def _():
            each_copy(shard_copies(dp, down_send, down_recv, 0, dp - 2, True), action)

    def relay_shards(distance, took, action):
        def pass_on(owner, send, recv, neighbour, goes_on, place):
            coming = shard_copies(owner, send, recv, distance - 1, neighbour)
            aside = shard_copies(owner, y_send, y_recv, place, partner)
            onward = [None] * len(coming)
            if distance < 3:
                onward = shard_copies(owner, send, recv, distance, neighbour)
            for came_in, on, over in zip(coming, onward, aside):
                each_copy([came_in], took)
                if on is not None:

                    @pl.when(goes_on)
                    def _(on=on):
                        each_copy([on], action)

                each_copy([over], action)

        @pl.when(z >= distance)
        def _():
            pass_on(dp - 2 * distance, up_send, up_recv, dp + 2, z < 3, z - distance)

        @pl.when(z + distance <= 3)
        def _():
            pass_on(dp + 2 * distance, down_send, down_recv, dp - 2, z > 0, z + distance)

    def serve(distance):
        if by_groups(n_dp):
            relay_shards(distance, lambda copy: copy.wait_recv(), lambda copy: copy.start())

    blocks = second_blocks(ahead_hbm, second_ref, hidden_cols(me), second_sem, n_dp)
    for copy in blocks:
        copy.start()
    if by_groups(n_dp):
        early = ahead_copies(ahead_hbm, ahead, weight_sem, high, low, n_dp)
        late = []
        for which, (source_hbm, owner) in enumerate(((behind_hbm, dp), (swapped_hbm, partner))):
            for piece, (condition, place, source) in enumerate(shard_pieces(owner)):
                late.append(
                    (
                        condition,
                        pltpu.make_async_copy(
                            source_hbm.at[source, :],
                            behind.at[place, :],
                            out_sem.at[2 + 3 * which + piece],
                        ),
                    )
                )
        wipe_slots(ahead, low)
        wipe_slots(behind, low)
    else:
        early, late = whole_copies(ahead_hbm, (ahead, behind), weight_sem), []
    each_copy((*early, *late), lambda copy: copy.start())

    def chunk_rows(which):
        return pl.ds(pl.multiple_of(which * rows, 16), rows)

    order = (corner, across, sibling, me)
    chunks = [
        pltpu.make_async_copy(
            pooled_hbm.at[chunk_rows(which), :], pooled.at[chunk_rows(which), :], pooled_sem.at[i]
        )
        for i, which in enumerate(order)
    ]
    for chunk in chunks:
        chunk.start()
    pl.semaphore_wait(barrier, 3 + len(peers))
    counts = [
        pltpu.make_async_remote_copy(
            src_ref=aux_ref.at[pl.ds(0, 8), :],
            dst_ref=valid_came.at[index],
            send_sem=valid_send.at[index],
            recv_sem=valid_recv.at[index],
            device_id={"dp": peer},
            device_id_type=MESH,
        )
        for index, peer in enumerate(peers)
    ]
    if by_groups(n_dp):
        own_shard(lambda copy: copy.start())
    for copy in counts:
        copy.start()

    def remote(source, target, index, other):
        return pltpu.make_async_remote_copy(
            src_ref=source,
            dst_ref=target,
            send_sem=send_sem.at[index],
            recv_sem=recv_sem.at[index],
            device_id={"blk": other},
            device_id_type=MESH,
        )

    for copy in blocks:
        copy.wait()
    mine, theirs = second_ref.at[:, hidden_cols(me)], second_ref.at[:, hidden_cols(across)]
    second_sibling = remote(mine, mine, 3, sibling)
    second_across = remote(mine, mine, 4, across)
    second_forward = remote(theirs, theirs, 5, sibling)
    second_across.start()
    second_sibling.start()

    def in_blocks(count, body):
        def step(index, carry):
            body(index)
            return carry

        lax.fori_loop(0, count, step, 0)

    def block32(step):
        return pl.ds(pl.multiple_of(step * 32, 32), 32)

    def first_half_product(which):
        cols = slice(which * AHEAD, (which + 1) * AHEAD)
        weight = (ahead, behind)[which]
        base = 18 * which
        to_sibling = remote(sent.at[0, :, cols], came.at[0, :, cols], base, sibling)
        to_across = remote(sent.at[1, :, cols], came.at[1, :, cols], base + 1, across)
        to_sibling_last = remote(sent.at[2, :, cols], came.at[2, :, cols], base + 2, sibling)

        def chunk_dot(i):
            if which == 0:
                chunks[i].wait()

            def cols_dot(step):
                lanes = pl.ds(pl.multiple_of(step * 256, 256), 256)
                target = pl.ds(pl.multiple_of(which * AHEAD + step * 256, 256), 256)
                part[:, target] = jnp.dot(
                    pooled[chunk_rows(order[i]), :],
                    weight[:, lanes],
                    preferred_element_type=jnp.float32,
                )

            in_blocks(AHEAD // 256, cols_dot)

        def hand_on(slot, came_slot=None):
            def store(step):
                block = block32(step)
                value = part[block, cols]
                if came_slot is not None:
                    value = value + came[came_slot, block, cols].astype(jnp.float32)
                sent[slot, block, cols] = value.astype(jnp.bfloat16)

            in_blocks(rows // 32, store)

        def step0():
            chunk_dot(0)
            hand_on(0)
            to_sibling.start()

        def step1():
            chunk_dot(1)
            to_sibling.wait_recv()
            hand_on(1, 0)
            to_across.start()

        def step2():
            chunk_dot(2)
            hand_on(2)
            to_sibling_last.start()

        def step3():
            chunk_dot(3)
            to_sibling_last.wait_recv()
            to_across.wait_recv()

            def activate(step):
                block = block32(step)
                value = (
                    part[block, cols]
                    + came[1, block, cols].astype(jnp.float32)
                    + came[2, block, cols].astype(jnp.float32)
                    + bias_ref[0:1, cols]
                )
                first_pre[block, cols] = value
                first_act[block, cols] = gelu_parts(value)[0].astype(jnp.bfloat16)

            in_blocks(rows // 32, activate)

        return (step0, step1, step2, step3), (to_sibling, to_across, to_sibling_last)

    steps, sums = first_half_product(0)
    each_copy(early, lambda copy: copy.wait())
    steps[0]()
    steps[1]()
    serve(1)
    second_across.wait_recv()
    second_forward.start()
    steps[2]()
    serve(2)
    steps[3]()
    serve(3)
    each_copy(late, lambda copy: copy.wait())
    if by_groups(n_dp):
        for place in range(4):

            @pl.when(z != place)
            def _(place=place):
                each_copy(
                    shard_copies(2 * place + 1 - y, y_send, y_recv, place, partner),
                    lambda copy: copy.wait_recv(),
                )
    ordered_copies = [
        pltpu.make_async_copy(
            source, ordered_hbm.at[:, pl.ds(which * AHEAD, AHEAD)], out_sem.at[which]
        )
        for which, source in enumerate((ahead, behind))
    ]
    for copy in ordered_copies:
        copy.start()
    steps, more_sums = first_half_product(1)
    for step in steps:
        step()
    my_rows = chunk_rows(me)
    across_rows = chunk_rows(across)
    second_sibling.wait_recv()
    second_forward.wait_recv()

    def second_dot(step):
        cols = pl.ds(pl.multiple_of(step * 256, 256), 256)
        second_pre[:, cols] = (
            jnp.dot(first_act[...], second_ref[:, cols], preferred_element_type=jnp.float32)
            + bias_ref[1:2, cols]
        )

    in_blocks(H // 256, second_dot)

    def activate_second(step):
        block = block32(step)
        second_act[block, :] = gelu_parts(second_pre[block, :])[0].astype(jnp.bfloat16)

    in_blocks(rows // 32, activate_second)
    head_out = (
        jnp.dot(second_act[...], predict_ref[...], preferred_element_type=jnp.float32)
        + bias_ref[2:3, :HALF]
    )
    lane = lax.broadcasted_iota(jnp.int32, (rows, HALF), 1)
    is_logit = lane < CLASSES
    is_delta = (lane >= CLASSES) & (lane < CLASSES + 4)
    label = aux_ref[:, 0:1]
    count_lane = slice(CLASSES + 4, CLASSES + 5)
    valid_total = aux_ref[0:1, count_lane]
    for index, copy in enumerate(counts):
        copy.wait_recv()
        valid_total = valid_total + valid_came[index, 0:1, count_lane]
    share = aux_ref[:, 1:2] / jnp.maximum(valid_total, 1.0)
    foreground = (label > 0.5).astype(jnp.float32)
    onehot = (lane.astype(jnp.float32) == label).astype(jnp.float32)
    top = jnp.max(jnp.where(is_logit, head_out, -jnp.inf), axis=1, keepdims=True)
    exped = jnp.where(is_logit, jnp.exp(jnp.minimum(head_out - top, 0.0)), 0.0)
    exp_sum = jnp.sum(exped, axis=1, keepdims=True)
    chosen = jnp.sum(onehot * head_out, axis=1, keepdims=True)
    error = jnp.where(is_delta, head_out - aux_ref[...], 0.0)
    absolute = jnp.abs(error)
    huber = jnp.where(absolute < 1.0, 0.5 * error * error, absolute - 0.5)
    huber_sum = jnp.sum(jnp.where(is_delta, huber, 0.0), axis=1, keepdims=True)
    loss_rows = share * (jnp.log(exp_sum) + top - chosen + foreground * huber_sum)
    delta_slope = foreground * jnp.minimum(jnp.maximum(error, -1.0), 1.0)
    head_grad = (share * (exped / exp_sum - jnp.where(is_logit, onehot, 0.0) + delta_slope)).astype(
        jnp.bfloat16
    )
    wide = head_grad.astype(jnp.float32)
    lane1 = lax.broadcasted_iota(jnp.int32, (1, HALF), 1)
    head_bias = jnp.sum(wide, axis=0, keepdims=True) + jnp.where(
        lane1 == CLASSES + 4, jnp.sum(loss_rows, axis=0, keepdims=True), 0.0
    )

    def second_back(step):
        cols = pl.ds(pl.multiple_of(step * 256, 256), 256)
        back = contract_cols(head_grad, predict_ref[cols, :])
        second_grad[:, cols] = (back * gelu_parts(second_pre[:, cols])[1]).astype(jnp.bfloat16)

    in_blocks(H // 256, second_back)
    def first_back(step):
        cols = slice(step * quarter, (step + 1) * quarter)
        back = contract_cols(second_grad[...], second_ref[cols, :])
        first_grad[:, cols] = (back * gelu_parts(first_pre[:, cols])[1]).astype(jnp.bfloat16)
        source, target = first_grad.at[:, cols], all_grad.at[my_rows, cols]
        to_other = remote(source, target, 6 + step, across)
        to_twin = remote(source, target, 10 + step, sibling)
        to_other.start()
        to_twin.start()
        relayed = all_grad.at[across_rows, cols]
        return to_other, to_twin, remote(relayed, relayed, 14 + step, sibling)

    grad_copies = [first_back(step) for step in range(4)]
    grad_own = pltpu.make_async_copy(first_grad, all_grad.at[my_rows, :], own_sem.at[2])
    grad_own.start()

    def bias_rows(grads):
        total = jnp.sum(grads[...].astype(jnp.float32), axis=0, keepdims=True)
        return [total[:, i * HALF : (i + 1) * HALF] for i in range(H // HALF)]

    nothing = jnp.zeros((1, HALF), jnp.float32)
    bias_sums = (
        bias_rows(first_grad),
        bias_rows(second_grad),
        [head_bias] + [nothing] * 7,
        [nothing] * 8,
    )
    for step in range(4):
        piece = contract_rows(second_act[:, step * quarter : (step + 1) * quarter], head_grad)
        if by_groups(n_dp):
            for owner in range(n_dp):
                tail_ref[step, owner, :32, :] = piece[owner * 32 : owner * 32 + 32, :]
                tail_ref[step, owner, 32:, :] = jnp.concatenate(
                    [bias_sums[step][owner]] + [nothing] * 7, axis=0
                )
        else:
            tail_ref[step, :quarter, :] = piece
            tail_ref[step, quarter:, :] = jnp.concatenate(bias_sums[step], axis=0)

    for to_other, _, relay in grad_copies:
        to_other.wait_recv()
        relay.start()

    def second_block(step):
        cols = pl.ds(pl.multiple_of(step * 256, 256), 256)
        second_out[:, cols] = contract_rows(first_act[...], second_grad[:, cols]).astype(
            jnp.bfloat16
        )

    in_blocks(H // 256, second_block)
    grad_own.wait()
    for _, to_twin, relay in grad_copies:
        to_twin.wait_recv()
        relay.wait_recv()
    for copy in ordered_copies:
        copy.wait()
    if by_groups(n_dp):

        def sent_off(copy):
            copy.wait_send()

        own_shard(sent_off)
        for distance in (1, 2, 3):
            relay_shards(distance, lambda copy: None, sent_off)
    for copy in (
        *sums,
        *more_sums,
        second_sibling,
        second_across,
        second_forward,
        *(copy for three in grad_copies for copy in three),
        *counts,
    ):
        copy.wait_send()


def middle(pooled, ahead, behind, swapped, predict, bias, aux, n_dp):
    count = pooled.shape[0]
    rows = aux.shape[0]
    tail = (4, n_dp, 40, HALF) if by_groups(n_dp) else (4, H // 4 + 8, HALF)
    any_spec = pl.BlockSpec(memory_space=pl.ANY)
    vmem_spec = pl.BlockSpec(memory_space=pltpu.VMEM)
    return pl.pallas_call(
        functools.partial(middle_kernel, n_dp),
        out_shape=(
            jax.ShapeDtypeStruct((count, H), jnp.bfloat16),
            jax.ShapeDtypeStruct((H, H), jnp.bfloat16),
            jax.ShapeDtypeStruct(tail, jnp.float32),
            jax.ShapeDtypeStruct((KQ, H), jnp.bfloat16),
        ),
        in_specs=[any_spec] * 4 + [vmem_spec] * 3,
        out_specs=(any_spec, vmem_spec, vmem_spec, any_spec),
        scratch_shapes=[
            pltpu.VMEM((count, KQ), jnp.bfloat16),
            pltpu.VMEM((KQ, AHEAD), jnp.bfloat16),
            pltpu.VMEM((KQ, AHEAD), jnp.bfloat16),
            pltpu.VMEM((H, H), jnp.bfloat16),
            pltpu.VMEM((rows, H), jnp.float32),
            pltpu.VMEM((3, rows, H), jnp.bfloat16),
            pltpu.VMEM((3, rows, H), jnp.bfloat16),
            pltpu.VMEM((rows, H), jnp.float32),
            pltpu.VMEM((rows, H), jnp.float32),
            pltpu.VMEM((rows, H), jnp.bfloat16),
            pltpu.VMEM((rows, H), jnp.bfloat16),
            pltpu.VMEM((rows, H), jnp.bfloat16),
            pltpu.VMEM((rows, H), jnp.bfloat16),
            pltpu.VMEM((7, 8, HALF), jnp.float32),
            pltpu.SemaphoreType.DMA((4,)),
            pltpu.SemaphoreType.DMA((SLOTS,)),
            pltpu.SemaphoreType.DMA((3,)),
            pltpu.SemaphoreType.DMA((4 * n_dp if by_groups(n_dp) else 4,)),
            pltpu.SemaphoreType.DMA((8,)),
            pltpu.SemaphoreType.DMA((9,)),
            pltpu.SemaphoreType.DMA((9,)),
            pltpu.SemaphoreType.DMA((9,)),
            pltpu.SemaphoreType.DMA((9,)),
            pltpu.SemaphoreType.DMA((12,)),
            pltpu.SemaphoreType.DMA((12,)),
            pltpu.SemaphoreType.DMA((7,)),
            pltpu.SemaphoreType.DMA((7,)),
            pltpu.SemaphoreType.DMA((21,)),
            pltpu.SemaphoreType.DMA((21,)),
        ],
        compiler_params=pltpu.CompilerParams(
            vmem_limit_bytes=VMEM_LIMIT, collective_id=0, has_side_effects=True
        ),
        cost_estimate=pl.CostEstimate(
            flops=9_000_000_000, bytes_accessed=25_000_000, transcendentals=1_500_000
        ),
        name="middle",
    )(pooled, ahead, behind, swapped, predict, bias, aux)


def weight_grad_kernel(n_dp, meta, pooled_ref, grad_ref, here_hbm, there_hbm, later_hbm, stage, sems):
    half, parity, y = meta[0], meta[1], meta[2]
    step = pl.program_id(0)
    last = pl.num_programs(0) - 1

    def copies(which):
        buffer = which % 2
        for one in range(256 // GROUP):
            slot = 2 * which + one // 4
            owner, local = group_place(half, parity, slot, one % 4, n_dp)
            row = jnp.right_shift(owner, 1)
            inside = slot < SLOTS - 1 - parity
            here = jnp.bitwise_and(owner, 1) == y
            there = jnp.logical_not(here)
            for condition, target, place in (
                (here, here_hbm, row * OWNED + local),
                (there & (local < SWAPPED), there_hbm, row * SWAPPED + local),
                (there & (local >= SWAPPED), later_hbm, row * LATER + local - SWAPPED),
            ):

                @pl.when(inside & condition)
                def _(target=target, one=one, place=place):
                    rows = pl.ds(pl.multiple_of(place * GROUP, GROUP), GROUP)
                    pltpu.make_async_copy(
                        stage.at[buffer, pl.ds(one * GROUP, GROUP), :],
                        target.at[rows, :],
                        sems.at[buffer, one],
                    ).start()

    def waits(which):
        buffer = which % 2
        for one in range(256 // GROUP):

            @pl.when(2 * which + one // 4 < SLOTS - 1 - parity)
            def _(one=one):
                rows = pl.ds(one * GROUP, GROUP)
                pltpu.make_async_copy(
                    stage.at[buffer, rows, :], here_hbm.at[rows, :], sems.at[buffer, one]
                ).wait()

    @pl.when(step >= 2)
    def _():
        waits(step - 2)

    stage[step % 2] = contract_rows(pooled_ref[...], grad_ref[...]).astype(jnp.bfloat16)
    copies(step)

    @pl.when(step == last)
    def _():
        waits(step - 1)
        waits(step)


def weight_grad(pooled, all_grad, meta, n_dp):
    count = pooled.shape[0]
    shapes = tuple(
        jax.ShapeDtypeStruct((n_dp // 2 * groups * GROUP, H), jnp.bfloat16)
        for groups in (OWNED, SWAPPED, LATER)
    )
    any_spec = pl.BlockSpec(memory_space=pl.ANY)
    return pl.pallas_call(
        functools.partial(weight_grad_kernel, n_dp),
        grid=(SLOTS // 2,),
        out_shape=shapes,
        in_specs=[
            pl.BlockSpec(memory_space=pltpu.SMEM),
            pl.BlockSpec((count, 256), lambda i: (0, i)),
            pl.BlockSpec((count, H), lambda i: (0, 0)),
        ],
        out_specs=(any_spec, any_spec, any_spec),
        scratch_shapes=[
            pltpu.VMEM((2, 256, H), jnp.bfloat16),
            pltpu.SemaphoreType.DMA((2, 256 // GROUP)),
        ],
        compiler_params=pltpu.CompilerParams(vmem_limit_bytes=VMEM_LIMIT),
        cost_estimate=pl.CostEstimate(
            flops=7_000_000_000, bytes_accessed=16_000_000, transcendentals=0
        ),
        name="weight_grad",
    )(meta, pooled, all_grad)


def reduce_kernel(
    n_dp,
    here_hbm,
    swapped_hbm,
    later_hbm,
    tail_ref,
    second_ref,
    cells_hbm,
    home_ref,
    second_out,
    tails_ref,
    kept_hbm,
    far_hbm,
    cells_kept,
    cells_near,
    cells_own,
    cells_sum,
    mine,
    y_came,
    up_came,
    down_came,
    final,
    tail_near,
    tail_mine,
    tail_came,
    second_came,
    tail_send,
    tail_recv,
    second_send,
    second_recv,
    cells_load,
    cells_send,
    cells_recv,
    shard_load,
    y_send,
    y_recv,
    up_send,
    up_recv,
    down_send,
    down_recv,
    home_send,
    home_recv,
):
    dp = lax.axis_index("dp")
    me = lax.axis_index("blk")
    half, parity = me // 2, me % 2
    z, y = dp // 2, dp % 2
    home_rows = OWNED * GROUP
    quarter = H // 4
    sibling, across = me // 2 * 2 + 1 - me % 2, (me + 2) % 4
    others = ((me + 1) % 4, (me + 2) % 4, (me + 3) % 4)
    has_below, has_above = z > 0, z < 3

    barrier = pltpu.get_barrier_semaphore()

    def greet(**where):
        pl.semaphore_signal(barrier, inc=1, device_id=where, device_id_type=MESH)

    peers = tuple((dp + step) % n_dp for step in range(1, n_dp))
    for peer in peers:
        greet(dp=peer)
    for other in others:
        greet(blk=other)

    def order(k):
        near, far = ((3, 3), (2, 0), (1, 2), (0, 1))[k]
        low_side = jnp.where(z % 3 == 0, near, far)
        return jnp.where(z < 2, low_side, 3 - low_side)

    def shard_loads(k):
        target = order(k)
        rows = pl.ds(pl.multiple_of(target * home_rows, GROUP), home_rows)
        some = SWAPPED * GROUP
        swapped = pl.ds(pl.multiple_of(target * some, GROUP), some)
        return [
            pltpu.make_async_copy(here_hbm.at[rows, :], mine.at[target], shard_load.at[2 * k]),
            pltpu.make_async_copy(
                swapped_hbm.at[swapped, :],
                y_came.at[target, pl.ds(0, some)],
                shard_load.at[2 * k + 1],
            ),
        ]

    for k in range(4):
        for copy in shard_loads(k):
            copy.start()
    pl.semaphore_wait(barrier, n_dp + 2)

    def remote(source, target, send, recv, **where):
        return pltpu.make_async_remote_copy(
            src_ref=source,
            dst_ref=target,
            send_sem=send,
            recv_sem=recv,
            device_id=where,
            device_id_type=MESH,
        )

    piece = tail_ref.shape[2]
    nears, seconds = [], []
    for index, other in enumerate(others):
        nears.append(
            remote(
                tail_ref.at[other],
                tail_near.at[index],
                tail_send.at[index],
                tail_recv.at[index],
                blk=other,
            )
        )
        seconds.append(
            remote(
                second_ref.at[:, pl.ds(pl.multiple_of(other * quarter, quarter), quarter)],
                second_came.at[index],
                second_send.at[index],
                second_recv.at[index],
                blk=other,
            )
        )

    quarter_cells = cells_sum.shape[0]

    def cell_rows(which):
        return cells_hbm.at[pl.ds(pl.multiple_of(which * quarter_cells, 16), quarter_cells), :]

    loads, gives = [], []
    for index, chip in enumerate((1 - half, half)):
        loads.append(
            pltpu.make_async_copy(
                cell_rows(2 * chip + parity), cells_own.at[index], cells_load.at[index]
            )
        )
        gives.append(
            remote(
                cell_rows(2 * chip + 1 - parity),
                cells_near.at[index],
                cells_send.at[index],
                cells_recv.at[index],
                blk=sibling,
            )
        )
    kept_out = pltpu.make_async_copy(cells_kept, kept_hbm, cells_load.at[2])
    crossing = remote(cells_sum, far_hbm, cells_send.at[2], cells_recv.at[2], blk=across)
    parts = (pl.ds(0, SWAPPED * GROUP), pl.ds(SWAPPED * GROUP, LATER * GROUP))

    def y_copy(k):
        target = order(k)
        rows = pl.ds(pl.multiple_of(target * LATER * GROUP, GROUP), LATER * GROUP)
        return remote(
            later_hbm.at[rows, :],
            y_came.at[target, parts[1]],
            y_send.at[k],
            y_recv.at[k],
            dp=2 * z + 1 - y,
        )

    for k in range(4):
        y_copy(k).start()
    for copy in (*nears, *seconds, *gives, *loads):
        copy.start()

    def cell_blocks(body):
        def step(index, carry):
            body(pl.ds(pl.multiple_of(index * 160, 160), 160))
            return carry

        lax.fori_loop(0, quarter_cells // 160, step, 0)

    def give_across():
        loads[0].wait()
        gives[0].wait_recv()

        def add(rows):
            cells_sum[rows, :] = (
                cells_own[0, rows, :].astype(jnp.float32)
                + cells_near[0, rows, :].astype(jnp.float32)
            ).astype(jnp.bfloat16)

        cell_blocks(add)
        crossing.start()

    def keep_here():
        loads[1].wait()
        gives[1].wait_recv()

        def add(rows):
            cells_kept[rows, :] = cells_own[1, rows, :].astype(jnp.float32) + cells_near[
                1, rows, :
            ].astype(jnp.float32)

        cell_blocks(add)
        kept_out.start()

    def add_up(target, sources, part):
        first, groups = ((0, SWAPPED), (SWAPPED, LATER))[part]

        def step(index, carry):
            rows = pl.ds(pl.multiple_of((first + index) * GROUP, GROUP), GROUP)
            total = mine[target, rows, :].astype(jnp.float32)
            for ref in sources:
                total = total + ref[target, rows, :].astype(jnp.float32)
            mine[target, rows, :] = total.astype(jnp.bfloat16)
            return carry

        lax.fori_loop(0, groups, step, 0)

    def z_copy(target, part, came, send, recv, neighbour):
        sem = 2 * target + part
        return remote(
            mine.at[target, parts[part]],
            came.at[target, parts[part]],
            send.at[sem],
            recv.at[sem],
            dp=neighbour,
        )

    def up_copy(target, part):
        return z_copy(target, part, up_came, up_send, up_recv, dp + 2)

    def down_copy(target, part):
        return z_copy(target, part, down_came, down_send, down_recv, dp - 2)

    def arrive(k, part):
        if part == 0:
            for copy in shard_loads(k):
                copy.wait()
        else:
            y_copy(k).wait_recv()

    def chain(k, part):
        target = order(k)
        arrive(k, part)

        @pl.when(target > z)
        def _():
            @pl.when(has_below)
            def _():
                up_copy(target, part).wait_recv()
                add_up(target, (y_came, up_came), part)

            @pl.when(jnp.logical_not(has_below))
            def _():
                add_up(target, (y_came,), part)

            up_copy(target, part).start()

        @pl.when(target < z)
        def _():
            @pl.when(has_above)
            def _():
                down_copy(target, part).wait_recv()
                add_up(target, (y_came, down_came), part)

            @pl.when(jnp.logical_not(has_above))
            def _():
                add_up(target, (y_came,), part)

            down_copy(target, part).start()

    def last(part):
        arrive(3, part)
        add_up(z, (y_came,), part)

        @pl.when(has_below)
        def _():
            up_copy(z, part).wait_recv()
            add_up(z, (up_came,), part)

        @pl.when(has_above)
        def _():
            down_copy(z, part).wait_recv()
            add_up(z, (down_came,), part)

    def home_copies(part):
        copies = []
        for index, other in enumerate(others):
            cols = pl.ds(pl.multiple_of(other * quarter, quarter), quarter)
            copies.append(
                remote(
                    mine.at[z, parts[part], cols],
                    final.at[me, parts[part]],
                    home_send.at[3 * part + index],
                    home_recv.at[3 * part + index],
                    blk=other,
                )
            )
        return copies

    chain(0, 0)
    give_across()
    for copy in nears:
        copy.wait_recv()
    tail_mine[...] = tail_ref[me] + tail_near[0] + tail_near[1] + tail_near[2]
    tails = []
    for index, peer in enumerate(peers):
        sem = 3 + index
        tails.append(
            remote(
                tail_mine.at[peer],
                tail_came.at[index],
                tail_send.at[sem],
                tail_recv.at[sem],
                dp=peer,
            )
        )
    for copy in tails:
        copy.start()
    chain(1, 0)
    for copy in tails:
        copy.wait_recv()
    my_tail = pl.ds(pl.multiple_of((me * n_dp + dp) * piece, 8), piece)
    total = tail_mine[dp]
    for index in range(n_dp - 1):
        total = total + tail_came[index]
    tails_ref[my_tail, :] = total
    spreads = []
    for index, peer in enumerate(peers):
        spot = tails_ref.at[my_tail, :]
        sem = n_dp + 2 + index
        spreads.append(remote(spot, spot, tail_send.at[sem], tail_recv.at[sem], dp=peer))
    for copy in spreads:
        copy.start()
    keep_here()
    chain(2, 0)
    last(0)
    homes = home_copies(0)
    for copy in homes:
        copy.start()
    for k in range(3):
        chain(k, 1)
    block = tails_ref.at[pl.ds(pl.multiple_of(me * n_dp * piece, 8), n_dp * piece), :]
    shares = []
    for index, other in enumerate(others):
        sem = 2 * n_dp + 1 + index
        shares.append(remote(block, block, tail_send.at[sem], tail_recv.at[sem], blk=other))
    for copy in spreads:
        copy.wait_recv()
    for copy in shares:
        copy.start()
    own_cols = pl.ds(pl.multiple_of(me * quarter, quarter), quarter)
    second = second_ref[:, own_cols].astype(jnp.float32)
    for index, copy in enumerate(seconds):
        copy.wait_recv()
        second = second + second_came[index].astype(jnp.float32)
    second_out[...] = second
    last(1)
    homes_later = home_copies(1)
    for copy in homes_later:
        copy.start()
    home_ref[pl.ds(pl.multiple_of(me * home_rows, GROUP), home_rows), :] = mine[z, :, own_cols]
    for copy in shares:
        copy.wait_recv()
    for index in range(3):
        sender = (me + 3 - index) % 4
        homes[index].wait_recv()
        homes_later[index].wait_recv()
        rows = pl.ds(pl.multiple_of(sender * home_rows, GROUP), home_rows)
        home_ref[rows, :] = final[sender]
    for copy in (
        *homes,
        *homes_later,
        *nears,
        *tails,
        *spreads,
        *shares,
        *seconds,
        *gives,
        crossing,
        *(y_copy(k) for k in range(4)),
    ):
        copy.wait_send()
    kept_out.wait()
    crossing.wait_recv()
    for k in range(3):
        target = order(k)

        @pl.when(target > z)
        def _():
            up_copy(target, 0).wait_send()
            up_copy(target, 1).wait_send()

        @pl.when(target < z)
        def _():
            down_copy(target, 0).wait_send()
            down_copy(target, 1).wait_send()


def reduce_home(here, swapped, later, tail, second, cell_grads, n_dp):
    home = OWNED * GROUP
    piece = tail.shape[2]
    cells = cell_grads.shape[0] // 4
    vmem_spec = pl.BlockSpec(memory_space=pltpu.VMEM)
    any_spec = pl.BlockSpec(memory_space=pl.ANY)
    shards = pltpu.VMEM((4, home, H), jnp.bfloat16)

    def sems(number):
        return pltpu.SemaphoreType.DMA((number,))

    return pl.pallas_call(
        functools.partial(reduce_kernel, n_dp),
        out_shape=(
            jax.ShapeDtypeStruct((4 * home, H // 4), jnp.bfloat16),
            jax.ShapeDtypeStruct((H // n_dp, H // 4), jnp.float32),
            jax.ShapeDtypeStruct((4 * n_dp * piece, HALF), jnp.float32),
            jax.ShapeDtypeStruct((cells, HALF), jnp.float32),
            jax.ShapeDtypeStruct((cells, HALF), jnp.bfloat16),
        ),
        in_specs=[any_spec, any_spec, any_spec, vmem_spec, vmem_spec, any_spec],
        out_specs=(vmem_spec,) * 3 + (any_spec,) * 2,
        scratch_shapes=[
            pltpu.VMEM((cells, HALF), jnp.float32),
            pltpu.VMEM((2, cells, HALF), jnp.bfloat16),
            pltpu.VMEM((2, cells, HALF), jnp.bfloat16),
            pltpu.VMEM((cells, HALF), jnp.bfloat16),
            shards,
            shards,
            shards,
            shards,
            pltpu.VMEM((4, home, H // 4), jnp.bfloat16),
            pltpu.VMEM((3, n_dp, piece, HALF), jnp.float32),
            pltpu.VMEM((n_dp, piece, HALF), jnp.float32),
            pltpu.VMEM((n_dp - 1, piece, HALF), jnp.float32),
            pltpu.VMEM((3, H // n_dp, H // 4), jnp.bfloat16),
            sems(2 * n_dp + 4),
            sems(2 * n_dp + 4),
            sems(3),
            sems(3),
            sems(3),
            sems(3),
            sems(3),
            sems(8),
            sems(4),
            sems(4),
            sems(8),
            sems(8),
            sems(8),
            sems(8),
            sems(6),
            sems(6),
        ],
        compiler_params=pltpu.CompilerParams(
            vmem_limit_bytes=VMEM_LIMIT, collective_id=1, has_side_effects=True
        ),
        cost_estimate=pl.CostEstimate(
            flops=60_000_000_000, bytes_accessed=200_000_000, transcendentals=0
        ),
        name="reduce_home",
    )(here, swapped, later, tail, second, cell_grads)


def sum_apart(pooled, all_grad, n_blk):
    first_wgrad = contract_rows(pooled, all_grad).astype(jnp.bfloat16)
    split = first_wgrad.reshape(KQ, n_blk, -1).transpose(1, 0, 2)
    mine = lax.all_to_all(split, "blk", split_axis=0, concat_axis=0, tiled=True)
    cols = mine.shape[2]
    mine = mine.reshape(2, 2, SLOTS, HALF, cols).transpose(2, 1, 0, 3, 4)
    mine = mine.reshape(2 * SLOTS, C, cols)[:BINS].reshape(K1, cols)
    first_sum = lax.psum_scatter(mine, "dp", scatter_dimension=0, tiled=True).astype(jnp.float32)
    return first_sum


def finish_kernel(
    table,
    home_ref,
    weight_ref,
    mean_ref,
    square_ref,
    kept_ref,
    far_ref,
    new_ref,
    new_mean_ref,
    new_square_ref,
    features_ref,
):
    groups = weight_ref.shape[0] // GROUP
    span = K1 // GROUP // lax.axis_size("dp")
    base = lax.axis_index("dp") * span + pl.program_id(0) * groups
    my_half = lax.axis_index("blk") // 2
    for index in range(groups):
        source = pl.ds(pl.multiple_of(table[base + index] * GROUP, GROUP), GROUP)
        rows = slice(index * GROUP, (index + 1) * GROUP)
        updated = adamw(
            weight_ref[rows, :],
            home_ref[source, :].astype(jnp.float32),
            mean_ref[rows, :],
            square_ref[rows, :],
            rate_first,
        )
        new_ref[rows, :], new_mean_ref[rows, :], new_square_ref[rows, :] = updated
    for half in range(2):

        @pl.when(my_half == half)
        def _(half=half):
            features_ref[:, half * HALF : (half + 1) * HALF] = kept_ref[...]
            features_ref[:, (1 - half) * HALF : (2 - half) * HALF] = far_ref[...].astype(
                jnp.float32
            )


def finish(home, kept, far, first_weight, first_mean, first_square, n_dp):
    cols = first_weight.shape[1]
    steps = 7
    table = jnp.asarray(group_sources(n_dp).reshape(-1))
    block = pl.BlockSpec((first_weight.shape[0] // steps, cols), lambda i: (i, 0))
    shape = jax.ShapeDtypeStruct(first_weight.shape, jnp.float32)
    cells = kept.shape[0]
    some = -(-cells // steps // 16) * 16
    part = pl.BlockSpec((some, HALF), lambda i: (i, 0))
    return pl.pallas_call(
        finish_kernel,
        grid=(steps,),
        out_shape=(shape, shape, shape, jax.ShapeDtypeStruct((cells, C), jnp.float32)),
        in_specs=[
            pl.BlockSpec(memory_space=pltpu.SMEM),
            pl.BlockSpec(memory_space=pltpu.VMEM),
            block,
            block,
            block,
            part,
            part,
        ],
        out_specs=(block, block, block, pl.BlockSpec((some, C), lambda i: (i, 0))),
        compiler_params=pltpu.CompilerParams(vmem_limit_bytes=VMEM_LIMIT),
        name="finish",
    )(table, home, first_weight, first_mean, first_square, kept, far)


def on_device(
    features,
    roi_table,
    offsets,
    box_targets,
    first_weight,
    first_mean,
    first_square,
    second_weight,
    second_mean,
    second_square,
    out_weight,
    out_mean,
    out_square,
    biases,
    bias_mean,
    bias_square,
    n_dp,
    n_blk,
):
    place = lax.axis_index("blk")
    half = place // 2
    parity = place % 2
    roi_count = roi_table.shape[1]
    outw = out_weight.shape[1]
    rois = jnp.concatenate((roi_table.astype(jnp.float32), box_targets), axis=0)
    weight, all_rois = gather_quarter(first_weight, second_weight, rois, n_dp)
    valid_here = jnp.sum(all_rois[7])
    if not by_groups(n_dp):
        valid_here = lax.psum(valid_here, "dp")
    predict = jnp.pad(out_weight.astype(jnp.bfloat16), ((0, 0), (0, HALF - outw)))
    bias = jnp.zeros((8, H), jnp.float32)
    bias = bias.at[0].set(biases[:H]).at[1].set(biases[H : 2 * H]).at[2, :outw].set(biases[2 * H :])

    table, targets, starts = sort_rois(all_rois[:8].astype(jnp.int32), all_rois[8:])
    lows = window_lows(offsets)
    row_sevens, col_sevens, rows_at, cols_at = sample_points(table, offsets, parity)
    apart = ((0, 0), (0, 64 - 7))
    points = jnp.concatenate((jnp.pad(row_sevens, apart), jnp.pad(col_sevens, apart)), axis=1)

    def by_group(values):
        return values[:, :MAIN].reshape(-1, BATCH, MAIN).transpose(0, 2, 1).reshape(-1, LANES)

    my_table = lax.dynamic_slice_in_dim(table, place * roi_count, roi_count, axis=1)
    my_targets = lax.dynamic_slice_in_dim(targets, place * roi_count, roi_count, axis=0)
    aux = jnp.concatenate(
        (
            my_table[6].astype(jnp.float32)[:, None],
            my_table[7].astype(jnp.float32)[:, None],
            jnp.zeros((roi_count, CLASSES - 2), jnp.float32),
            my_targets,
            jnp.broadcast_to(valid_here, (roi_count, 1)),
            jnp.zeros((roi_count, HALF - CLASSES - 5), jnp.float32),
        ),
        axis=1,
    )
    meta = jnp.stack((half, parity, lax.axis_index("dp") % 2))
    pooled = pool(features, meta, starts, lows, points)
    all_grad, second_wgrad, tail, ordered = middle(
        pooled, *weight, predict, bias, aux, n_dp
    )
    second_part = lax.psum_scatter(second_wgrad, "dp", scatter_dimension=0, tiled=True)
    if by_groups(n_dp):
        here, there, later = weight_grad(pooled, all_grad, meta, n_dp)
        swapped = lax.ppermute(there, "dp", [(spot, spot ^ 1) for spot in range(n_dp)])
    cell_grads = spread(
        all_grad,
        ordered,
        starts,
        lows,
        (
            by_group(rows_at),
            by_group(cols_at),
            rows_at[:, MAIN].reshape(-1, HALF),
            cols_at[:, MAIN].reshape(-1, HALF),
        ),
        features.shape[0],
    )
    if by_groups(n_dp):
        home, second_sum, tails, kept, far = reduce_home(
            here, swapped, later, tail, second_part, cell_grads, n_dp
        )
        first_new, first_mean_new, first_square_new, feature_grads = finish(
            home, kept, far, first_weight, first_mean, first_square, n_dp
        )
        tails = tails.reshape(n_blk, n_dp, -1, HALF)
        out_sum = tails[:, :, : -8].reshape(H, HALF)[:, :outw]
        bias_flat = tails[:, :, -8].reshape(-1)
    else:
        first_new, first_mean_new, first_square_new = adamw(
            first_weight, sum_apart(pooled, all_grad, n_blk), first_mean, first_square, rate_first
        )
        parts = lax.all_to_all(
            cell_grads.reshape(n_blk, -1, HALF), "blk", split_axis=0, concat_axis=0, tiled=True
        ).astype(jnp.float32)
        feature_grads = jnp.concatenate((parts[0] + parts[1], parts[2] + parts[3]), axis=1)
        second_sum = lax.psum_scatter(second_part, "blk", scatter_dimension=1, tiled=True)
        second_sum = second_sum.astype(jnp.float32)
        tails = lax.psum(tail, ("dp", "blk"))
        out_sum = tails[:, : H // n_blk].reshape(H, HALF)[:, :outw]
        bias_flat = tails[:, H // n_blk :].reshape(-1)
    bias_sum = bias_flat[: biases.shape[0]]
    total_loss = bias_flat[biases.shape[0]]

    second_new, second_mean_new, second_square_new = adamw(
        second_weight, second_sum, second_mean, second_square, rate_second
    )
    out_new, out_mean_new, out_square_new = adamw(
        out_weight, out_sum, out_mean, out_square, rate_out
    )
    bias_new, bias_mean_new, bias_square_new = adamw(
        biases, bias_sum, bias_mean, bias_square, rate_bias
    )
    return (
        feature_grads,
        total_loss,
        first_new,
        first_mean_new,
        first_square_new,
        second_new,
        second_mean_new,
        second_square_new,
        out_new,
        out_mean_new,
        out_square_new,
        bias_new,
        bias_mean_new,
        bias_square_new,
    )


def solution(mesh):
    in_specs = (
        P("dp", None),
        P(None, ("dp", "blk")),
        P(None, "dp"),
        P(None, ("dp", "blk")),
        P("dp", "blk"),
        P("dp", "blk"),
        P("dp", "blk"),
        P("dp", "blk"),
        P("dp", "blk"),
        P("dp", "blk"),
        P(),
        P(),
        P(),
        P(),
        P(),
        P(),
    )
    out_specs = (
        P(("dp", "blk"), None),
        P(),
        P("dp", "blk"),
        P("dp", "blk"),
        P("dp", "blk"),
        P("dp", "blk"),
        P("dp", "blk"),
        P("dp", "blk"),
        P(),
        P(),
        P(),
        P(),
        P(),
        P(),
    )
    return jax.shard_map(
        functools.partial(on_device, n_dp=mesh.shape["dp"], n_blk=mesh.shape["blk"]),
        mesh=mesh,
        in_specs=in_specs,
        out_specs=out_specs,
        check_vma=False,
    )
```

```python
import functools

import jax
import jax.numpy as jnp
import numpy as np
from jax import lax
from jax.experimental import pallas as pl
from jax.experimental.pallas import tpu as pltpu
from jax.sharding import PartitionSpec as P

C = 256
H = 1024
CLASSES = 81
CANVAS = 512
IMAGES = 4
LEVELS = 4
STEP = 10
K1 = 12544
BINS = 49

HALF = 128
SLOTS = 26
KQ = SLOTS * HALF
FAR = -1.0e6
BATCH = 16
LANES = 512
SIDES = (128, 64, 32, 16)
BASES = (0, 16384, 20480, 21504)
WIN_ROWS = (52, 28, 16, 16)
WIN_COLS = (64, 32, 16, 16)
BACK_COLS = (56, 32, 16, 16)
VMEM_LIMIT = 60 * 1024 * 1024
GROUP = 32
OWNED = 13
SHARD = OWNED + 1
AHEAD = H // 2
SWAPPED = 9
LATER = OWNED - SWAPPED
AHEAD_ROWS = (OWNED + 2) * GROUP
MESH = pl.DeviceIdType.MESH

third = 1.0 / 3.0
rate_first = 0.018
rate_second = 0.06
rate_out = 0.18
rate_bias = 0.2


def contract_rows(left_side, right_side):
    return lax.dot_general(
        left_side, right_side, (((0,), (0,)), ((), ())), preferred_element_type=jnp.float32
    )


def contract_cols(left_side, right_side):
    return lax.dot_general(
        left_side, right_side, (((1,), (1,)), ((), ())), preferred_element_type=jnp.float32
    )


def sort_rois(roi_table, box_targets):
    count = roi_table.shape[1]
    key = roi_table[5] * IMAGES + roi_table[4]
    place = jnp.arange(count, dtype=jnp.int32)
    before = (key[None, :] < key[:, None]) | (
        (key[None, :] == key[:, None]) & (place[None, :] < place[:, None])
    )
    rank = jnp.sum(before.astype(jnp.int32), axis=1)
    segments = jnp.arange(LEVELS * IMAGES + 1, dtype=jnp.int32)
    starts = jnp.sum((key[None, :] < segments[:, None]).astype(jnp.int32), axis=1)
    rows = jnp.concatenate((roi_table.astype(jnp.float32), box_targets), axis=0)
    pick = (rank[None, :] == place[:, None]).astype(jnp.float32)
    ordered = lax.dot_general(
        pick, rows, (((1,), (1,)), ((), ())), precision=lax.Precision.HIGHEST
    )
    return ordered[:, :8].astype(jnp.int32).T, ordered[:, 8:], starts


def sample_points(table, offsets, parity):
    level_of = table[5]
    image_of = table[4]
    choose = (image_of[:, None] == jnp.arange(IMAGES, dtype=jnp.int32)[None, :]).astype(jnp.int32)
    shift_y = jnp.sum(choose * offsets[0][None, :], axis=1)
    shift_x = jnp.sum(choose * offsets[1][None, :], axis=1)
    grid_side = jnp.right_shift(jnp.full_like(level_of, CANVAS // 4), level_of)
    stride_px = (4 * jnp.left_shift(jnp.ones_like(level_of), level_of)).astype(jnp.float32)
    bins = 2 * jnp.arange(SLOTS, dtype=jnp.int32) + parity
    inside = bins < BINS
    every = jnp.arange(7, dtype=jnp.int32)

    def axis_points(low_edge, high_edge, shift_by, which, keep):
        centres = (which.astype(jnp.float32) + 0.5) / 7.0
        start_px = (low_edge + shift_by).astype(jnp.float32)
        extent = (high_edge - low_edge).astype(jnp.float32)
        points = start_px[:, None] + centres[None, :] * extent[:, None]
        limit_max = (grid_side - 1).astype(jnp.float32)[:, None]
        scaled = jnp.clip(points / stride_px[:, None] - 0.5, 0.0, limit_max)
        return jnp.where(keep[None, :], scaled, FAR)

    rows = (table[1], table[3], shift_y)
    cols = (table[0], table[2], shift_x)
    return (
        axis_points(*rows, every, every >= 0),
        axis_points(*cols, every, every >= 0),
        axis_points(*rows, bins // 7, inside),
        axis_points(*cols, bins % 7, inside),
    )


def window_lows(offsets):
    lows = []
    for level in range(LEVELS - 1):
        half_stride = 2 << level
        lows.append(jnp.maximum(jnp.right_shift(offsets - half_stride, 2 + level), 0))
    lows.append(jnp.zeros_like(offsets))
    return jnp.stack(lows, axis=1).reshape(-1)


def segment_loop(starts, lows, visit):
    for level in range(LEVELS):

        def image_step(image, carry, level=level):
            segment = level * IMAGES + image
            begin = starts[segment]
            end = starts[segment + 1]
            row_low = lows[level * IMAGES + image]
            col_low = lows[(LEVELS + level) * IMAGES + image]

            @pl.when(end > begin)
            def _():
                visit(level, begin, end, row_low, col_low)

            return carry

        lax.fori_loop(0, IMAGES, image_step, 0)


def hat(distance):
    return jnp.maximum(1.0 - jnp.abs(distance), 0.0)


def pool_kernel(starts, lows, meta, feat_hbm, uv_ref, out_ref, raw, cells, win, acc, sem):
    total = raw.shape[0]
    lane0 = pl.multiple_of(meta[0] * HALF, HALF)
    fetch = pltpu.make_async_copy(feat_hbm.at[:, pl.ds(lane0, HALF)], raw, sem)
    fetch.start()
    count = acc.shape[0]

    def clear(step, carry):
        acc[pl.ds(pl.multiple_of(step * 8, 8), 8), :] = jnp.zeros((8, KQ), jnp.float32)
        return carry

    lax.fori_loop(0, count // 8, clear, 0)
    fetch.wait()

    def widen(step, carry):
        rows = pl.ds(pl.multiple_of(step * 128, 128), 128)
        cells[rows, :] = raw[rows, :].astype(jnp.float32)
        return carry

    lax.fori_loop(0, total // 128, widen, 0)

    def visit(level, begin, end, row_low, col_low):
        side, base = SIDES[level], BASES[level]
        height, width = WIN_ROWS[level], WIN_COLS[level]
        shift = width.bit_length() - 1
        per_tile = HALF // width
        tiles = height // per_tile
        depth = tiles * HALF

        def take(row, carry):
            source = pl.ds(base + (row_low + row) * side + col_low, width)
            target = pl.ds(pl.multiple_of(row * width, width), width)
            win[target, :] = cells[source, :].astype(jnp.bfloat16)
            return carry

        lax.fori_loop(0, height, take, 0)
        row_shift = row_low.astype(jnp.float32)
        col_shift = col_low.astype(jnp.float32)

        def group(parity, step, carry):
            first = pl.multiple_of(step * BATCH, BATCH)
            lane = lax.broadcasted_iota(jnp.int32, (BATCH, HALF), 1)
            lane_row = jnp.right_shift(lane, shift).astype(jnp.float32) + row_shift
            lane_col = jnp.bitwise_and(lane, width - 1).astype(jnp.float32) + col_shift
            roi = first + lax.broadcasted_iota(jnp.int32, (BATCH, HALF), 0)
            mine = (roi >= begin) & (roi < end)
            points = jnp.where(mine, uv_ref[pl.ds(first, BATCH), :], FAR)
            row_at = [points[:, a : a + 1] - lane_row for a in range(7)]
            col_hats = [hat(points[:, 64 + b : 65 + b] - lane_col) for b in range(7)]
            bins = [2 * slot + parity for slot in range(SLOTS)]
            pooled = None
            for begin_tile in range(0, tiles, 4):
                columns = []
                for tile in range(begin_tile, min(begin_tile + 4, tiles)):
                    row_hats = [hat(at - float(tile * per_tile)) for at in row_at]
                    weights = [
                        (row_hats[one // 7] * col_hats[one % 7]).astype(jnp.bfloat16)
                        if one < BINS
                        else jnp.zeros((BATCH, HALF), jnp.bfloat16)
                        for one in bins
                    ]
                    columns.append(jnp.concatenate(weights, axis=0))
                part = jnp.dot(
                    jnp.concatenate(columns, axis=1),
                    win[begin_tile * HALF : (begin_tile + len(columns)) * HALF, :],
                    preferred_element_type=jnp.float32,
                )
                pooled = part if pooled is None else pooled + part
            for slot in range(SLOTS):
                where = (pl.ds(first, BATCH), slice(slot * HALF, (slot + 1) * HALF))
                acc[where] = acc[where] + pooled[slot * BATCH : (slot + 1) * BATCH, :]
            return carry

        for parity in (0, 1):

            @pl.when(meta[1] == parity)
            def _(parity=parity):
                lax.fori_loop(
                    begin // BATCH, (end + BATCH - 1) // BATCH, functools.partial(group, parity), 0
                )

    segment_loop(starts, lows, visit)

    def narrow(step, carry):
        rows = pl.ds(pl.multiple_of(step * 16, 16), 16)
        out_ref[rows, :] = acc[rows, :].astype(jnp.bfloat16)
        return carry

    lax.fori_loop(0, count // 16, narrow, 0)


def pool(features, meta, starts, lows, points):
    count = points.shape[0]
    cells = features.shape[0]
    return pl.pallas_call(
        pool_kernel,
        out_shape=jax.ShapeDtypeStruct((count, KQ), jnp.bfloat16),
        in_specs=[
            pl.BlockSpec(memory_space=pltpu.SMEM),
            pl.BlockSpec(memory_space=pltpu.SMEM),
            pl.BlockSpec(memory_space=pltpu.SMEM),
            pl.BlockSpec(memory_space=pl.ANY),
            pl.BlockSpec(memory_space=pltpu.VMEM),
        ],
        out_specs=pl.BlockSpec(memory_space=pltpu.VMEM),
        scratch_shapes=[
            pltpu.VMEM((cells, HALF), jnp.bfloat16),
            pltpu.VMEM((cells, HALF), jnp.float32),
            pltpu.VMEM((KQ, HALF), jnp.bfloat16),
            pltpu.VMEM((count, KQ), jnp.float32),
            pltpu.SemaphoreType.DMA,
        ],
        compiler_params=pltpu.CompilerParams(vmem_limit_bytes=VMEM_LIMIT),
        cost_estimate=pl.CostEstimate(
            flops=40_000_000_000, bytes_accessed=13_000_000, transcendentals=0
        ),
        name="pool_bins",
    )(starts, lows, meta, features, points)


def spread_kernel(
    starts,
    lows,
    grad_ref,
    weight_hbm,
    row_ref,
    col_ref,
    out_ref,
    weight_ref,
    pooled,
    cells,
    part,
    row_hat,
    right,
    weight_sem,
):
    total = cells.shape[0]
    fetch = pltpu.make_async_copy(weight_hbm, weight_ref, weight_sem)
    fetch.start()

    def clear(step, carry):
        rows = pl.ds(pl.multiple_of(step * 128, 128), 128)
        cells[rows, :] = jnp.zeros((128, HALF), jnp.float32)
        return carry

    lax.fori_loop(0, total // 128, clear, 0)
    fetch.wait()

    def back_dot(step, carry):
        cols = pl.ds(pl.multiple_of(step * 256, 256), 256)
        pooled[:, cols] = contract_cols(grad_ref[...], weight_ref[cols, :]).astype(jnp.bfloat16)
        return carry

    lax.fori_loop(0, KQ // 256, back_dot, 0)
    right[SLOTS * BATCH :, :] = jnp.zeros((LANES - SLOTS * BATCH, HALF), jnp.bfloat16)

    def visit(level, begin, end, row_low, col_low):
        side, base = SIDES[level], BASES[level]
        height, width = WIN_ROWS[level], BACK_COLS[level]
        chunk = (26, 28, 16, 16)[level]
        row_shift = row_low.astype(jnp.float32)
        col_shift = col_low.astype(jnp.float32)

        def wipe(row, carry):
            rows = pl.ds(pl.multiple_of(row * width, 8), width)
            part[rows, :] = jnp.zeros((width, HALF), jnp.float32)
            return carry

        lax.fori_loop(0, height, wipe, 0)

        def group(step, carry):
            first = pl.multiple_of(step * BATCH, BATCH)
            for slot in range(SLOTS):
                right[slot * BATCH : (slot + 1) * BATCH, :] = pooled[
                    pl.ds(first, BATCH), slot * HALF : (slot + 1) * HALF
                ]
            lane = lax.broadcasted_iota(jnp.int32, (1, LANES), 1)
            roi = first + jnp.bitwise_and(lane, BATCH - 1)
            mine = (roi >= begin) & (roi < end)
            row_at = jnp.where(mine, row_ref[pl.ds(step, 1), :], FAR) - row_shift
            col_at = jnp.where(mine, col_ref[pl.ds(step, 1), :], FAR) - col_shift
            row_hat[...] = hat(
                row_at - lax.broadcasted_iota(jnp.int32, (56, LANES), 0).astype(jnp.float32)
            )
            col_hat = hat(
                col_at - lax.broadcasted_iota(jnp.int32, (width, LANES), 0).astype(jnp.float32)
            )
            for row in range(0, height, chunk):
                left = jnp.concatenate(
                    [col_hat * row_hat[row + one : row + one + 1, :] for one in range(chunk)], axis=0
                ).astype(jnp.bfloat16)
                rows = slice(row * width, (row + chunk) * width)
                part[rows, :] += jnp.dot(left, right[...], preferred_element_type=jnp.float32)
            return carry

        lax.fori_loop(begin // BATCH, (end + BATCH - 1) // BATCH, group, 0)

        def flush(row, carry):
            target = pl.ds(base + (row_low + row) * side + col_low, width)
            source = pl.ds(pl.multiple_of(row * width, 8), width)
            cells[target, :] = cells[target, :] + part[source, :]
            return carry

        lax.fori_loop(0, height, flush, 0)

    segment_loop(starts, lows, visit)

    def narrow(step, carry):
        rows = pl.ds(pl.multiple_of(step * 128, 128), 128)
        out_ref[rows, :] = (cells[rows, :] * third).astype(jnp.bfloat16)
        return carry

    lax.fori_loop(0, total // 128, narrow, 0)


def spread(first_grad, weight, starts, lows, rows_at, cols_at, cells):
    count = first_grad.shape[0]
    return pl.pallas_call(
        spread_kernel,
        out_shape=jax.ShapeDtypeStruct((cells, HALF), jnp.bfloat16),
        in_specs=[
            pl.BlockSpec(memory_space=pltpu.SMEM),
            pl.BlockSpec(memory_space=pltpu.SMEM),
            pl.BlockSpec(memory_space=pltpu.VMEM),
            pl.BlockSpec(memory_space=pl.ANY),
            pl.BlockSpec(memory_space=pltpu.VMEM),
            pl.BlockSpec(memory_space=pltpu.VMEM),
        ],
        out_specs=pl.BlockSpec(memory_space=pltpu.VMEM),
        scratch_shapes=[
            pltpu.VMEM((KQ, H), jnp.bfloat16),
            pltpu.VMEM((count, KQ), jnp.bfloat16),
            pltpu.VMEM((cells, HALF), jnp.float32),
            pltpu.VMEM((WIN_ROWS[0] * BACK_COLS[0], HALF), jnp.float32),
            pltpu.VMEM((56, LANES), jnp.float32),
            pltpu.VMEM((LANES, HALF), jnp.bfloat16),
            pltpu.SemaphoreType.DMA,
        ],
        compiler_params=pltpu.CompilerParams(vmem_limit_bytes=VMEM_LIMIT),
        cost_estimate=pl.CostEstimate(
            flops=40_000_000_000, bytes_accessed=15_000_000, transcendentals=0
        ),
        name="spread_bins",
    )(starts, lows, first_grad, weight, rows_at, cols_at)


def adamw(weight, gradient, moment, square, step_rate):
    new_mean = 0.9 * moment + 0.1 * gradient
    new_square = 0.999 * square + 0.001 * gradient * gradient
    mean_hat = new_mean / (1.0 - 0.9**STEP)
    square_hat = new_square / (1.0 - 0.999**STEP)
    new_weight = weight - step_rate * (mean_hat / (jnp.sqrt(square_hat) + 1e-08) + 0.0001 * weight)
    return (new_weight, new_mean, new_square)


def groups_before(half, parity, index):
    inside = index % 16 - (8 * parity + 4 * half)
    return index // 16 * 4 + jnp.minimum(jnp.maximum(inside, 0), 4)


def group_place(half, parity, slot, part, n_dp):
    span = K1 // GROUP // n_dp

    def earlier(index):
        inside = jnp.bitwise_and(index, 15) - (8 * parity + 4 * half)
        return jnp.right_shift(index, 4) * 4 + jnp.minimum(jnp.maximum(inside, 0), 4)

    group = 8 * (2 * slot + parity) + 4 * half + part
    owner = sum((group >= span * other).astype(jnp.int32) for other in range(1, n_dp))
    return owner, earlier(group) - earlier(owner * span)


def owned_groups(n_dp):
    span = K1 // GROUP // n_dp
    table = np.zeros((n_dp, 4, OWNED), np.int32)
    for owner in range(n_dp):
        for quarter in range(4):
            found = [
                local
                for local in range(span)
                if (owner * span + local) // 8 % 2 == quarter % 2
                and (owner * span + local) % 8 // 4 == quarter // 2
            ]
            table[owner, quarter] = (found + [0] * OWNED)[:OWNED]
    return table


def group_sources(n_dp):
    span = K1 // GROUP // n_dp
    table = np.zeros((n_dp, span), np.int32)
    for owner in range(n_dp):
        met = [0] * 4
        for local in range(span):
            group = owner * span + local
            quarter = group % 8 // 4 * 2 + group // 8 % 2
            table[owner, local] = quarter * OWNED + met[quarter]
            met[quarter] += 1
    return table


def by_groups(n_dp):
    return n_dp == 8


def deal_kernel(table, weight_ref, rois_ref, out_ref):
    base = lax.axis_index("dp") * 4 * OWNED
    for quarter in range(4):

        def step(index, carry, quarter=quarter):
            source = pl.ds(
                pl.multiple_of(table[base + quarter * OWNED + index] * GROUP, GROUP), GROUP
            )
            target = pl.ds(pl.multiple_of(index * GROUP, GROUP), GROUP)
            out_ref[quarter, target, :] = weight_ref[source, :].astype(jnp.bfloat16)
            return carry

        lax.fori_loop(0, OWNED, step, 0)
        out_ref[quarter, OWNED * GROUP :, :] = rois_ref[...]


def gather_quarter(first_weight, second_weight, rois, n_dp):
    cols = first_weight.shape[1]
    second = second_weight.astype(jnp.bfloat16)
    if by_groups(n_dp):
        table = jnp.asarray(owned_groups(n_dp).reshape(-1))
        top = lax.optimization_barrier(rois[8:].astype(jnp.bfloat16))
        rest = rois[8:] - top.astype(jnp.float32)
        middle_term = lax.optimization_barrier(rest.astype(jnp.bfloat16))
        last = (rest - middle_term.astype(jnp.float32)).astype(jnp.bfloat16)
        riders = jnp.concatenate((rois[:8].astype(jnp.bfloat16), top, middle_term, last), axis=0)
        riders = jnp.pad(riders, ((0, GROUP - riders.shape[0]), (0, 0)))
        dealt = pl.pallas_call(
            deal_kernel,
            out_shape=jax.ShapeDtypeStruct((4, SHARD * GROUP, cols), jnp.bfloat16),
            in_specs=[
                pl.BlockSpec(memory_space=pltpu.SMEM),
                pl.BlockSpec(memory_space=pltpu.VMEM),
                pl.BlockSpec(memory_space=pltpu.VMEM),
            ],
            out_specs=pl.BlockSpec(memory_space=pltpu.VMEM),
            name="deal_rows",
        )(table, first_weight, riders)
        swapped = lax.all_to_all(dealt, "blk", split_axis=0, concat_axis=0, tiled=True)
        ridden = swapped[:, OWNED * GROUP :].astype(jnp.float32).transpose(1, 0, 2)
        ridden = ridden.reshape(GROUP, -1)
        all_rois = jnp.concatenate(
            (ridden[:8], (ridden[8:12] + ridden[12:16]) + ridden[16:20]), axis=0
        )
        rows = swapped[:, : OWNED * GROUP].transpose(1, 0, 2).reshape(OWNED * GROUP, -1)
        block = second.reshape(2, 2, GROUP, cols).transpose(0, 2, 1, 3).reshape(2 * GROUP, -1)
        ahead = jnp.concatenate((rows[:, :AHEAD], block), axis=0)
        gathered = lax.all_gather(ahead, "dp", axis=0, tiled=True)
        behind = rows[:, AHEAD:]
        swapped = lax.ppermute(behind, "dp", [(spot, spot ^ 1) for spot in range(n_dp)])
        return (gathered, behind, swapped), all_rois
    all_rois = lax.all_gather(rois, "blk", axis=1, tiled=True)
    rows = lax.all_gather(first_weight.astype(jnp.bfloat16), "dp", axis=0, tiled=True)
    split = jnp.pad(rows.reshape(BINS, C, cols), ((0, 2 * SLOTS - BINS), (0, 0), (0, 0)))
    split = split.reshape(SLOTS, 2, 2, HALF, cols).transpose(2, 1, 0, 3, 4)
    split = split.reshape(4, KQ, cols)
    mine = lax.all_to_all(split, "blk", split_axis=0, concat_axis=0, tiled=True)
    mine = mine.transpose(1, 0, 2).reshape(KQ, -1)
    second = lax.all_gather(second, "dp", axis=0, tiled=True)
    block = second.reshape(4, -1, cols).transpose(1, 0, 2).reshape(-1, 4 * cols)
    rows = jnp.concatenate((mine, block), axis=0)
    return (rows, rows, rows), all_rois


def second_blocks(source, target, column, sem, n_dp):
    owners, rows = (n_dp, GROUP) if by_groups(n_dp) else (1, H // 4)
    copies = []
    for owner in range(owners):
        for part in range(4):
            if by_groups(n_dp):
                first = owner * AHEAD_ROWS + (OWNED + part // 2) * GROUP
                lane = part % 2 * 256
            else:
                first, lane = KQ, part * 256
            copies.append(
                pltpu.make_async_copy(
                    source.at[pl.ds(first, rows), pl.ds(lane, 256)],
                    target.at[pl.ds((owner * 4 + part) * rows, rows), column],
                    sem.at[owner * 4 + part],
                )
            )
    return copies


def owner_rows(half, parity, owner, n_dp):
    span = K1 // GROUP // n_dp
    begin = groups_before(half, parity, owner * span)
    end = groups_before(half, parity, (owner + 1) * span)
    many = pl.ds(pl.multiple_of(begin * GROUP, GROUP), (OWNED - 1) * GROUP)
    last = pl.ds(pl.multiple_of((end - 1) * GROUP, GROUP), GROUP)
    return many, last, end - begin == OWNED


def ahead_copies(source, target, sems, half, parity, n_dp):
    copies = []
    for owner in range(n_dp):
        many, last, full = owner_rows(half, parity, owner, n_dp)
        first, rows = owner * AHEAD_ROWS, (OWNED - 1) * GROUP
        copies.append(
            (
                None,
                pltpu.make_async_copy(
                    source.at[pl.ds(first, rows), :], target.at[many, :], sems.at[2 * owner]
                ),
            )
        )
        copies.append(
            (
                full,
                pltpu.make_async_copy(
                    source.at[pl.ds(first + rows, GROUP), :],
                    target.at[last, :],
                    sems.at[2 * owner + 1],
                ),
            )
        )
    return copies


def whole_copies(source, targets, sems):
    return [
        (
            None,
            pltpu.make_async_copy(
                source.at[pl.ds(0, KQ), pl.ds(half * AHEAD, AHEAD)], target, sems.at[half]
            ),
        )
        for half, target in enumerate(targets)
    ]


def each_copy(copies, action):
    for condition, copy in copies:
        if condition is None:
            action(copy)
        else:

            @pl.when(condition)
            def _(copy=copy):
                action(copy)


def wipe_slots(target, parity):
    target[KQ - HALF :, :] = jnp.zeros((HALF, AHEAD), jnp.bfloat16)

    @pl.when(parity == 1)
    def _():
        target[KQ - 2 * HALF : KQ - HALF, :] = jnp.zeros((HALF, AHEAD), jnp.bfloat16)


def gelu_parts(values):
    cdf = 0.5 * (1.0 + lax.erf(values * np.float32(np.sqrt(0.5))))
    density = jnp.exp(-0.5 * values * values) * np.float32(1.0 / np.sqrt(2.0 * np.pi))
    return values * cdf, cdf + values * density


def middle_kernel(
    n_dp,
    pooled_hbm,
    ahead_hbm,
    behind_hbm,
    swapped_hbm,
    predict_ref,
    bias_ref,
    aux_ref,
    all_grad,
    second_out,
    tail_ref,
    ordered_hbm,
    pooled,
    ahead,
    behind,
    second_ref,
    part,
    sent,
    came,
    first_pre,
    second_pre,
    first_act,
    second_act,
    first_grad,
    second_grad,
    valid_came,
    pooled_sem,
    weight_sem,
    own_sem,
    second_sem,
    out_sem,
    up_send,
    up_recv,
    down_send,
    down_recv,
    y_send,
    y_recv,
    valid_send,
    valid_recv,
    send_sem,
    recv_sem,
):
    me = lax.axis_index("blk")
    dp = lax.axis_index("dp")
    peers = [(dp + step) % n_dp for step in range(1, n_dp)] if by_groups(n_dp) else []
    high, low = me // 2, me % 2
    sibling = high * 2 + (1 - low)
    across = (1 - high) * 2 + low
    corner = (1 - high) * 2 + (1 - low)
    rows = part.shape[0]
    quarter = H // 4

    barrier = pltpu.get_barrier_semaphore()
    for other in (sibling, across, corner):
        pl.semaphore_signal(barrier, inc=1, device_id={"blk": other}, device_id_type=MESH)
    for peer in peers:
        pl.semaphore_signal(barrier, inc=1, device_id={"dp": peer}, device_id_type=MESH)

    def hidden_cols(which):
        return pl.ds(pl.multiple_of(which * quarter, quarter), quarter)

    z, y = dp // 2, dp % 2
    partner = 2 * z + 1 - y
    shard = (OWNED - 1) * GROUP

    def shard_pieces(owner):
        many, last, full = owner_rows(high, low, owner, n_dp)
        first = many.start
        return (
            (None, pl.ds(pl.multiple_of(first, GROUP), shard // 2), pl.ds(0, shard // 2)),
            (
                None,
                pl.ds(pl.multiple_of(first + shard // 2, GROUP), shard // 2),
                pl.ds(shard // 2, shard // 2),
            ),
            (full, last, pl.ds(shard, GROUP)),
        )

    def shard_copies(owner, send, recv, index, target, own=False):
        copies = []
        for piece, (condition, place, source) in enumerate(shard_pieces(owner)):
            copies.append(
                (
                    condition,
                    pltpu.make_async_remote_copy(
                        src_ref=behind_hbm.at[source, :] if own else behind.at[place, :],
                        dst_ref=behind.at[place, :],
                        send_sem=send.at[3 * index + piece],
                        recv_sem=recv.at[3 * index + piece],
                        device_id={"dp": target},
                        device_id_type=MESH,
                    ),
                )
            )
        return copies

    def own_shard(action):
        @pl.when(z < 3)
        def _():
            each_copy(shard_copies(dp, up_send, up_recv, 0, dp + 2, True), action)

        @pl.when(z > 0)
        def _():
            each_copy(shard_copies(dp, down_send, down_recv, 0, dp - 2, True), action)

    def relay_shards(distance, took, action):
        def pass_on(owner, send, recv, neighbour, goes_on, place):
            coming = shard_copies(owner, send, recv, distance - 1, neighbour)
            aside = shard_copies(owner, y_send, y_recv, place, partner)
            onward = [None] * len(coming)
            if distance < 3:
                onward = shard_copies(owner, send, recv, distance, neighbour)
            for came_in, on, over in zip(coming, onward, aside):
                each_copy([came_in], took)
                if on is not None:

                    @pl.when(goes_on)
                    def _(on=on):
                        each_copy([on], action)

                each_copy([over], action)

        @pl.when(z >= distance)
        def _():
            pass_on(dp - 2 * distance, up_send, up_recv, dp + 2, z < 3, z - distance)

        @pl.when(z + distance <= 3)
        def _():
            pass_on(dp + 2 * distance, down_send, down_recv, dp - 2, z > 0, z + distance)

    def serve(distance):
        if by_groups(n_dp):
            relay_shards(distance, lambda copy: copy.wait_recv(), lambda copy: copy.start())

    blocks = second_blocks(ahead_hbm, second_ref, hidden_cols(me), second_sem, n_dp)
    for copy in blocks:
        copy.start()
    if by_groups(n_dp):
        early = ahead_copies(ahead_hbm, ahead, weight_sem, high, low, n_dp)
        late = []
        for which, (source_hbm, owner) in enumerate(((behind_hbm, dp), (swapped_hbm, partner))):
            for piece, (condition, place, source) in enumerate(shard_pieces(owner)):
                late.append(
                    (
                        condition,
                        pltpu.make_async_copy(
                            source_hbm.at[source, :],
                            behind.at[place, :],
                            out_sem.at[2 + 3 * which + piece],
                        ),
                    )
                )
        wipe_slots(ahead, low)
        wipe_slots(behind, low)
    else:
        early, late = whole_copies(ahead_hbm, (ahead, behind), weight_sem), []
    each_copy((*early, *late), lambda copy: copy.start())

    def chunk_rows(which):
        return pl.ds(pl.multiple_of(which * rows, 16), rows)

    order = (corner, across, sibling, me)
    chunks = [
        pltpu.make_async_copy(
            pooled_hbm.at[chunk_rows(which), :], pooled.at[chunk_rows(which), :], pooled_sem.at[i]
        )
        for i, which in enumerate(order)
    ]
    for chunk in chunks:
        chunk.start()
    pl.semaphore_wait(barrier, 3 + len(peers))
    counts = [
        pltpu.make_async_remote_copy(
            src_ref=aux_ref.at[pl.ds(0, 8), :],
            dst_ref=valid_came.at[index],
            send_sem=valid_send.at[index],
            recv_sem=valid_recv.at[index],
            device_id={"dp": peer},
            device_id_type=MESH,
        )
        for index, peer in enumerate(peers)
    ]
    if by_groups(n_dp):
        own_shard(lambda copy: copy.start())
    for copy in counts:
        copy.start()

    def remote(source, target, index, other):
        return pltpu.make_async_remote_copy(
            src_ref=source,
            dst_ref=target,
            send_sem=send_sem.at[index],
            recv_sem=recv_sem.at[index],
            device_id={"blk": other},
            device_id_type=MESH,
        )

    for copy in blocks:
        copy.wait()
    mine, theirs = second_ref.at[:, hidden_cols(me)], second_ref.at[:, hidden_cols(across)]
    second_sibling = remote(mine, mine, 3, sibling)
    second_across = remote(mine, mine, 4, across)
    second_forward = remote(theirs, theirs, 5, sibling)
    second_across.start()
    second_sibling.start()

    def in_blocks(count, body):
        def step(index, carry):
            body(index)
            return carry

        lax.fori_loop(0, count, step, 0)

    def block32(step):
        return pl.ds(pl.multiple_of(step * 32, 32), 32)

    def first_half_product(which):
        cols = slice(which * AHEAD, (which + 1) * AHEAD)
        weight = (ahead, behind)[which]
        base = 18 * which
        to_sibling = remote(sent.at[0, :, cols], came.at[0, :, cols], base, sibling)
        to_across = remote(sent.at[1, :, cols], came.at[1, :, cols], base + 1, across)
        to_sibling_last = remote(sent.at[2, :, cols], came.at[2, :, cols], base + 2, sibling)

        def chunk_dot(i):
            if which == 0:
                chunks[i].wait()

            def cols_dot(step):
                lanes = pl.ds(pl.multiple_of(step * 256, 256), 256)
                target = pl.ds(pl.multiple_of(which * AHEAD + step * 256, 256), 256)
                part[:, target] = jnp.dot(
                    pooled[chunk_rows(order[i]), :],
                    weight[:, lanes],
                    preferred_element_type=jnp.float32,
                )

            in_blocks(AHEAD // 256, cols_dot)

        def hand_on(slot, came_slot=None):
            def store(step):
                block = block32(step)
                value = part[block, cols]
                if came_slot is not None:
                    value = value + came[came_slot, block, cols].astype(jnp.float32)
                sent[slot, block, cols] = value.astype(jnp.bfloat16)

            in_blocks(rows // 32, store)

        def step0():
            chunk_dot(0)
            hand_on(0)
            to_sibling.start()

        def step1():
            chunk_dot(1)
            to_sibling.wait_recv()
            hand_on(1, 0)
            to_across.start()

        def step2():
            chunk_dot(2)
            hand_on(2)
            to_sibling_last.start()

        def step3():
            chunk_dot(3)
            to_sibling_last.wait_recv()
            to_across.wait_recv()

            def activate(step):
                block = block32(step)
                value = (
                    part[block, cols]
                    + came[1, block, cols].astype(jnp.float32)
                    + came[2, block, cols].astype(jnp.float32)
                    + bias_ref[0:1, cols]
                )
                first_pre[block, cols] = value
                first_act[block, cols] = gelu_parts(value)[0].astype(jnp.bfloat16)

            in_blocks(rows // 32, activate)

        return (step0, step1, step2, step3), (to_sibling, to_across, to_sibling_last)

    steps, sums = first_half_product(0)
    each_copy(early, lambda copy: copy.wait())
    steps[0]()
    steps[1]()
    serve(1)
    second_across.wait_recv()
    second_forward.start()
    steps[2]()
    serve(2)
    steps[3]()
    serve(3)
    each_copy(late, lambda copy: copy.wait())
    if by_groups(n_dp):
        for place in range(4):

            @pl.when(z != place)
            def _(place=place):
                each_copy(
                    shard_copies(2 * place + 1 - y, y_send, y_recv, place, partner),
                    lambda copy: copy.wait_recv(),
                )
    ordered_copies = [
        pltpu.make_async_copy(
            source, ordered_hbm.at[:, pl.ds(which * AHEAD, AHEAD)], out_sem.at[which]
        )
        for which, source in enumerate((ahead, behind))
    ]
    for copy in ordered_copies:
        copy.start()
    steps, more_sums = first_half_product(1)
    for step in steps:
        step()
    my_rows = chunk_rows(me)
    across_rows = chunk_rows(across)
    second_sibling.wait_recv()
    second_forward.wait_recv()

    def second_dot(step):
        cols = pl.ds(pl.multiple_of(step * 256, 256), 256)
        second_pre[:, cols] = (
            jnp.dot(first_act[...], second_ref[:, cols], preferred_element_type=jnp.float32)
            + bias_ref[1:2, cols]
        )

    in_blocks(H // 256, second_dot)

    def activate_second(step):
        block = block32(step)
        second_act[block, :] = gelu_parts(second_pre[block, :])[0].astype(jnp.bfloat16)

    in_blocks(rows // 32, activate_second)
    head_out = (
        jnp.dot(second_act[...], predict_ref[...], preferred_element_type=jnp.float32)
        + bias_ref[2:3, :HALF]
    )
    lane = lax.broadcasted_iota(jnp.int32, (rows, HALF), 1)
    is_logit = lane < CLASSES
    is_delta = (lane >= CLASSES) & (lane < CLASSES + 4)
    label = aux_ref[:, 0:1]
    count_lane = slice(CLASSES + 4, CLASSES + 5)
    valid_total = aux_ref[0:1, count_lane]
    for index, copy in enumerate(counts):
        copy.wait_recv()
        valid_total = valid_total + valid_came[index, 0:1, count_lane]
    share = aux_ref[:, 1:2] / jnp.maximum(valid_total, 1.0)
    foreground = (label > 0.5).astype(jnp.float32)
    onehot = (lane.astype(jnp.float32) == label).astype(jnp.float32)
    top = jnp.max(jnp.where(is_logit, head_out, -jnp.inf), axis=1, keepdims=True)
    exped = jnp.where(is_logit, jnp.exp(jnp.minimum(head_out - top, 0.0)), 0.0)
    exp_sum = jnp.sum(exped, axis=1, keepdims=True)
    chosen = jnp.sum(onehot * head_out, axis=1, keepdims=True)
    error = jnp.where(is_delta, head_out - aux_ref[...], 0.0)
    absolute = jnp.abs(error)
    huber = jnp.where(absolute < 1.0, 0.5 * error * error, absolute - 0.5)
    huber_sum = jnp.sum(jnp.where(is_delta, huber, 0.0), axis=1, keepdims=True)
    loss_rows = share * (jnp.log(exp_sum) + top - chosen + foreground * huber_sum)
    delta_slope = foreground * jnp.minimum(jnp.maximum(error, -1.0), 1.0)
    head_grad = (share * (exped / exp_sum - jnp.where(is_logit, onehot, 0.0) + delta_slope)).astype(
        jnp.bfloat16
    )
    wide = head_grad.astype(jnp.float32)
    lane1 = lax.broadcasted_iota(jnp.int32, (1, HALF), 1)
    head_bias = jnp.sum(wide, axis=0, keepdims=True) + jnp.where(
        lane1 == CLASSES + 4, jnp.sum(loss_rows, axis=0, keepdims=True), 0.0
    )

    def second_back(step):
        cols = pl.ds(pl.multiple_of(step * 256, 256), 256)
        back = contract_cols(head_grad, predict_ref[cols, :])
        second_grad[:, cols] = (back * gelu_parts(second_pre[:, cols])[1]).astype(jnp.bfloat16)

    in_blocks(H // 256, second_back)
    def first_back(step):
        cols = slice(step * quarter, (step + 1) * quarter)
        back = contract_cols(second_grad[...], second_ref[cols, :])
        first_grad[:, cols] = (back * gelu_parts(first_pre[:, cols])[1]).astype(jnp.bfloat16)
        source, target = first_grad.at[:, cols], all_grad.at[my_rows, cols]
        to_other = remote(source, target, 6 + step, across)
        to_twin = remote(source, target, 10 + step, sibling)
        to_other.start()
        to_twin.start()
        relayed = all_grad.at[across_rows, cols]
        return to_other, to_twin, remote(relayed, relayed, 14 + step, sibling)

    grad_copies = [first_back(step) for step in range(4)]
    grad_own = pltpu.make_async_copy(first_grad, all_grad.at[my_rows, :], own_sem.at[2])
    grad_own.start()

    def bias_rows(grads):
        total = jnp.sum(grads[...].astype(jnp.float32), axis=0, keepdims=True)
        return [total[:, i * HALF : (i + 1) * HALF] for i in range(H // HALF)]

    nothing = jnp.zeros((1, HALF), jnp.float32)
    bias_sums = (
        bias_rows(first_grad),
        bias_rows(second_grad),
        [head_bias] + [nothing] * 7,
        [nothing] * 8,
    )
    for step in range(4):
        piece = contract_rows(second_act[:, step * quarter : (step + 1) * quarter], head_grad)
        if by_groups(n_dp):
            for owner in range(n_dp):
                tail_ref[step, owner, :32, :] = piece[owner * 32 : owner * 32 + 32, :]
                tail_ref[step, owner, 32:, :] = jnp.concatenate(
                    [bias_sums[step][owner]] + [nothing] * 7, axis=0
                )
        else:
            tail_ref[step, :quarter, :] = piece
            tail_ref[step, quarter:, :] = jnp.concatenate(bias_sums[step], axis=0)

    for to_other, _, relay in grad_copies:
        to_other.wait_recv()
        relay.start()

    def second_block(step):
        cols = pl.ds(pl.multiple_of(step * 256, 256), 256)
        second_out[:, cols] = contract_rows(first_act[...], second_grad[:, cols]).astype(
            jnp.bfloat16
        )

    in_blocks(H // 256, second_block)
    grad_own.wait()
    for _, to_twin, relay in grad_copies:
        to_twin.wait_recv()
        relay.wait_recv()
    for copy in ordered_copies:
        copy.wait()
    if by_groups(n_dp):

        def sent_off(copy):
            copy.wait_send()

        own_shard(sent_off)
        for distance in (1, 2, 3):
            relay_shards(distance, lambda copy: None, sent_off)
    for copy in (
        *sums,
        *more_sums,
        second_sibling,
        second_across,
        second_forward,
        *(copy for three in grad_copies for copy in three),
        *counts,
    ):
        copy.wait_send()


def middle(pooled, ahead, behind, swapped, predict, bias, aux, n_dp):
    count = pooled.shape[0]
    rows = aux.shape[0]
    tail = (4, n_dp, 40, HALF) if by_groups(n_dp) else (4, H // 4 + 8, HALF)
    any_spec = pl.BlockSpec(memory_space=pl.ANY)
    vmem_spec = pl.BlockSpec(memory_space=pltpu.VMEM)
    return pl.pallas_call(
        functools.partial(middle_kernel, n_dp),
        out_shape=(
            jax.ShapeDtypeStruct((count, H), jnp.bfloat16),
            jax.ShapeDtypeStruct((H, H), jnp.bfloat16),
            jax.ShapeDtypeStruct(tail, jnp.float32),
            jax.ShapeDtypeStruct((KQ, H), jnp.bfloat16),
        ),
        in_specs=[any_spec] * 4 + [vmem_spec] * 3,
        out_specs=(any_spec, vmem_spec, vmem_spec, any_spec),
        scratch_shapes=[
            pltpu.VMEM((count, KQ), jnp.bfloat16),
            pltpu.VMEM((KQ, AHEAD), jnp.bfloat16),
            pltpu.VMEM((KQ, AHEAD), jnp.bfloat16),
            pltpu.VMEM((H, H), jnp.bfloat16),
            pltpu.VMEM((rows, H), jnp.float32),
            pltpu.VMEM((3, rows, H), jnp.bfloat16),
            pltpu.VMEM((3, rows, H), jnp.bfloat16),
            pltpu.VMEM((rows, H), jnp.float32),
            pltpu.VMEM((rows, H), jnp.float32),
            pltpu.VMEM((rows, H), jnp.bfloat16),
            pltpu.VMEM((rows, H), jnp.bfloat16),
            pltpu.VMEM((rows, H), jnp.bfloat16),
            pltpu.VMEM((rows, H), jnp.bfloat16),
            pltpu.VMEM((7, 8, HALF), jnp.float32),
            pltpu.SemaphoreType.DMA((4,)),
            pltpu.SemaphoreType.DMA((SLOTS,)),
            pltpu.SemaphoreType.DMA((3,)),
            pltpu.SemaphoreType.DMA((4 * n_dp if by_groups(n_dp) else 4,)),
            pltpu.SemaphoreType.DMA((8,)),
            pltpu.SemaphoreType.DMA((9,)),
            pltpu.SemaphoreType.DMA((9,)),
            pltpu.SemaphoreType.DMA((9,)),
            pltpu.SemaphoreType.DMA((9,)),
            pltpu.SemaphoreType.DMA((12,)),
            pltpu.SemaphoreType.DMA((12,)),
            pltpu.SemaphoreType.DMA((7,)),
            pltpu.SemaphoreType.DMA((7,)),
            pltpu.SemaphoreType.DMA((21,)),
            pltpu.SemaphoreType.DMA((21,)),
        ],
        compiler_params=pltpu.CompilerParams(
            vmem_limit_bytes=VMEM_LIMIT, collective_id=0, has_side_effects=True
        ),
        cost_estimate=pl.CostEstimate(
            flops=9_000_000_000, bytes_accessed=25_000_000, transcendentals=1_500_000
        ),
        name="middle",
    )(pooled, ahead, behind, swapped, predict, bias, aux)


def weight_grad_kernel(n_dp, meta, pooled_ref, grad_ref, here_hbm, there_hbm, later_hbm, stage, sems):
    half, parity, y = meta[0], meta[1], meta[2]
    step = pl.program_id(0)
    last = pl.num_programs(0) - 1

    def copies(which):
        buffer = which % 2
        for one in range(256 // GROUP):
            slot = 2 * which + one // 4
            owner, local = group_place(half, parity, slot, one % 4, n_dp)
            row = jnp.right_shift(owner, 1)
            inside = slot < SLOTS - 1 - parity
            here = jnp.bitwise_and(owner, 1) == y
            there = jnp.logical_not(here)
            for condition, target, place in (
                (here, here_hbm, row * OWNED + local),
                (there & (local < SWAPPED), there_hbm, row * SWAPPED + local),
                (there & (local >= SWAPPED), later_hbm, row * LATER + local - SWAPPED),
            ):

                @pl.when(inside & condition)
                def _(target=target, one=one, place=place):
                    rows = pl.ds(pl.multiple_of(place * GROUP, GROUP), GROUP)
                    pltpu.make_async_copy(
                        stage.at[buffer, pl.ds(one * GROUP, GROUP), :],
                        target.at[rows, :],
                        sems.at[buffer, one],
                    ).start()

    def waits(which):
        buffer = which % 2
        for one in range(256 // GROUP):

            @pl.when(2 * which + one // 4 < SLOTS - 1 - parity)
            def _(one=one):
                rows = pl.ds(one * GROUP, GROUP)
                pltpu.make_async_copy(
                    stage.at[buffer, rows, :], here_hbm.at[rows, :], sems.at[buffer, one]
                ).wait()

    @pl.when(step >= 2)
    def _():
        waits(step - 2)

    stage[step % 2] = contract_rows(pooled_ref[...], grad_ref[...]).astype(jnp.bfloat16)
    copies(step)

    @pl.when(step == last)
    def _():
        waits(step - 1)
        waits(step)


def weight_grad(pooled, all_grad, meta, n_dp):
    count = pooled.shape[0]
    shapes = tuple(
        jax.ShapeDtypeStruct((n_dp // 2 * groups * GROUP, H), jnp.bfloat16)
        for groups in (OWNED, SWAPPED, LATER)
    )
    any_spec = pl.BlockSpec(memory_space=pl.ANY)
    return pl.pallas_call(
        functools.partial(weight_grad_kernel, n_dp),
        grid=(SLOTS // 2,),
        out_shape=shapes,
        in_specs=[
            pl.BlockSpec(memory_space=pltpu.SMEM),
            pl.BlockSpec((count, 256), lambda i: (0, i)),
            pl.BlockSpec((count, H), lambda i: (0, 0)),
        ],
        out_specs=(any_spec, any_spec, any_spec),
        scratch_shapes=[
            pltpu.VMEM((2, 256, H), jnp.bfloat16),
            pltpu.SemaphoreType.DMA((2, 256 // GROUP)),
        ],
        compiler_params=pltpu.CompilerParams(vmem_limit_bytes=VMEM_LIMIT),
        cost_estimate=pl.CostEstimate(
            flops=7_000_000_000, bytes_accessed=16_000_000, transcendentals=0
        ),
        name="weight_grad",
    )(meta, pooled, all_grad)


def reduce_kernel(
    n_dp,
    here_hbm,
    swapped_hbm,
    later_hbm,
    tail_ref,
    second_ref,
    cells_hbm,
    home_ref,
    second_out,
    tails_ref,
    kept_hbm,
    far_hbm,
    cells_kept,
    cells_near,
    cells_own,
    cells_sum,
    mine,
    y_came,
    up_came,
    down_came,
    final,
    tail_near,
    tail_mine,
    tail_came,
    second_came,
    tail_send,
    tail_recv,
    second_send,
    second_recv,
    cells_load,
    cells_send,
    cells_recv,
    shard_load,
    y_send,
    y_recv,
    up_send,
    up_recv,
    down_send,
    down_recv,
    home_send,
    home_recv,
):
    dp = lax.axis_index("dp")
    me = lax.axis_index("blk")
    half, parity = me // 2, me % 2
    z, y = dp // 2, dp % 2
    home_rows = OWNED * GROUP
    quarter = H // 4
    sibling, across = me // 2 * 2 + 1 - me % 2, (me + 2) % 4
    others = ((me + 1) % 4, (me + 2) % 4, (me + 3) % 4)
    has_below, has_above = z > 0, z < 3

    barrier = pltpu.get_barrier_semaphore()

    def greet(**where):
        pl.semaphore_signal(barrier, inc=1, device_id=where, device_id_type=MESH)

    peers = tuple((dp + step) % n_dp for step in range(1, n_dp))
    for peer in peers:
        greet(dp=peer)
    for other in others:
        greet(blk=other)

    def order(k):
        near, far = ((3, 3), (2, 0), (1, 2), (0, 1))[k]
        low_side = jnp.where(z % 3 == 0, near, far)
        return jnp.where(z < 2, low_side, 3 - low_side)

    def shard_loads(k):
        target = order(k)
        rows = pl.ds(pl.multiple_of(target * home_rows, GROUP), home_rows)
        some = SWAPPED * GROUP
        swapped = pl.ds(pl.multiple_of(target * some, GROUP), some)
        return [
            pltpu.make_async_copy(here_hbm.at[rows, :], mine.at[target], shard_load.at[2 * k]),
            pltpu.make_async_copy(
                swapped_hbm.at[swapped, :],
                y_came.at[target, pl.ds(0, some)],
                shard_load.at[2 * k + 1],
            ),
        ]

    for k in range(4):
        for copy in shard_loads(k):
            copy.start()
    pl.semaphore_wait(barrier, n_dp + 2)

    def remote(source, target, send, recv, **where):
        return pltpu.make_async_remote_copy(
            src_ref=source,
            dst_ref=target,
            send_sem=send,
            recv_sem=recv,
            device_id=where,
            device_id_type=MESH,
        )

    piece = tail_ref.shape[2]
    nears, seconds = [], []
    for index, other in enumerate(others):
        nears.append(
            remote(
                tail_ref.at[other],
                tail_near.at[index],
                tail_send.at[index],
                tail_recv.at[index],
                blk=other,
            )
        )
        seconds.append(
            remote(
                second_ref.at[:, pl.ds(pl.multiple_of(other * quarter, quarter), quarter)],
                second_came.at[index],
                second_send.at[index],
                second_recv.at[index],
                blk=other,
            )
        )

    quarter_cells = cells_sum.shape[0]

    def cell_rows(which):
        return cells_hbm.at[pl.ds(pl.multiple_of(which * quarter_cells, 16), quarter_cells), :]

    loads, gives = [], []
    for index, chip in enumerate((1 - half, half)):
        loads.append(
            pltpu.make_async_copy(
                cell_rows(2 * chip + parity), cells_own.at[index], cells_load.at[index]
            )
        )
        gives.append(
            remote(
                cell_rows(2 * chip + 1 - parity),
                cells_near.at[index],
                cells_send.at[index],
                cells_recv.at[index],
                blk=sibling,
            )
        )
    kept_out = pltpu.make_async_copy(cells_kept, kept_hbm, cells_load.at[2])
    crossing = remote(cells_sum, far_hbm, cells_send.at[2], cells_recv.at[2], blk=across)
    parts = (pl.ds(0, SWAPPED * GROUP), pl.ds(SWAPPED * GROUP, LATER * GROUP))

    def y_copy(k):
        target = order(k)
        rows = pl.ds(pl.multiple_of(target * LATER * GROUP, GROUP), LATER * GROUP)
        return remote(
            later_hbm.at[rows, :],
            y_came.at[target, parts[1]],
            y_send.at[k],
            y_recv.at[k],
            dp=2 * z + 1 - y,
        )

    for k in range(4):
        y_copy(k).start()
    for copy in (*nears, *seconds, *gives, *loads):
        copy.start()

    def cell_blocks(body):
        def step(index, carry):
            body(pl.ds(pl.multiple_of(index * 160, 160), 160))
            return carry

        lax.fori_loop(0, quarter_cells // 160, step, 0)

    def give_across():
        loads[0].wait()
        gives[0].wait_recv()

        def add(rows):
            cells_sum[rows, :] = (
                cells_own[0, rows, :].astype(jnp.float32)
                + cells_near[0, rows, :].astype(jnp.float32)
            ).astype(jnp.bfloat16)

        cell_blocks(add)
        crossing.start()

    def keep_here():
        loads[1].wait()
        gives[1].wait_recv()

        def add(rows):
            cells_kept[rows, :] = cells_own[1, rows, :].astype(jnp.float32) + cells_near[
                1, rows, :
            ].astype(jnp.float32)

        cell_blocks(add)
        kept_out.start()

    def add_up(target, sources, part):
        first, groups = ((0, SWAPPED), (SWAPPED, LATER))[part]

        def step(index, carry):
            rows = pl.ds(pl.multiple_of((first + index) * GROUP, GROUP), GROUP)
            total = mine[target, rows, :].astype(jnp.float32)
            for ref in sources:
                total = total + ref[target, rows, :].astype(jnp.float32)
            mine[target, rows, :] = total.astype(jnp.bfloat16)
            return carry

        lax.fori_loop(0, groups, step, 0)

    def z_copy(target, part, came, send, recv, neighbour):
        sem = 2 * target + part
        return remote(
            mine.at[target, parts[part]],
            came.at[target, parts[part]],
            send.at[sem],
            recv.at[sem],
            dp=neighbour,
        )

    def up_copy(target, part):
        return z_copy(target, part, up_came, up_send, up_recv, dp + 2)

    def down_copy(target, part):
        return z_copy(target, part, down_came, down_send, down_recv, dp - 2)

    def arrive(k, part):
        if part == 0:
            for copy in shard_loads(k):
                copy.wait()
        else:
            y_copy(k).wait_recv()

    def chain(k, part):
        target = order(k)
        arrive(k, part)

        @pl.when(target > z)
        def _():
            @pl.when(has_below)
            def _():
                up_copy(target, part).wait_recv()
                add_up(target, (y_came, up_came), part)

            @pl.when(jnp.logical_not(has_below))
            def _():
                add_up(target, (y_came,), part)

            up_copy(target, part).start()

        @pl.when(target < z)
        def _():
            @pl.when(has_above)
            def _():
                down_copy(target, part).wait_recv()
                add_up(target, (y_came, down_came), part)

            @pl.when(jnp.logical_not(has_above))
            def _():
                add_up(target, (y_came,), part)

            down_copy(target, part).start()

    def last(part):
        arrive(3, part)
        add_up(z, (y_came,), part)

        @pl.when(has_below)
        def _():
            up_copy(z, part).wait_recv()
            add_up(z, (up_came,), part)

        @pl.when(has_above)
        def _():
            down_copy(z, part).wait_recv()
            add_up(z, (down_came,), part)

    def home_copies(part):
        copies = []
        for index, other in enumerate(others):
            cols = pl.ds(pl.multiple_of(other * quarter, quarter), quarter)
            copies.append(
                remote(
                    mine.at[z, parts[part], cols],
                    final.at[me, parts[part]],
                    home_send.at[3 * part + index],
                    home_recv.at[3 * part + index],
                    blk=other,
                )
            )
        return copies

    chain(0, 0)
    give_across()
    for copy in nears:
        copy.wait_recv()
    tail_mine[...] = tail_ref[me] + tail_near[0] + tail_near[1] + tail_near[2]
    tails = []
    for index, peer in enumerate(peers):
        sem = 3 + index
        tails.append(
            remote(
                tail_mine.at[peer],
                tail_came.at[index],
                tail_send.at[sem],
                tail_recv.at[sem],
                dp=peer,
            )
        )
    for copy in tails:
        copy.start()
    chain(1, 0)
    for copy in tails:
        copy.wait_recv()
    my_tail = pl.ds(pl.multiple_of((me * n_dp + dp) * piece, 8), piece)
    total = tail_mine[dp]
    for index in range(n_dp - 1):
        total = total + tail_came[index]
    tails_ref[my_tail, :] = total
    spreads = []
    for index, peer in enumerate(peers):
        spot = tails_ref.at[my_tail, :]
        sem = n_dp + 2 + index
        spreads.append(remote(spot, spot, tail_send.at[sem], tail_recv.at[sem], dp=peer))
    for copy in spreads:
        copy.start()
    keep_here()
    chain(2, 0)
    last(0)
    homes = home_copies(0)
    for copy in homes:
        copy.start()
    for k in range(3):
        chain(k, 1)
    block = tails_ref.at[pl.ds(pl.multiple_of(me * n_dp * piece, 8), n_dp * piece), :]
    shares = []
    for index, other in enumerate(others):
        sem = 2 * n_dp + 1 + index
        shares.append(remote(block, block, tail_send.at[sem], tail_recv.at[sem], blk=other))
    for copy in spreads:
        copy.wait_recv()
    for copy in shares:
        copy.start()
    own_cols = pl.ds(pl.multiple_of(me * quarter, quarter), quarter)
    second = second_ref[:, own_cols].astype(jnp.float32)
    for index, copy in enumerate(seconds):
        copy.wait_recv()
        second = second + second_came[index].astype(jnp.float32)
    second_out[...] = second
    last(1)
    homes_later = home_copies(1)
    for copy in homes_later:
        copy.start()
    home_ref[pl.ds(pl.multiple_of(me * home_rows, GROUP), home_rows), :] = mine[z, :, own_cols]
    for copy in shares:
        copy.wait_recv()
    for index in range(3):
        sender = (me + 3 - index) % 4
        homes[index].wait_recv()
        homes_later[index].wait_recv()
        rows = pl.ds(pl.multiple_of(sender * home_rows, GROUP), home_rows)
        home_ref[rows, :] = final[sender]
    for copy in (
        *homes,
        *homes_later,
        *nears,
        *tails,
        *spreads,
        *shares,
        *seconds,
        *gives,
        crossing,
        *(y_copy(k) for k in range(4)),
    ):
        copy.wait_send()
    kept_out.wait()
    crossing.wait_recv()
    for k in range(3):
        target = order(k)

        @pl.when(target > z)
        def _():
            up_copy(target, 0).wait_send()
            up_copy(target, 1).wait_send()

        @pl.when(target < z)
        def _():
            down_copy(target, 0).wait_send()
            down_copy(target, 1).wait_send()


def reduce_home(here, swapped, later, tail, second, cell_grads, n_dp):
    home = OWNED * GROUP
    piece = tail.shape[2]
    cells = cell_grads.shape[0] // 4
    vmem_spec = pl.BlockSpec(memory_space=pltpu.VMEM)
    any_spec = pl.BlockSpec(memory_space=pl.ANY)
    shards = pltpu.VMEM((4, home, H), jnp.bfloat16)

    def sems(number):
        return pltpu.SemaphoreType.DMA((number,))

    return pl.pallas_call(
        functools.partial(reduce_kernel, n_dp),
        out_shape=(
            jax.ShapeDtypeStruct((4 * home, H // 4), jnp.bfloat16),
            jax.ShapeDtypeStruct((H // n_dp, H // 4), jnp.float32),
            jax.ShapeDtypeStruct((4 * n_dp * piece, HALF), jnp.float32),
            jax.ShapeDtypeStruct((cells, HALF), jnp.float32),
            jax.ShapeDtypeStruct((cells, HALF), jnp.bfloat16),
        ),
        in_specs=[any_spec, any_spec, any_spec, vmem_spec, vmem_spec, any_spec],
        out_specs=(vmem_spec,) * 3 + (any_spec,) * 2,
        scratch_shapes=[
            pltpu.VMEM((cells, HALF), jnp.float32),
            pltpu.VMEM((2, cells, HALF), jnp.bfloat16),
            pltpu.VMEM((2, cells, HALF), jnp.bfloat16),
            pltpu.VMEM((cells, HALF), jnp.bfloat16),
            shards,
            shards,
            shards,
            shards,
            pltpu.VMEM((4, home, H // 4), jnp.bfloat16),
            pltpu.VMEM((3, n_dp, piece, HALF), jnp.float32),
            pltpu.VMEM((n_dp, piece, HALF), jnp.float32),
            pltpu.VMEM((n_dp - 1, piece, HALF), jnp.float32),
            pltpu.VMEM((3, H // n_dp, H // 4), jnp.bfloat16),
            sems(2 * n_dp + 4),
            sems(2 * n_dp + 4),
            sems(3),
            sems(3),
            sems(3),
            sems(3),
            sems(3),
            sems(8),
            sems(4),
            sems(4),
            sems(8),
            sems(8),
            sems(8),
            sems(8),
            sems(6),
            sems(6),
        ],
        compiler_params=pltpu.CompilerParams(
            vmem_limit_bytes=VMEM_LIMIT, collective_id=1, has_side_effects=True
        ),
        cost_estimate=pl.CostEstimate(
            flops=60_000_000_000, bytes_accessed=200_000_000, transcendentals=0
        ),
        name="reduce_home",
    )(here, swapped, later, tail, second, cell_grads)


def sum_apart(pooled, all_grad, n_blk):
    first_wgrad = contract_rows(pooled, all_grad).astype(jnp.bfloat16)
    split = first_wgrad.reshape(KQ, n_blk, -1).transpose(1, 0, 2)
    mine = lax.all_to_all(split, "blk", split_axis=0, concat_axis=0, tiled=True)
    cols = mine.shape[2]
    mine = mine.reshape(2, 2, SLOTS, HALF, cols).transpose(2, 1, 0, 3, 4)
    mine = mine.reshape(2 * SLOTS, C, cols)[:BINS].reshape(K1, cols)
    first_sum = lax.psum_scatter(mine, "dp", scatter_dimension=0, tiled=True).astype(jnp.float32)
    return first_sum


def finish_kernel(
    table,
    home_ref,
    weight_ref,
    mean_ref,
    square_ref,
    kept_ref,
    far_ref,
    tails_ref,
    second_grad_ref,
    second_refs_0,
    second_refs_1,
    second_refs_2,
    out_refs_0,
    out_refs_1,
    out_refs_2,
    new_ref,
    new_mean_ref,
    new_square_ref,
    features_ref,
    second_new_0,
    second_new_1,
    second_new_2,
    out_new_0,
    out_new_1,
    out_new_2,
):
    @pl.when(pl.program_id(0) == 0)
    def _():
        seconds = adamw(
            second_refs_0[...],
            second_grad_ref[...],
            second_refs_1[...],
            second_refs_2[...],
            rate_second,
        )
        second_new_0[...], second_new_1[...], second_new_2[...] = seconds

        def owner_step(owner, carry):
            source = pl.ds(pl.multiple_of(owner * 40, 8), 32)
            rows = pl.ds(pl.multiple_of(owner * 32, 32), 32)
            outs = adamw(
                out_refs_0[rows, :],
                tails_ref[source, :][:, : CLASSES + 4],
                out_refs_1[rows, :],
                out_refs_2[rows, :],
                rate_out,
            )
            out_new_0[rows, :], out_new_1[rows, :], out_new_2[rows, :] = outs
            return carry

        lax.fori_loop(0, H // 32, owner_step, 0)

    groups = weight_ref.shape[0] // GROUP
    span = K1 // GROUP // lax.axis_size("dp")
    base = lax.axis_index("dp") * span + pl.program_id(0) * groups
    my_half = lax.axis_index("blk") // 2
    for index in range(groups):
        source = pl.ds(pl.multiple_of(table[base + index] * GROUP, GROUP), GROUP)
        rows = slice(index * GROUP, (index + 1) * GROUP)
        updated = adamw(
            weight_ref[rows, :],
            home_ref[source, :].astype(jnp.float32),
            mean_ref[rows, :],
            square_ref[rows, :],
            rate_first,
        )
        new_ref[rows, :], new_mean_ref[rows, :], new_square_ref[rows, :] = updated
    for half in range(2):

        @pl.when(my_half == half)
        def _(half=half):
            features_ref[:, half * HALF : (half + 1) * HALF] = kept_ref[...]
            features_ref[:, (1 - half) * HALF : (2 - half) * HALF] = far_ref[...].astype(
                jnp.float32
            )


def finish(home, kept, far, tails, second_sum, firsts, seconds, outs, n_dp):
    first_weight, first_mean, first_square = firsts
    cols = first_weight.shape[1]
    steps = 7
    table = jnp.asarray(group_sources(n_dp).reshape(-1))
    block = pl.BlockSpec((first_weight.shape[0] // steps, cols), lambda i: (i, 0))
    shape = jax.ShapeDtypeStruct(first_weight.shape, jnp.float32)
    cells = kept.shape[0]
    some = -(-cells // steps // 16) * 16
    part = pl.BlockSpec((some, HALF), lambda i: (i, 0))

    def whole(values):
        return pl.BlockSpec(values.shape, lambda i: (0, 0))

    others = (tails, second_sum, *seconds, *outs)
    return pl.pallas_call(
        finish_kernel,
        grid=(steps,),
        out_shape=(
            (shape, shape, shape, jax.ShapeDtypeStruct((cells, C), jnp.float32))
            + tuple(jax.ShapeDtypeStruct(one.shape, jnp.float32) for one in (*seconds, *outs))
        ),
        in_specs=[
            pl.BlockSpec(memory_space=pltpu.SMEM),
            pl.BlockSpec(memory_space=pltpu.VMEM),
            block,
            block,
            block,
            part,
            part,
            *(whole(one) for one in others),
        ],
        out_specs=(
            (block, block, block, pl.BlockSpec((some, C), lambda i: (i, 0)))
            + tuple(whole(one) for one in (*seconds, *outs))
        ),
        compiler_params=pltpu.CompilerParams(vmem_limit_bytes=VMEM_LIMIT),
        name="finish",
    )(table, home, first_weight, first_mean, first_square, kept, far, *others)


def on_device(
    features,
    roi_table,
    offsets,
    box_targets,
    first_weight,
    first_mean,
    first_square,
    second_weight,
    second_mean,
    second_square,
    out_weight,
    out_mean,
    out_square,
    biases,
    bias_mean,
    bias_square,
    n_dp,
    n_blk,
):
    place = lax.axis_index("blk")
    half = place // 2
    parity = place % 2
    roi_count = roi_table.shape[1]
    outw = out_weight.shape[1]
    rois = jnp.concatenate((roi_table.astype(jnp.float32), box_targets), axis=0)
    weight, all_rois = gather_quarter(first_weight, second_weight, rois, n_dp)
    valid_here = jnp.sum(all_rois[7])
    if not by_groups(n_dp):
        valid_here = lax.psum(valid_here, "dp")
    predict = jnp.pad(out_weight.astype(jnp.bfloat16), ((0, 0), (0, HALF - outw)))
    bias = jnp.zeros((8, H), jnp.float32)
    bias = bias.at[0].set(biases[:H]).at[1].set(biases[H : 2 * H]).at[2, :outw].set(biases[2 * H :])

    table, targets, starts = sort_rois(all_rois[:8].astype(jnp.int32), all_rois[8:])
    lows = window_lows(offsets)
    row_sevens, col_sevens, rows_at, cols_at = sample_points(table, offsets, parity)
    apart = ((0, 0), (0, 64 - 7))
    points = jnp.concatenate((jnp.pad(row_sevens, apart), jnp.pad(col_sevens, apart)), axis=1)

    def by_group(values):
        grouped = values.reshape(-1, BATCH, SLOTS).transpose(0, 2, 1).reshape(-1, SLOTS * BATCH)
        return jnp.pad(grouped, ((0, 0), (0, LANES - SLOTS * BATCH)), constant_values=FAR)

    my_table = lax.dynamic_slice_in_dim(table, place * roi_count, roi_count, axis=1)
    my_targets = lax.dynamic_slice_in_dim(targets, place * roi_count, roi_count, axis=0)
    aux = jnp.concatenate(
        (
            my_table[6].astype(jnp.float32)[:, None],
            my_table[7].astype(jnp.float32)[:, None],
            jnp.zeros((roi_count, CLASSES - 2), jnp.float32),
            my_targets,
            jnp.broadcast_to(valid_here, (roi_count, 1)),
            jnp.zeros((roi_count, HALF - CLASSES - 5), jnp.float32),
        ),
        axis=1,
    )
    meta = jnp.stack((half, parity, lax.axis_index("dp") % 2))
    pooled = pool(features, meta, starts, lows, points)
    all_grad, second_wgrad, tail, ordered = middle(
        pooled, *weight, predict, bias, aux, n_dp
    )
    second_part = lax.psum_scatter(second_wgrad, "dp", scatter_dimension=0, tiled=True)
    if by_groups(n_dp):
        here, there, later = weight_grad(pooled, all_grad, meta, n_dp)
        swapped = lax.ppermute(there, "dp", [(spot, spot ^ 1) for spot in range(n_dp)])
    cell_grads = spread(
        all_grad, ordered, starts, lows, by_group(rows_at), by_group(cols_at), features.shape[0]
    )
    if by_groups(n_dp):
        home, second_sum, tails, kept, far = reduce_home(
            here, swapped, later, tail, second_part, cell_grads, n_dp
        )
        first_new, first_mean_new, first_square_new, feature_grads, *rest = finish(
            home,
            kept,
            far,
            tails,
            second_sum,
            (first_weight, first_mean, first_square),
            (second_weight, second_mean, second_square),
            (out_weight, out_mean, out_square),
            n_dp,
        )
        second_new, second_mean_new, second_square_new = rest[:3]
        out_new, out_mean_new, out_square_new = rest[3:]
        tails = tails.reshape(n_blk, n_dp, -1, HALF)
        bias_flat = tails[:, :, -8].reshape(-1)
    else:
        first_new, first_mean_new, first_square_new = adamw(
            first_weight, sum_apart(pooled, all_grad, n_blk), first_mean, first_square, rate_first
        )
        parts = lax.all_to_all(
            cell_grads.reshape(n_blk, -1, HALF), "blk", split_axis=0, concat_axis=0, tiled=True
        ).astype(jnp.float32)
        feature_grads = jnp.concatenate((parts[0] + parts[1], parts[2] + parts[3]), axis=1)
        second_sum = lax.psum_scatter(second_part, "blk", scatter_dimension=1, tiled=True)
        second_sum = second_sum.astype(jnp.float32)
        tails = lax.psum(tail, ("dp", "blk"))
        out_sum = tails[:, : H // n_blk].reshape(H, HALF)[:, :outw]
        bias_flat = tails[:, H // n_blk :].reshape(-1)
        second_new, second_mean_new, second_square_new = adamw(
            second_weight, second_sum, second_mean, second_square, rate_second
        )
        out_new, out_mean_new, out_square_new = adamw(
            out_weight, out_sum, out_mean, out_square, rate_out
        )
    bias_sum = bias_flat[: biases.shape[0]]
    total_loss = bias_flat[biases.shape[0]]

    bias_new, bias_mean_new, bias_square_new = adamw(
        biases, bias_sum, bias_mean, bias_square, rate_bias
    )
    return (
        feature_grads,
        total_loss,
        first_new,
        first_mean_new,
        first_square_new,
        second_new,
        second_mean_new,
        second_square_new,
        out_new,
        out_mean_new,
        out_square_new,
        bias_new,
        bias_mean_new,
        bias_square_new,
    )


def solution(mesh):
    in_specs = (
        P("dp", None),
        P(None, ("dp", "blk")),
        P(None, "dp"),
        P(None, ("dp", "blk")),
        P("dp", "blk"),
        P("dp", "blk"),
        P("dp", "blk"),
        P("dp", "blk"),
        P("dp", "blk"),
        P("dp", "blk"),
        P(),
        P(),
        P(),
        P(),
        P(),
        P(),
    )
    out_specs = (
        P(("dp", "blk"), None),
        P(),
        P("dp", "blk"),
        P("dp", "blk"),
        P("dp", "blk"),
        P("dp", "blk"),
        P("dp", "blk"),
        P("dp", "blk"),
        P(),
        P(),
        P(),
        P(),
        P(),
        P(),
    )
    return jax.shard_map(
        functools.partial(on_device, n_dp=mesh.shape["dp"], n_blk=mesh.shape["blk"]),
        mesh=mesh,
        in_specs=in_specs,
        out_specs=out_specs,
        check_vma=False,
    )
```

```python
import functools

import jax
import jax.numpy as jnp
import numpy as np
from jax import lax
from jax.experimental import pallas as pl
from jax.experimental.pallas import tpu as pltpu
from jax.sharding import PartitionSpec as P

C = 256
H = 1024
CLASSES = 81
CANVAS = 512
IMAGES = 4
LEVELS = 4
STEP = 10
K1 = 12544
BINS = 49

HALF = 128
SLOTS = 26
KQ = SLOTS * HALF
FAR = -1.0e6
BATCH = 16
LANES = 512
SIDES = (128, 64, 32, 16)
BASES = (0, 16384, 20480, 21504)
WIN_ROWS = (52, 28, 16, 16)
WIN_COLS = (64, 32, 16, 16)
BACK_COLS = (56, 32, 16, 16)
VMEM_LIMIT = 60 * 1024 * 1024
GROUP = 32
OWNED = 13
SHARD = OWNED + 1
AHEAD = H // 2
SWAPPED = 9
LATER = OWNED - SWAPPED
AHEAD_ROWS = (OWNED + 2) * GROUP
MESH = pl.DeviceIdType.MESH

third = 1.0 / 3.0
rate_first = 0.018
rate_second = 0.06
rate_out = 0.18
rate_bias = 0.2


def contract_rows(left_side, right_side):
    return lax.dot_general(
        left_side, right_side, (((0,), (0,)), ((), ())), preferred_element_type=jnp.float32
    )


def contract_cols(left_side, right_side):
    return lax.dot_general(
        left_side, right_side, (((1,), (1,)), ((), ())), preferred_element_type=jnp.float32
    )


def sort_rois(roi_table, box_targets):
    count = roi_table.shape[1]
    key = roi_table[5] * IMAGES + roi_table[4]
    place = jnp.arange(count, dtype=jnp.int32)
    before = (key[None, :] < key[:, None]) | (
        (key[None, :] == key[:, None]) & (place[None, :] < place[:, None])
    )
    rank = jnp.sum(before.astype(jnp.int32), axis=1)
    segments = jnp.arange(LEVELS * IMAGES + 1, dtype=jnp.int32)
    starts = jnp.sum((key[None, :] < segments[:, None]).astype(jnp.int32), axis=1)
    rows = jnp.concatenate((roi_table.astype(jnp.float32), box_targets), axis=0)
    pick = (rank[None, :] == place[:, None]).astype(jnp.float32)
    ordered = lax.dot_general(
        pick, rows, (((1,), (1,)), ((), ())), precision=lax.Precision.HIGHEST
    )
    return ordered[:, :8].astype(jnp.int32).T, ordered[:, 8:], starts


def sample_points(table, offsets, parity):
    level_of = table[5]
    image_of = table[4]
    choose = (image_of[:, None] == jnp.arange(IMAGES, dtype=jnp.int32)[None, :]).astype(jnp.int32)
    shift_y = jnp.sum(choose * offsets[0][None, :], axis=1)
    shift_x = jnp.sum(choose * offsets[1][None, :], axis=1)
    grid_side = jnp.right_shift(jnp.full_like(level_of, CANVAS // 4), level_of)
    stride_px = (4 * jnp.left_shift(jnp.ones_like(level_of), level_of)).astype(jnp.float32)
    bins = 2 * jnp.arange(SLOTS, dtype=jnp.int32) + parity
    inside = bins < BINS
    every = jnp.arange(7, dtype=jnp.int32)

    def axis_points(low_edge, high_edge, shift_by, which, keep):
        centres = (which.astype(jnp.float32) + 0.5) / 7.0
        start_px = (low_edge + shift_by).astype(jnp.float32)
        extent = (high_edge - low_edge).astype(jnp.float32)
        points = start_px[:, None] + centres[None, :] * extent[:, None]
        limit_max = (grid_side - 1).astype(jnp.float32)[:, None]
        scaled = jnp.clip(points / stride_px[:, None] - 0.5, 0.0, limit_max)
        return jnp.where(keep[None, :], scaled, FAR)

    rows = (table[1], table[3], shift_y)
    cols = (table[0], table[2], shift_x)
    return (
        axis_points(*rows, every, every >= 0),
        axis_points(*cols, every, every >= 0),
        axis_points(*rows, bins // 7, inside),
        axis_points(*cols, bins % 7, inside),
    )


def window_lows(offsets):
    lows = []
    for level in range(LEVELS - 1):
        half_stride = 2 << level
        lows.append(jnp.maximum(jnp.right_shift(offsets - half_stride, 2 + level), 0))
    lows.append(jnp.zeros_like(offsets))
    return jnp.stack(lows, axis=1).reshape(-1)


def segment_loop(starts, lows, visit):
    for level in range(LEVELS):

        def image_step(image, carry, level=level):
            segment = level * IMAGES + image
            begin = starts[segment]
            end = starts[segment + 1]
            row_low = lows[level * IMAGES + image]
            col_low = lows[(LEVELS + level) * IMAGES + image]

            @pl.when(end > begin)
            def _():
                visit(level, begin, end, row_low, col_low)

            return carry

        lax.fori_loop(0, IMAGES, image_step, 0)


def hat(distance):
    return jnp.maximum(1.0 - jnp.abs(distance), 0.0)


def pool_kernel(starts, lows, meta, feat_hbm, uv_ref, out_ref, raw, cells, win, acc, sem):
    total = raw.shape[0]
    lane0 = pl.multiple_of(meta[0] * HALF, HALF)
    fetch = pltpu.make_async_copy(feat_hbm.at[:, pl.ds(lane0, HALF)], raw, sem)
    fetch.start()
    count = acc.shape[0]

    def clear(step, carry):
        acc[pl.ds(pl.multiple_of(step * 8, 8), 8), :] = jnp.zeros((8, KQ), jnp.float32)
        return carry

    lax.fori_loop(0, count // 8, clear, 0)
    fetch.wait()

    def widen(step, carry):
        rows = pl.ds(pl.multiple_of(step * 128, 128), 128)
        cells[rows, :] = raw[rows, :].astype(jnp.float32)
        return carry

    lax.fori_loop(0, total // 128, widen, 0)

    def visit(level, begin, end, row_low, col_low):
        side, base = SIDES[level], BASES[level]
        height, width = WIN_ROWS[level], WIN_COLS[level]
        shift = width.bit_length() - 1
        per_tile = HALF // width
        tiles = height // per_tile
        depth = tiles * HALF

        def take(row, carry):
            source = pl.ds(base + (row_low + row) * side + col_low, width)
            target = pl.ds(pl.multiple_of(row * width, width), width)
            win[target, :] = cells[source, :].astype(jnp.bfloat16)
            return carry

        lax.fori_loop(0, height, take, 0)
        row_shift = row_low.astype(jnp.float32)
        col_shift = col_low.astype(jnp.float32)

        def group(parity, step, carry):
            first = pl.multiple_of(step * BATCH, BATCH)
            lane = lax.broadcasted_iota(jnp.int32, (BATCH, HALF), 1)
            lane_row = jnp.right_shift(lane, shift).astype(jnp.float32) + row_shift
            lane_col = jnp.bitwise_and(lane, width - 1).astype(jnp.float32) + col_shift
            roi = first + lax.broadcasted_iota(jnp.int32, (BATCH, HALF), 0)
            mine = (roi >= begin) & (roi < end)
            points = jnp.where(mine, uv_ref[pl.ds(first, BATCH), :], FAR)
            row_at = [points[:, a : a + 1] - lane_row for a in range(7)]
            col_hats = [hat(points[:, 64 + b : 65 + b] - lane_col) for b in range(7)]
            bins = [2 * slot + parity for slot in range(SLOTS)]
            pooled = None
            for begin_tile in range(0, tiles, 4):
                columns = []
                for tile in range(begin_tile, min(begin_tile + 4, tiles)):
                    row_hats = [hat(at - float(tile * per_tile)) for at in row_at]
                    weights = [
                        (row_hats[one // 7] * col_hats[one % 7]).astype(jnp.bfloat16)
                        if one < BINS
                        else jnp.zeros((BATCH, HALF), jnp.bfloat16)
                        for one in bins
                    ]
                    columns.append(jnp.concatenate(weights, axis=0))
                part = jnp.dot(
                    jnp.concatenate(columns, axis=1),
                    win[begin_tile * HALF : (begin_tile + len(columns)) * HALF, :],
                    preferred_element_type=jnp.float32,
                )
                pooled = part if pooled is None else pooled + part
            for slot in range(SLOTS):
                where = (pl.ds(first, BATCH), slice(slot * HALF, (slot + 1) * HALF))
                acc[where] = acc[where] + pooled[slot * BATCH : (slot + 1) * BATCH, :]
            return carry

        for parity in (0, 1):

            @pl.when(meta[1] == parity)
            def _(parity=parity):
                lax.fori_loop(
                    begin // BATCH, (end + BATCH - 1) // BATCH, functools.partial(group, parity), 0
                )

    segment_loop(starts, lows, visit)

    def narrow(step, carry):
        rows = pl.ds(pl.multiple_of(step * 16, 16), 16)
        out_ref[rows, :] = acc[rows, :].astype(jnp.bfloat16)
        return carry

    lax.fori_loop(0, count // 16, narrow, 0)


def pool(features, meta, starts, lows, points):
    count = points.shape[0]
    cells = features.shape[0]
    return pl.pallas_call(
        pool_kernel,
        out_shape=jax.ShapeDtypeStruct((count, KQ), jnp.bfloat16),
        in_specs=[
            pl.BlockSpec(memory_space=pltpu.SMEM),
            pl.BlockSpec(memory_space=pltpu.SMEM),
            pl.BlockSpec(memory_space=pltpu.SMEM),
            pl.BlockSpec(memory_space=pl.ANY),
            pl.BlockSpec(memory_space=pltpu.VMEM),
        ],
        out_specs=pl.BlockSpec(memory_space=pltpu.VMEM),
        scratch_shapes=[
            pltpu.VMEM((cells, HALF), jnp.bfloat16),
            pltpu.VMEM((cells, HALF), jnp.float32),
            pltpu.VMEM((KQ, HALF), jnp.bfloat16),
            pltpu.VMEM((count, KQ), jnp.float32),
            pltpu.SemaphoreType.DMA,
        ],
        compiler_params=pltpu.CompilerParams(vmem_limit_bytes=VMEM_LIMIT),
        cost_estimate=pl.CostEstimate(
            flops=40_000_000_000, bytes_accessed=13_000_000, transcendentals=0
        ),
        name="pool_bins",
    )(starts, lows, meta, features, points)


def spread_kernel(
    starts,
    lows,
    grad_ref,
    weight_hbm,
    row_ref,
    col_ref,
    out_ref,
    weight_ref,
    pooled,
    cells,
    part,
    row_hat,
    right,
    weight_sem,
):
    total = cells.shape[0]
    fetch = pltpu.make_async_copy(weight_hbm, weight_ref, weight_sem)
    fetch.start()

    def clear(step, carry):
        rows = pl.ds(pl.multiple_of(step * 128, 128), 128)
        cells[rows, :] = jnp.zeros((128, HALF), jnp.float32)
        return carry

    lax.fori_loop(0, total // 128, clear, 0)
    fetch.wait()

    def back_dot(step, carry):
        cols = pl.ds(pl.multiple_of(step * 256, 256), 256)
        pooled[:, cols] = contract_cols(grad_ref[...], weight_ref[cols, :]).astype(jnp.bfloat16)
        return carry

    lax.fori_loop(0, KQ // 256, back_dot, 0)
    right[SLOTS * BATCH :, :] = jnp.zeros((LANES - SLOTS * BATCH, HALF), jnp.bfloat16)

    def visit(level, begin, end, row_low, col_low):
        side, base = SIDES[level], BASES[level]
        height, width = WIN_ROWS[level], BACK_COLS[level]
        chunk = (26, 28, 16, 16)[level]
        row_shift = row_low.astype(jnp.float32)
        col_shift = col_low.astype(jnp.float32)

        def wipe(row, carry):
            rows = pl.ds(pl.multiple_of(row * width, 8), width)
            part[rows, :] = jnp.zeros((width, HALF), jnp.float32)
            return carry

        lax.fori_loop(0, height, wipe, 0)

        def group(step, carry):
            first = pl.multiple_of(step * BATCH, BATCH)
            for slot in range(SLOTS):
                right[slot * BATCH : (slot + 1) * BATCH, :] = pooled[
                    pl.ds(first, BATCH), slot * HALF : (slot + 1) * HALF
                ]
            lane = lax.broadcasted_iota(jnp.int32, (1, LANES), 1)
            roi = first + jnp.bitwise_and(lane, BATCH - 1)
            mine = (roi >= begin) & (roi < end)
            row_at = jnp.where(mine, row_ref[pl.ds(step, 1), :], FAR) - row_shift
            col_at = jnp.where(mine, col_ref[pl.ds(step, 1), :], FAR) - col_shift
            row_hat[...] = hat(
                row_at - lax.broadcasted_iota(jnp.int32, (56, LANES), 0).astype(jnp.float32)
            )
            col_hat = hat(
                col_at - lax.broadcasted_iota(jnp.int32, (width, LANES), 0).astype(jnp.float32)
            )
            for row in range(0, height, chunk):
                left = jnp.concatenate(
                    [col_hat * row_hat[row + one : row + one + 1, :] for one in range(chunk)], axis=0
                ).astype(jnp.bfloat16)
                rows = slice(row * width, (row + chunk) * width)
                part[rows, :] += jnp.dot(left, right[...], preferred_element_type=jnp.float32)
            return carry

        lax.fori_loop(begin // BATCH, (end + BATCH - 1) // BATCH, group, 0)

        def flush(row, carry):
            target = pl.ds(base + (row_low + row) * side + col_low, width)
            source = pl.ds(pl.multiple_of(row * width, 8), width)
            cells[target, :] = cells[target, :] + part[source, :]
            return carry

        lax.fori_loop(0, height, flush, 0)

    segment_loop(starts, lows, visit)

    def narrow(step, carry):
        rows = pl.ds(pl.multiple_of(step * 128, 128), 128)
        out_ref[rows, :] = (cells[rows, :] * third).astype(jnp.bfloat16)
        return carry

    lax.fori_loop(0, total // 128, narrow, 0)


def spread(first_grad, weight, starts, lows, rows_at, cols_at, cells):
    count = first_grad.shape[0]
    return pl.pallas_call(
        spread_kernel,
        out_shape=jax.ShapeDtypeStruct((cells, HALF), jnp.bfloat16),
        in_specs=[
            pl.BlockSpec(memory_space=pltpu.SMEM),
            pl.BlockSpec(memory_space=pltpu.SMEM),
            pl.BlockSpec(memory_space=pltpu.VMEM),
            pl.BlockSpec(memory_space=pl.ANY),
            pl.BlockSpec(memory_space=pltpu.VMEM),
            pl.BlockSpec(memory_space=pltpu.VMEM),
        ],
        out_specs=pl.BlockSpec(memory_space=pltpu.VMEM),
        scratch_shapes=[
            pltpu.VMEM((KQ, H), jnp.bfloat16),
            pltpu.VMEM((count, KQ), jnp.bfloat16),
            pltpu.VMEM((cells, HALF), jnp.float32),
            pltpu.VMEM((WIN_ROWS[0] * BACK_COLS[0], HALF), jnp.float32),
            pltpu.VMEM((56, LANES), jnp.float32),
            pltpu.VMEM((LANES, HALF), jnp.bfloat16),
            pltpu.SemaphoreType.DMA,
        ],
        compiler_params=pltpu.CompilerParams(vmem_limit_bytes=VMEM_LIMIT),
        cost_estimate=pl.CostEstimate(
            flops=40_000_000_000, bytes_accessed=15_000_000, transcendentals=0
        ),
        name="spread_bins",
    )(starts, lows, first_grad, weight, rows_at, cols_at)


def adamw(weight, gradient, moment, square, step_rate):
    new_mean = 0.9 * moment + 0.1 * gradient
    new_square = 0.999 * square + 0.001 * gradient * gradient
    mean_hat = new_mean / (1.0 - 0.9**STEP)
    square_hat = new_square / (1.0 - 0.999**STEP)
    new_weight = weight - step_rate * (mean_hat / (jnp.sqrt(square_hat) + 1e-08) + 0.0001 * weight)
    return (new_weight, new_mean, new_square)


def groups_before(half, parity, index):
    inside = index % 16 - (8 * parity + 4 * half)
    return index // 16 * 4 + jnp.minimum(jnp.maximum(inside, 0), 4)


def group_place(half, parity, slot, part, n_dp):
    span = K1 // GROUP // n_dp

    def earlier(index):
        inside = jnp.bitwise_and(index, 15) - (8 * parity + 4 * half)
        return jnp.right_shift(index, 4) * 4 + jnp.minimum(jnp.maximum(inside, 0), 4)

    group = 8 * (2 * slot + parity) + 4 * half + part
    owner = sum((group >= span * other).astype(jnp.int32) for other in range(1, n_dp))
    return owner, earlier(group) - earlier(owner * span)


def owned_groups(n_dp):
    span = K1 // GROUP // n_dp
    table = np.zeros((n_dp, 4, OWNED), np.int32)
    for owner in range(n_dp):
        for quarter in range(4):
            found = [
                local
                for local in range(span)
                if (owner * span + local) // 8 % 2 == quarter % 2
                and (owner * span + local) % 8 // 4 == quarter // 2
            ]
            table[owner, quarter] = (found + [0] * OWNED)[:OWNED]
    return table


def group_sources(n_dp):
    span = K1 // GROUP // n_dp
    table = np.zeros((n_dp, span), np.int32)
    for owner in range(n_dp):
        met = [0] * 4
        for local in range(span):
            group = owner * span + local
            quarter = group % 8 // 4 * 2 + group // 8 % 2
            table[owner, local] = quarter * OWNED + met[quarter]
            met[quarter] += 1
    return table


def by_groups(n_dp):
    return n_dp == 8


def deal_kernel(table, weight_ref, rois_ref, out_ref):
    base = lax.axis_index("dp") * 4 * OWNED
    for quarter in range(4):

        def step(index, carry, quarter=quarter):
            source = pl.ds(
                pl.multiple_of(table[base + quarter * OWNED + index] * GROUP, GROUP), GROUP
            )
            target = pl.ds(pl.multiple_of(index * GROUP, GROUP), GROUP)
            out_ref[quarter, target, :] = weight_ref[source, :].astype(jnp.bfloat16)
            return carry

        lax.fori_loop(0, OWNED, step, 0)
        out_ref[quarter, OWNED * GROUP :, :] = rois_ref[...]


def gather_quarter(first_weight, second_weight, rois, n_dp):
    cols = first_weight.shape[1]
    second = second_weight.astype(jnp.bfloat16)
    if by_groups(n_dp):
        table = jnp.asarray(owned_groups(n_dp).reshape(-1))
        top = lax.optimization_barrier(rois[8:].astype(jnp.bfloat16))
        rest = rois[8:] - top.astype(jnp.float32)
        middle_term = lax.optimization_barrier(rest.astype(jnp.bfloat16))
        last = (rest - middle_term.astype(jnp.float32)).astype(jnp.bfloat16)
        riders = jnp.concatenate((rois[:8].astype(jnp.bfloat16), top, middle_term, last), axis=0)
        riders = jnp.pad(riders, ((0, GROUP - riders.shape[0]), (0, 0)))
        dealt = pl.pallas_call(
            deal_kernel,
            out_shape=jax.ShapeDtypeStruct((4, SHARD * GROUP, cols), jnp.bfloat16),
            in_specs=[
                pl.BlockSpec(memory_space=pltpu.SMEM),
                pl.BlockSpec(memory_space=pltpu.VMEM),
                pl.BlockSpec(memory_space=pltpu.VMEM),
            ],
            out_specs=pl.BlockSpec(memory_space=pltpu.VMEM),
            name="deal_rows",
        )(table, first_weight, riders)
        swapped = lax.all_to_all(dealt, "blk", split_axis=0, concat_axis=0, tiled=True)
        ridden = swapped[:, OWNED * GROUP :].astype(jnp.float32).transpose(1, 0, 2)
        ridden = ridden.reshape(GROUP, -1)
        all_rois = jnp.concatenate(
            (ridden[:8], (ridden[8:12] + ridden[12:16]) + ridden[16:20]), axis=0
        )
        rows = swapped[:, : OWNED * GROUP].transpose(1, 0, 2).reshape(OWNED * GROUP, -1)
        block = second.reshape(2, 2, GROUP, cols).transpose(0, 2, 1, 3).reshape(2 * GROUP, -1)
        ahead = jnp.concatenate((rows[:, :AHEAD], block), axis=0)
        gathered = lax.all_gather(ahead, "dp", axis=0, tiled=True)
        behind = rows[:, AHEAD:]
        swapped = lax.ppermute(behind, "dp", [(spot, spot ^ 1) for spot in range(n_dp)])
        return (gathered, behind, swapped), all_rois
    all_rois = lax.all_gather(rois, "blk", axis=1, tiled=True)
    rows = lax.all_gather(first_weight.astype(jnp.bfloat16), "dp", axis=0, tiled=True)
    split = jnp.pad(rows.reshape(BINS, C, cols), ((0, 2 * SLOTS - BINS), (0, 0), (0, 0)))
    split = split.reshape(SLOTS, 2, 2, HALF, cols).transpose(2, 1, 0, 3, 4)
    split = split.reshape(4, KQ, cols)
    mine = lax.all_to_all(split, "blk", split_axis=0, concat_axis=0, tiled=True)
    mine = mine.transpose(1, 0, 2).reshape(KQ, -1)
    second = lax.all_gather(second, "dp", axis=0, tiled=True)
    block = second.reshape(4, -1, cols).transpose(1, 0, 2).reshape(-1, 4 * cols)
    rows = jnp.concatenate((mine, block), axis=0)
    return (rows, rows, rows), all_rois


def second_blocks(source, target, column, sem, n_dp):
    owners, rows = (n_dp, GROUP) if by_groups(n_dp) else (1, H // 4)
    copies = []
    for owner in range(owners):
        for part in range(4):
            if by_groups(n_dp):
                first = owner * AHEAD_ROWS + (OWNED + part // 2) * GROUP
                lane = part % 2 * 256
            else:
                first, lane = KQ, part * 256
            copies.append(
                pltpu.make_async_copy(
                    source.at[pl.ds(first, rows), pl.ds(lane, 256)],
                    target.at[pl.ds((owner * 4 + part) * rows, rows), column],
                    sem.at[owner * 4 + part],
                )
            )
    return copies


def owner_rows(half, parity, owner, n_dp):
    span = K1 // GROUP // n_dp
    begin = groups_before(half, parity, owner * span)
    end = groups_before(half, parity, (owner + 1) * span)
    many = pl.ds(pl.multiple_of(begin * GROUP, GROUP), (OWNED - 1) * GROUP)
    last = pl.ds(pl.multiple_of((end - 1) * GROUP, GROUP), GROUP)
    return many, last, end - begin == OWNED


def ahead_copies(source, target, sems, half, parity, n_dp):
    copies = []
    for owner in range(n_dp):
        many, last, full = owner_rows(half, parity, owner, n_dp)
        first, rows = owner * AHEAD_ROWS, (OWNED - 1) * GROUP
        copies.append(
            (
                None,
                pltpu.make_async_copy(
                    source.at[pl.ds(first, rows), :], target.at[many, :], sems.at[2 * owner]
                ),
            )
        )
        copies.append(
            (
                full,
                pltpu.make_async_copy(
                    source.at[pl.ds(first + rows, GROUP), :],
                    target.at[last, :],
                    sems.at[2 * owner + 1],
                ),
            )
        )
    return copies


def whole_copies(source, targets, sems):
    return [
        (
            None,
            pltpu.make_async_copy(
                source.at[pl.ds(0, KQ), pl.ds(half * AHEAD, AHEAD)], target, sems.at[half]
            ),
        )
        for half, target in enumerate(targets)
    ]


def each_copy(copies, action):
    for condition, copy in copies:
        if condition is None:
            action(copy)
        else:

            @pl.when(condition)
            def _(copy=copy):
                action(copy)


def wipe_slots(target, parity):
    target[KQ - HALF :, :] = jnp.zeros((HALF, AHEAD), jnp.bfloat16)

    @pl.when(parity == 1)
    def _():
        target[KQ - 2 * HALF : KQ - HALF, :] = jnp.zeros((HALF, AHEAD), jnp.bfloat16)


def gelu_parts(values):
    cdf = 0.5 * (1.0 + lax.erf(values * np.float32(np.sqrt(0.5))))
    density = jnp.exp(-0.5 * values * values) * np.float32(1.0 / np.sqrt(2.0 * np.pi))
    return values * cdf, cdf + values * density


def middle_kernel(
    n_dp,
    pooled_hbm,
    ahead_hbm,
    behind_hbm,
    swapped_hbm,
    predict_ref,
    bias_ref,
    aux_ref,
    valid_ref,
    all_grad,
    second_out,
    tail_ref,
    ordered_hbm,
    pooled,
    ahead,
    behind,
    second_ref,
    part,
    sent,
    came,
    first_pre,
    second_pre,
    first_act,
    second_act,
    first_grad,
    second_grad,
    valid_came,
    pooled_sem,
    weight_sem,
    own_sem,
    second_sem,
    out_sem,
    up_send,
    up_recv,
    down_send,
    down_recv,
    y_send,
    y_recv,
    valid_send,
    valid_recv,
    send_sem,
    recv_sem,
):
    me = lax.axis_index("blk")
    dp = lax.axis_index("dp")
    peers = [(dp + step) % n_dp for step in range(1, n_dp)] if by_groups(n_dp) else []
    high, low = me // 2, me % 2
    sibling = high * 2 + (1 - low)
    across = (1 - high) * 2 + low
    corner = (1 - high) * 2 + (1 - low)
    rows = part.shape[0]
    quarter = H // 4

    barrier = pltpu.get_barrier_semaphore()
    for other in (sibling, across, corner):
        pl.semaphore_signal(barrier, inc=1, device_id={"blk": other}, device_id_type=MESH)
    for peer in peers:
        pl.semaphore_signal(barrier, inc=1, device_id={"dp": peer}, device_id_type=MESH)

    def hidden_cols(which):
        return pl.ds(pl.multiple_of(which * quarter, quarter), quarter)

    z, y = dp // 2, dp % 2
    partner = 2 * z + 1 - y
    shard = (OWNED - 1) * GROUP

    def shard_pieces(owner):
        many, last, full = owner_rows(high, low, owner, n_dp)
        first = many.start
        return (
            (None, pl.ds(pl.multiple_of(first, GROUP), shard // 2), pl.ds(0, shard // 2)),
            (
                None,
                pl.ds(pl.multiple_of(first + shard // 2, GROUP), shard // 2),
                pl.ds(shard // 2, shard // 2),
            ),
            (full, last, pl.ds(shard, GROUP)),
        )

    def shard_copies(owner, send, recv, index, target, own=False):
        copies = []
        for piece, (condition, place, source) in enumerate(shard_pieces(owner)):
            copies.append(
                (
                    condition,
                    pltpu.make_async_remote_copy(
                        src_ref=behind_hbm.at[source, :] if own else behind.at[place, :],
                        dst_ref=behind.at[place, :],
                        send_sem=send.at[3 * index + piece],
                        recv_sem=recv.at[3 * index + piece],
                        device_id={"dp": target},
                        device_id_type=MESH,
                    ),
                )
            )
        return copies

    def own_shard(action):
        @pl.when(z < 3)
        def _():
            each_copy(shard_copies(dp, up_send, up_recv, 0, dp + 2, True), action)

        @pl.when(z > 0)
        def _():
            each_copy(shard_copies(dp, down_send, down_recv, 0, dp - 2, True), action)

    def relay_shards(distance, took, action, pieces=(0, 1, 2)):
        def pass_on(owner, send, recv, neighbour, goes_on, place):
            coming = shard_copies(owner, send, recv, distance - 1, neighbour)
            aside = shard_copies(owner, y_send, y_recv, place, partner)
            onward = [None] * len(coming)
            if distance < 3:
                onward = shard_copies(owner, send, recv, distance, neighbour)
            for piece in pieces:
                came_in, on, over = coming[piece], onward[piece], aside[piece]
                each_copy([came_in], took)
                if on is not None:

                    @pl.when(goes_on)
                    def _(on=on):
                        each_copy([on], action)

                each_copy([over], action)

        @pl.when(z >= distance)
        def _():
            pass_on(dp - 2 * distance, up_send, up_recv, dp + 2, z < 3, z - distance)

        @pl.when(z + distance <= 3)
        def _():
            pass_on(dp + 2 * distance, down_send, down_recv, dp - 2, z > 0, z + distance)

    def serve(distance, *pieces):
        if by_groups(n_dp):
            relay_shards(
                distance, lambda copy: copy.wait_recv(), lambda copy: copy.start(), pieces
            )

    blocks = second_blocks(ahead_hbm, second_ref, hidden_cols(me), second_sem, n_dp)
    for copy in blocks:
        copy.start()
    if by_groups(n_dp):
        early = ahead_copies(ahead_hbm, ahead, weight_sem, high, low, n_dp)
        late = []
        for which, (source_hbm, owner) in enumerate(((behind_hbm, dp), (swapped_hbm, partner))):
            for piece, (condition, place, source) in enumerate(shard_pieces(owner)):
                late.append(
                    (
                        condition,
                        pltpu.make_async_copy(
                            source_hbm.at[source, :],
                            behind.at[place, :],
                            out_sem.at[2 + 3 * which + piece],
                        ),
                    )
                )
        wipe_slots(ahead, low)
        wipe_slots(behind, low)
    else:
        early, late = whole_copies(ahead_hbm, (ahead, behind), weight_sem), []
    each_copy((*early, *late), lambda copy: copy.start())

    def chunk_rows(which):
        return pl.ds(pl.multiple_of(which * rows, 16), rows)

    order = (corner, across, sibling, me)
    chunks = [
        pltpu.make_async_copy(
            pooled_hbm.at[chunk_rows(which), :], pooled.at[chunk_rows(which), :], pooled_sem.at[i]
        )
        for i, which in enumerate(order)
    ]
    for chunk in chunks:
        chunk.start()
    pl.semaphore_wait(barrier, 3 + len(peers))
    counts = [
        pltpu.make_async_remote_copy(
            src_ref=valid_ref,
            dst_ref=valid_came.at[index],
            send_sem=valid_send.at[index],
            recv_sem=valid_recv.at[index],
            device_id={"dp": peer},
            device_id_type=MESH,
        )
        for index, peer in enumerate(peers)
    ]
    if by_groups(n_dp):
        own_shard(lambda copy: copy.start())
    for copy in counts:
        copy.start()

    def remote(source, target, index, other):
        return pltpu.make_async_remote_copy(
            src_ref=source,
            dst_ref=target,
            send_sem=send_sem.at[index],
            recv_sem=recv_sem.at[index],
            device_id={"blk": other},
            device_id_type=MESH,
        )

    for copy in blocks:
        copy.wait()
    mine, theirs = second_ref.at[:, hidden_cols(me)], second_ref.at[:, hidden_cols(across)]
    second_sibling = remote(mine, mine, 3, sibling)
    second_across = remote(mine, mine, 4, across)
    second_forward = remote(theirs, theirs, 5, sibling)
    second_across.start()
    second_sibling.start()

    def in_blocks(count, body):
        def step(index, carry):
            body(index)
            return carry

        lax.fori_loop(0, count, step, 0)

    def block32(step):
        return pl.ds(pl.multiple_of(step * 32, 32), 32)

    def first_half_product(which):
        cols = slice(which * AHEAD, (which + 1) * AHEAD)
        weight = (ahead, behind)[which]
        base = 18 * which
        to_sibling = remote(sent.at[0, :, cols], came.at[0, :, cols], base, sibling)
        to_across = remote(sent.at[1, :, cols], came.at[1, :, cols], base + 1, across)
        to_sibling_last = remote(sent.at[2, :, cols], came.at[2, :, cols], base + 2, sibling)

        def chunk_dot(i):
            if which == 0:
                chunks[i].wait()

            def cols_dot(step):
                lanes = pl.ds(pl.multiple_of(step * 256, 256), 256)
                target = pl.ds(pl.multiple_of(which * AHEAD + step * 256, 256), 256)
                part[:, target] = jnp.dot(
                    pooled[chunk_rows(order[i]), :],
                    weight[:, lanes],
                    preferred_element_type=jnp.float32,
                )

            in_blocks(AHEAD // 256, cols_dot)

        def hand_on(slot, came_slot=None):
            def store(step):
                block = block32(step)
                value = part[block, cols]
                if came_slot is not None:
                    value = value + came[came_slot, block, cols].astype(jnp.float32)
                sent[slot, block, cols] = value.astype(jnp.bfloat16)

            in_blocks(rows // 32, store)

        def step0():
            chunk_dot(0)
            hand_on(0)
            to_sibling.start()

        def step1():
            chunk_dot(1)
            to_sibling.wait_recv()
            hand_on(1, 0)
            to_across.start()

        def step2():
            chunk_dot(2)
            hand_on(2)
            to_sibling_last.start()

        def step3():
            chunk_dot(3)
            to_sibling_last.wait_recv()
            to_across.wait_recv()

            def activate(step):
                block = block32(step)
                value = (
                    part[block, cols]
                    + came[1, block, cols].astype(jnp.float32)
                    + came[2, block, cols].astype(jnp.float32)
                    + bias_ref[0:1, cols]
                )
                first_pre[block, cols] = value
                first_act[block, cols] = gelu_parts(value)[0].astype(jnp.bfloat16)

            in_blocks(rows // 32, activate)

        return (step0, step1, step2, step3), (to_sibling, to_across, to_sibling_last)

    steps, sums = first_half_product(0)
    each_copy(early, lambda copy: copy.wait())
    steps[0]()
    serve(1, 0)
    steps[1]()
    serve(1, 1, 2)
    serve(2, 0)
    second_across.wait_recv()
    second_forward.start()
    steps[2]()
    serve(2, 1, 2)
    steps[3]()
    serve(3, 0, 1, 2)
    each_copy(late, lambda copy: copy.wait())
    if by_groups(n_dp):
        for place in range(4):

            @pl.when(z != place)
            def _(place=place):
                each_copy(
                    shard_copies(2 * place + 1 - y, y_send, y_recv, place, partner),
                    lambda copy: copy.wait_recv(),
                )
    ordered_copies = [
        pltpu.make_async_copy(
            source, ordered_hbm.at[:, pl.ds(which * AHEAD, AHEAD)], out_sem.at[which]
        )
        for which, source in enumerate((ahead, behind))
    ]
    for copy in ordered_copies:
        copy.start()
    steps, more_sums = first_half_product(1)
    for step in steps:
        step()
    my_rows = chunk_rows(me)
    across_rows = chunk_rows(across)
    second_sibling.wait_recv()
    second_forward.wait_recv()

    def second_dot(step):
        cols = pl.ds(pl.multiple_of(step * 256, 256), 256)
        second_pre[:, cols] = (
            jnp.dot(first_act[...], second_ref[:, cols], preferred_element_type=jnp.float32)
            + bias_ref[1:2, cols]
        )

    in_blocks(H // 256, second_dot)

    def activate_second(step):
        block = block32(step)
        second_act[block, :] = gelu_parts(second_pre[block, :])[0].astype(jnp.bfloat16)

    in_blocks(rows // 32, activate_second)
    head_out = (
        jnp.dot(second_act[...], predict_ref[...], preferred_element_type=jnp.float32)
        + bias_ref[2:3, :HALF]
    )
    lane = lax.broadcasted_iota(jnp.int32, (rows, HALF), 1)
    is_logit = lane < CLASSES
    is_delta = (lane >= CLASSES) & (lane < CLASSES + 4)
    label = aux_ref[:, 0:1]
    valid_total = valid_ref[0:1, 0:1]
    for index, copy in enumerate(counts):
        copy.wait_recv()
        valid_total = valid_total + valid_came[index, 0:1, 0:1]
    share = aux_ref[:, 1:2] / jnp.maximum(valid_total, 1.0)
    foreground = (label > 0.5).astype(jnp.float32)
    onehot = (lane.astype(jnp.float32) == label).astype(jnp.float32)
    top = jnp.max(jnp.where(is_logit, head_out, -jnp.inf), axis=1, keepdims=True)
    exped = jnp.where(is_logit, jnp.exp(jnp.minimum(head_out - top, 0.0)), 0.0)
    exp_sum = jnp.sum(exped, axis=1, keepdims=True)
    chosen = jnp.sum(onehot * head_out, axis=1, keepdims=True)
    error = jnp.where(is_delta, head_out - aux_ref[...], 0.0)
    absolute = jnp.abs(error)
    huber = jnp.where(absolute < 1.0, 0.5 * error * error, absolute - 0.5)
    huber_sum = jnp.sum(jnp.where(is_delta, huber, 0.0), axis=1, keepdims=True)
    loss_rows = share * (jnp.log(exp_sum) + top - chosen + foreground * huber_sum)
    delta_slope = foreground * jnp.minimum(jnp.maximum(error, -1.0), 1.0)
    head_grad = (share * (exped / exp_sum - jnp.where(is_logit, onehot, 0.0) + delta_slope)).astype(
        jnp.bfloat16
    )
    wide = head_grad.astype(jnp.float32)
    lane1 = lax.broadcasted_iota(jnp.int32, (1, HALF), 1)
    head_bias = jnp.sum(wide, axis=0, keepdims=True) + jnp.where(
        lane1 == CLASSES + 4, jnp.sum(loss_rows, axis=0, keepdims=True), 0.0
    )

    def second_back(step):
        cols = pl.ds(pl.multiple_of(step * 256, 256), 256)
        back = contract_cols(head_grad, predict_ref[cols, :])
        second_grad[:, cols] = (back * gelu_parts(second_pre[:, cols])[1]).astype(jnp.bfloat16)

    in_blocks(H // 256, second_back)
    def first_back(step):
        cols = slice(step * quarter, (step + 1) * quarter)
        back = contract_cols(second_grad[...], second_ref[cols, :])
        first_grad[:, cols] = (back * gelu_parts(first_pre[:, cols])[1]).astype(jnp.bfloat16)
        source, target = first_grad.at[:, cols], all_grad.at[my_rows, cols]
        to_other = remote(source, target, 6 + step, across)
        to_twin = remote(source, target, 10 + step, sibling)
        to_other.start()
        to_twin.start()
        relayed = all_grad.at[across_rows, cols]
        return to_other, to_twin, remote(relayed, relayed, 14 + step, sibling)

    grad_copies = [first_back(step) for step in range(4)]
    grad_own = pltpu.make_async_copy(first_grad, all_grad.at[my_rows, :], own_sem.at[2])
    grad_own.start()

    def bias_rows(grads):
        total = jnp.sum(grads[...].astype(jnp.float32), axis=0, keepdims=True)
        return [total[:, i * HALF : (i + 1) * HALF] for i in range(H // HALF)]

    nothing = jnp.zeros((1, HALF), jnp.float32)
    bias_sums = (
        bias_rows(first_grad),
        bias_rows(second_grad),
        [head_bias] + [nothing] * 7,
        [nothing] * 8,
    )
    for step in range(4):
        piece = contract_rows(second_act[:, step * quarter : (step + 1) * quarter], head_grad)
        if by_groups(n_dp):
            for owner in range(n_dp):
                tail_ref[step, owner, :32, :] = piece[owner * 32 : owner * 32 + 32, :]
                tail_ref[step, owner, 32:, :] = jnp.concatenate(
                    [bias_sums[step][owner]] + [nothing] * 7, axis=0
                )
        else:
            tail_ref[step, :quarter, :] = piece
            tail_ref[step, quarter:, :] = jnp.concatenate(bias_sums[step], axis=0)

    for to_other, _, relay in grad_copies:
        to_other.wait_recv()
        relay.start()

    def second_block(step):
        cols = pl.ds(pl.multiple_of(step * 256, 256), 256)
        second_out[:, cols] = contract_rows(first_act[...], second_grad[:, cols]).astype(
            jnp.bfloat16
        )

    in_blocks(H // 256, second_block)
    grad_own.wait()
    for _, to_twin, relay in grad_copies:
        to_twin.wait_recv()
        relay.wait_recv()
    for copy in ordered_copies:
        copy.wait()
    if by_groups(n_dp):

        def sent_off(copy):
            copy.wait_send()

        own_shard(sent_off)
        for distance in (1, 2, 3):
            relay_shards(distance, lambda copy: None, sent_off)
    for copy in (
        *sums,
        *more_sums,
        second_sibling,
        second_across,
        second_forward,
        *(copy for three in grad_copies for copy in three),
        *counts,
    ):
        copy.wait_send()


def middle(pooled, ahead, behind, swapped, predict, bias, aux, valid_here, n_dp):
    count = pooled.shape[0]
    rows = aux.shape[0]
    tail = (4, n_dp, 40, HALF) if by_groups(n_dp) else (4, H // 4 + 8, HALF)
    any_spec = pl.BlockSpec(memory_space=pl.ANY)
    vmem_spec = pl.BlockSpec(memory_space=pltpu.VMEM)
    return pl.pallas_call(
        functools.partial(middle_kernel, n_dp),
        out_shape=(
            jax.ShapeDtypeStruct((count, H), jnp.bfloat16),
            jax.ShapeDtypeStruct((H, H), jnp.bfloat16),
            jax.ShapeDtypeStruct(tail, jnp.float32),
            jax.ShapeDtypeStruct((KQ, H), jnp.bfloat16),
        ),
        in_specs=[any_spec] * 4 + [vmem_spec] * 4,
        out_specs=(any_spec, vmem_spec, vmem_spec, any_spec),
        scratch_shapes=[
            pltpu.VMEM((count, KQ), jnp.bfloat16),
            pltpu.VMEM((KQ, AHEAD), jnp.bfloat16),
            pltpu.VMEM((KQ, AHEAD), jnp.bfloat16),
            pltpu.VMEM((H, H), jnp.bfloat16),
            pltpu.VMEM((rows, H), jnp.float32),
            pltpu.VMEM((3, rows, H), jnp.bfloat16),
            pltpu.VMEM((3, rows, H), jnp.bfloat16),
            pltpu.VMEM((rows, H), jnp.float32),
            pltpu.VMEM((rows, H), jnp.float32),
            pltpu.VMEM((rows, H), jnp.bfloat16),
            pltpu.VMEM((rows, H), jnp.bfloat16),
            pltpu.VMEM((rows, H), jnp.bfloat16),
            pltpu.VMEM((rows, H), jnp.bfloat16),
            pltpu.VMEM((7, 8, HALF), jnp.float32),
            pltpu.SemaphoreType.DMA((4,)),
            pltpu.SemaphoreType.DMA((SLOTS,)),
            pltpu.SemaphoreType.DMA((3,)),
            pltpu.SemaphoreType.DMA((4 * n_dp if by_groups(n_dp) else 4,)),
            pltpu.SemaphoreType.DMA((8,)),
            pltpu.SemaphoreType.DMA((9,)),
            pltpu.SemaphoreType.DMA((9,)),
            pltpu.SemaphoreType.DMA((9,)),
            pltpu.SemaphoreType.DMA((9,)),
            pltpu.SemaphoreType.DMA((12,)),
            pltpu.SemaphoreType.DMA((12,)),
            pltpu.SemaphoreType.DMA((7,)),
            pltpu.SemaphoreType.DMA((7,)),
            pltpu.SemaphoreType.DMA((21,)),
            pltpu.SemaphoreType.DMA((21,)),
        ],
        compiler_params=pltpu.CompilerParams(
            vmem_limit_bytes=VMEM_LIMIT, collective_id=0, has_side_effects=True
        ),
        cost_estimate=pl.CostEstimate(
            flops=9_000_000_000, bytes_accessed=25_000_000, transcendentals=1_500_000
        ),
        name="middle",
    )(pooled, ahead, behind, swapped, predict, bias, aux, valid_here)


def weight_grad_kernel(n_dp, meta, pooled_ref, grad_ref, here_hbm, there_hbm, later_hbm, stage, sems):
    half, parity, y = meta[0], meta[1], meta[2]
    step = pl.program_id(0)
    last = pl.num_programs(0) - 1

    def copies(which):
        buffer = which % 2
        for one in range(256 // GROUP):
            slot = 2 * which + one // 4
            owner, local = group_place(half, parity, slot, one % 4, n_dp)
            row = jnp.right_shift(owner, 1)
            inside = slot < SLOTS - 1 - parity
            here = jnp.bitwise_and(owner, 1) == y
            there = jnp.logical_not(here)
            for condition, target, place in (
                (here, here_hbm, row * OWNED + local),
                (there & (local < SWAPPED), there_hbm, row * SWAPPED + local),
                (there & (local >= SWAPPED), later_hbm, row * LATER + local - SWAPPED),
            ):

                @pl.when(inside & condition)
                def _(target=target, one=one, place=place):
                    rows = pl.ds(pl.multiple_of(place * GROUP, GROUP), GROUP)
                    pltpu.make_async_copy(
                        stage.at[buffer, pl.ds(one * GROUP, GROUP), :],
                        target.at[rows, :],
                        sems.at[buffer, one],
                    ).start()

    def waits(which):
        buffer = which % 2
        for one in range(256 // GROUP):

            @pl.when(2 * which + one // 4 < SLOTS - 1 - parity)
            def _(one=one):
                rows = pl.ds(one * GROUP, GROUP)
                pltpu.make_async_copy(
                    stage.at[buffer, rows, :], here_hbm.at[rows, :], sems.at[buffer, one]
                ).wait()

    @pl.when(step >= 2)
    def _():
        waits(step - 2)

    stage[step % 2] = contract_rows(pooled_ref[...], grad_ref[...]).astype(jnp.bfloat16)
    copies(step)

    @pl.when(step == last)
    def _():
        waits(step - 1)
        waits(step)


def weight_grad(pooled, all_grad, meta, n_dp):
    count = pooled.shape[0]
    shapes = tuple(
        jax.ShapeDtypeStruct((n_dp // 2 * groups * GROUP, H), jnp.bfloat16)
        for groups in (OWNED, SWAPPED, LATER)
    )
    any_spec = pl.BlockSpec(memory_space=pl.ANY)
    return pl.pallas_call(
        functools.partial(weight_grad_kernel, n_dp),
        grid=(SLOTS // 2,),
        out_shape=shapes,
        in_specs=[
            pl.BlockSpec(memory_space=pltpu.SMEM),
            pl.BlockSpec((count, 256), lambda i: (0, i)),
            pl.BlockSpec((count, H), lambda i: (0, 0)),
        ],
        out_specs=(any_spec, any_spec, any_spec),
        scratch_shapes=[
            pltpu.VMEM((2, 256, H), jnp.bfloat16),
            pltpu.SemaphoreType.DMA((2, 256 // GROUP)),
        ],
        compiler_params=pltpu.CompilerParams(vmem_limit_bytes=VMEM_LIMIT),
        cost_estimate=pl.CostEstimate(
            flops=7_000_000_000, bytes_accessed=16_000_000, transcendentals=0
        ),
        name="weight_grad",
    )(meta, pooled, all_grad)


def reduce_kernel(
    n_dp,
    here_hbm,
    swapped_hbm,
    later_hbm,
    tail_ref,
    second_ref,
    cells_hbm,
    home_ref,
    second_out,
    tails_ref,
    kept_hbm,
    far_hbm,
    cells_kept,
    cells_near,
    cells_own,
    cells_sum,
    mine,
    y_came,
    up_came,
    down_came,
    final,
    tail_near,
    tail_mine,
    tail_came,
    second_came,
    tail_send,
    tail_recv,
    second_send,
    second_recv,
    cells_load,
    cells_send,
    cells_recv,
    shard_load,
    y_send,
    y_recv,
    up_send,
    up_recv,
    down_send,
    down_recv,
    home_send,
    home_recv,
):
    dp = lax.axis_index("dp")
    me = lax.axis_index("blk")
    half, parity = me // 2, me % 2
    z, y = dp // 2, dp % 2
    home_rows = OWNED * GROUP
    quarter = H // 4
    sibling, across = me // 2 * 2 + 1 - me % 2, (me + 2) % 4
    others = ((me + 1) % 4, (me + 2) % 4, (me + 3) % 4)
    has_below, has_above = z > 0, z < 3

    barrier = pltpu.get_barrier_semaphore()

    def greet(**where):
        pl.semaphore_signal(barrier, inc=1, device_id=where, device_id_type=MESH)

    peers = tuple((dp + step) % n_dp for step in range(1, n_dp))
    for peer in peers:
        greet(dp=peer)
    for other in others:
        greet(blk=other)

    def order(k):
        near, far = ((3, 3), (2, 0), (1, 2), (0, 1))[k]
        low_side = jnp.where(z % 3 == 0, near, far)
        return jnp.where(z < 2, low_side, 3 - low_side)

    def shard_loads(k):
        target = order(k)
        rows = pl.ds(pl.multiple_of(target * home_rows, GROUP), home_rows)
        some = SWAPPED * GROUP
        swapped = pl.ds(pl.multiple_of(target * some, GROUP), some)
        return [
            pltpu.make_async_copy(here_hbm.at[rows, :], mine.at[target], shard_load.at[2 * k]),
            pltpu.make_async_copy(
                swapped_hbm.at[swapped, :],
                y_came.at[target, pl.ds(0, some)],
                shard_load.at[2 * k + 1],
            ),
        ]

    for k in range(4):
        for copy in shard_loads(k):
            copy.start()
    pl.semaphore_wait(barrier, n_dp + 2)

    def remote(source, target, send, recv, **where):
        return pltpu.make_async_remote_copy(
            src_ref=source,
            dst_ref=target,
            send_sem=send,
            recv_sem=recv,
            device_id=where,
            device_id_type=MESH,
        )

    piece = tail_ref.shape[2]
    nears, seconds = [], []
    for index, other in enumerate(others):
        nears.append(
            remote(
                tail_ref.at[other],
                tail_near.at[index],
                tail_send.at[index],
                tail_recv.at[index],
                blk=other,
            )
        )
        seconds.append(
            remote(
                second_ref.at[:, pl.ds(pl.multiple_of(other * quarter, quarter), quarter)],
                second_came.at[index],
                second_send.at[index],
                second_recv.at[index],
                blk=other,
            )
        )

    quarter_cells = cells_sum.shape[0]

    def cell_rows(which):
        return cells_hbm.at[pl.ds(pl.multiple_of(which * quarter_cells, 16), quarter_cells), :]

    loads, gives = [], []
    for index, chip in enumerate((1 - half, half)):
        loads.append(
            pltpu.make_async_copy(
                cell_rows(2 * chip + parity), cells_own.at[index], cells_load.at[index]
            )
        )
        gives.append(
            remote(
                cell_rows(2 * chip + 1 - parity),
                cells_near.at[index],
                cells_send.at[index],
                cells_recv.at[index],
                blk=sibling,
            )
        )
    kept_out = pltpu.make_async_copy(cells_kept, kept_hbm, cells_load.at[2])
    crossing = remote(cells_sum, far_hbm, cells_send.at[2], cells_recv.at[2], blk=across)
    parts = (pl.ds(0, SWAPPED * GROUP), pl.ds(SWAPPED * GROUP, LATER * GROUP))

    def y_copy(k):
        target = order(k)
        rows = pl.ds(pl.multiple_of(target * LATER * GROUP, GROUP), LATER * GROUP)
        return remote(
            later_hbm.at[rows, :],
            y_came.at[target, parts[1]],
            y_send.at[k],
            y_recv.at[k],
            dp=2 * z + 1 - y,
        )

    for k in range(4):
        y_copy(k).start()
    for copy in (*nears, *seconds, *gives, *loads):
        copy.start()

    def cell_blocks(body):
        def step(index, carry):
            body(pl.ds(pl.multiple_of(index * 160, 160), 160))
            return carry

        lax.fori_loop(0, quarter_cells // 160, step, 0)

    def give_across():
        loads[0].wait()
        gives[0].wait_recv()

        def add(rows):
            cells_sum[rows, :] = (
                cells_own[0, rows, :].astype(jnp.float32)
                + cells_near[0, rows, :].astype(jnp.float32)
            ).astype(jnp.bfloat16)

        cell_blocks(add)
        crossing.start()

    def keep_here():
        loads[1].wait()
        gives[1].wait_recv()

        def add(rows):
            cells_kept[rows, :] = cells_own[1, rows, :].astype(jnp.float32) + cells_near[
                1, rows, :
            ].astype(jnp.float32)

        cell_blocks(add)
        kept_out.start()

    def add_up(target, sources, part):
        first, groups = ((0, SWAPPED), (SWAPPED, LATER))[part]

        def step(index, carry):
            rows = pl.ds(pl.multiple_of((first + index) * GROUP, GROUP), GROUP)
            total = mine[target, rows, :].astype(jnp.float32)
            for ref in sources:
                total = total + ref[target, rows, :].astype(jnp.float32)
            mine[target, rows, :] = total.astype(jnp.bfloat16)
            return carry

        lax.fori_loop(0, groups, step, 0)

    def z_copy(target, part, came, send, recv, neighbour):
        sem = 2 * target + part
        return remote(
            mine.at[target, parts[part]],
            came.at[target, parts[part]],
            send.at[sem],
            recv.at[sem],
            dp=neighbour,
        )

    def up_copy(target, part):
        return z_copy(target, part, up_came, up_send, up_recv, dp + 2)

    def down_copy(target, part):
        return z_copy(target, part, down_came, down_send, down_recv, dp - 2)

    def arrive(k, part):
        if part == 0:
            for copy in shard_loads(k):
                copy.wait()
        else:
            y_copy(k).wait_recv()

    def chain(k, part):
        target = order(k)
        arrive(k, part)

        @pl.when(target > z)
        def _():
            @pl.when(has_below)
            def _():
                up_copy(target, part).wait_recv()
                add_up(target, (y_came, up_came), part)

            @pl.when(jnp.logical_not(has_below))
            def _():
                add_up(target, (y_came,), part)

            up_copy(target, part).start()

        @pl.when(target < z)
        def _():
            @pl.when(has_above)
            def _():
                down_copy(target, part).wait_recv()
                add_up(target, (y_came, down_came), part)

            @pl.when(jnp.logical_not(has_above))
            def _():
                add_up(target, (y_came,), part)

            down_copy(target, part).start()

    def last(part):
        arrive(3, part)
        add_up(z, (y_came,), part)

        @pl.when(has_below)
        def _():
            up_copy(z, part).wait_recv()
            add_up(z, (up_came,), part)

        @pl.when(has_above)
        def _():
            down_copy(z, part).wait_recv()
            add_up(z, (down_came,), part)

    def home_copies(part):
        copies = []
        for index, other in enumerate(others):
            cols = pl.ds(pl.multiple_of(other * quarter, quarter), quarter)
            copies.append(
                remote(
                    mine.at[z, parts[part], cols],
                    final.at[me, parts[part]],
                    home_send.at[3 * part + index],
                    home_recv.at[3 * part + index],
                    blk=other,
                )
            )
        return copies

    chain(0, 0)
    give_across()
    for copy in nears:
        copy.wait_recv()
    tail_mine[...] = tail_ref[me] + tail_near[0] + tail_near[1] + tail_near[2]
    tails = []
    for index, peer in enumerate(peers):
        sem = 3 + index
        tails.append(
            remote(
                tail_mine.at[peer],
                tail_came.at[index],
                tail_send.at[sem],
                tail_recv.at[sem],
                dp=peer,
            )
        )
    for copy in tails:
        copy.start()
    chain(1, 0)
    for copy in tails:
        copy.wait_recv()
    my_tail = pl.ds(pl.multiple_of((me * n_dp + dp) * piece, 8), piece)
    total = tail_mine[dp]
    for index in range(n_dp - 1):
        total = total + tail_came[index]
    tails_ref[my_tail, :] = total
    spreads = []
    for index, peer in enumerate(peers):
        spot = tails_ref.at[my_tail, :]
        sem = n_dp + 2 + index
        spreads.append(remote(spot, spot, tail_send.at[sem], tail_recv.at[sem], dp=peer))
    for copy in spreads:
        copy.start()
    keep_here()
    chain(2, 0)
    last(0)
    homes = home_copies(0)
    for copy in homes:
        copy.start()
    for k in range(3):
        chain(k, 1)
    block = tails_ref.at[pl.ds(pl.multiple_of(me * n_dp * piece, 8), n_dp * piece), :]
    shares = []
    for index, other in enumerate(others):
        sem = 2 * n_dp + 1 + index
        shares.append(remote(block, block, tail_send.at[sem], tail_recv.at[sem], blk=other))
    for copy in spreads:
        copy.wait_recv()
    for copy in shares:
        copy.start()
    own_cols = pl.ds(pl.multiple_of(me * quarter, quarter), quarter)
    second = second_ref[:, own_cols].astype(jnp.float32)
    for index, copy in enumerate(seconds):
        copy.wait_recv()
        second = second + second_came[index].astype(jnp.float32)
    second_out[...] = second
    last(1)
    homes_later = home_copies(1)
    for copy in homes_later:
        copy.start()
    home_ref[pl.ds(pl.multiple_of(me * home_rows, GROUP), home_rows), :] = mine[z, :, own_cols]
    for copy in shares:
        copy.wait_recv()
    for index in range(3):
        sender = (me + 3 - index) % 4
        homes[index].wait_recv()
        homes_later[index].wait_recv()
        rows = pl.ds(pl.multiple_of(sender * home_rows, GROUP), home_rows)
        home_ref[rows, :] = final[sender]
    for copy in (
        *homes,
        *homes_later,
        *nears,
        *tails,
        *spreads,
        *shares,
        *seconds,
        *gives,
        crossing,
        *(y_copy(k) for k in range(4)),
    ):
        copy.wait_send()
    kept_out.wait()
    crossing.wait_recv()
    for k in range(3):
        target = order(k)

        @pl.when(target > z)
        def _():
            up_copy(target, 0).wait_send()
            up_copy(target, 1).wait_send()

        @pl.when(target < z)
        def _():
            down_copy(target, 0).wait_send()
            down_copy(target, 1).wait_send()


def reduce_home(here, swapped, later, tail, second, cell_grads, n_dp):
    home = OWNED * GROUP
    piece = tail.shape[2]
    cells = cell_grads.shape[0] // 4
    vmem_spec = pl.BlockSpec(memory_space=pltpu.VMEM)
    any_spec = pl.BlockSpec(memory_space=pl.ANY)
    shards = pltpu.VMEM((4, home, H), jnp.bfloat16)

    def sems(number):
        return pltpu.SemaphoreType.DMA((number,))

    return pl.pallas_call(
        functools.partial(reduce_kernel, n_dp),
        out_shape=(
            jax.ShapeDtypeStruct((4 * home, H // 4), jnp.bfloat16),
            jax.ShapeDtypeStruct((H // n_dp, H // 4), jnp.float32),
            jax.ShapeDtypeStruct((4 * n_dp * piece, HALF), jnp.float32),
            jax.ShapeDtypeStruct((cells, HALF), jnp.float32),
            jax.ShapeDtypeStruct((cells, HALF), jnp.bfloat16),
        ),
        in_specs=[any_spec, any_spec, any_spec, vmem_spec, vmem_spec, any_spec],
        out_specs=(vmem_spec,) * 3 + (any_spec,) * 2,
        scratch_shapes=[
            pltpu.VMEM((cells, HALF), jnp.float32),
            pltpu.VMEM((2, cells, HALF), jnp.bfloat16),
            pltpu.VMEM((2, cells, HALF), jnp.bfloat16),
            pltpu.VMEM((cells, HALF), jnp.bfloat16),
            shards,
            shards,
            shards,
            shards,
            pltpu.VMEM((4, home, H // 4), jnp.bfloat16),
            pltpu.VMEM((3, n_dp, piece, HALF), jnp.float32),
            pltpu.VMEM((n_dp, piece, HALF), jnp.float32),
            pltpu.VMEM((n_dp - 1, piece, HALF), jnp.float32),
            pltpu.VMEM((3, H // n_dp, H // 4), jnp.bfloat16),
            sems(2 * n_dp + 4),
            sems(2 * n_dp + 4),
            sems(3),
            sems(3),
            sems(3),
            sems(3),
            sems(3),
            sems(8),
            sems(4),
            sems(4),
            sems(8),
            sems(8),
            sems(8),
            sems(8),
            sems(6),
            sems(6),
        ],
        compiler_params=pltpu.CompilerParams(
            vmem_limit_bytes=VMEM_LIMIT, collective_id=1, has_side_effects=True
        ),
        cost_estimate=pl.CostEstimate(
            flops=60_000_000_000, bytes_accessed=200_000_000, transcendentals=0
        ),
        name="reduce_home",
    )(here, swapped, later, tail, second, cell_grads)


def sum_apart(pooled, all_grad, n_blk):
    first_wgrad = contract_rows(pooled, all_grad).astype(jnp.bfloat16)
    split = first_wgrad.reshape(KQ, n_blk, -1).transpose(1, 0, 2)
    mine = lax.all_to_all(split, "blk", split_axis=0, concat_axis=0, tiled=True)
    cols = mine.shape[2]
    mine = mine.reshape(2, 2, SLOTS, HALF, cols).transpose(2, 1, 0, 3, 4)
    mine = mine.reshape(2 * SLOTS, C, cols)[:BINS].reshape(K1, cols)
    first_sum = lax.psum_scatter(mine, "dp", scatter_dimension=0, tiled=True).astype(jnp.float32)
    return first_sum


def finish_kernel(
    table,
    home_ref,
    weight_ref,
    mean_ref,
    square_ref,
    kept_ref,
    far_ref,
    new_ref,
    new_mean_ref,
    new_square_ref,
    features_ref,
):
    groups = weight_ref.shape[0] // GROUP
    span = K1 // GROUP // lax.axis_size("dp")
    base = lax.axis_index("dp") * span + pl.program_id(0) * groups
    my_half = lax.axis_index("blk") // 2
    for index in range(groups):
        source = pl.ds(pl.multiple_of(table[base + index] * GROUP, GROUP), GROUP)
        rows = slice(index * GROUP, (index + 1) * GROUP)
        updated = adamw(
            weight_ref[rows, :],
            home_ref[source, :].astype(jnp.float32),
            mean_ref[rows, :],
            square_ref[rows, :],
            rate_first,
        )
        new_ref[rows, :], new_mean_ref[rows, :], new_square_ref[rows, :] = updated
    for half in range(2):

        @pl.when(my_half == half)
        def _(half=half):
            features_ref[:, half * HALF : (half + 1) * HALF] = kept_ref[...]
            features_ref[:, (1 - half) * HALF : (2 - half) * HALF] = far_ref[...].astype(
                jnp.float32
            )


def finish(home, kept, far, first_weight, first_mean, first_square, n_dp):
    cols = first_weight.shape[1]
    steps = 7
    table = jnp.asarray(group_sources(n_dp).reshape(-1))
    block = pl.BlockSpec((first_weight.shape[0] // steps, cols), lambda i: (i, 0))
    shape = jax.ShapeDtypeStruct(first_weight.shape, jnp.float32)
    cells = kept.shape[0]
    some = -(-cells // steps // 16) * 16
    part = pl.BlockSpec((some, HALF), lambda i: (i, 0))
    return pl.pallas_call(
        finish_kernel,
        grid=(steps,),
        out_shape=(shape, shape, shape, jax.ShapeDtypeStruct((cells, C), jnp.float32)),
        in_specs=[
            pl.BlockSpec(memory_space=pltpu.SMEM),
            pl.BlockSpec(memory_space=pltpu.VMEM),
            block,
            block,
            block,
            part,
            part,
        ],
        out_specs=(block, block, block, pl.BlockSpec((some, C), lambda i: (i, 0))),
        compiler_params=pltpu.CompilerParams(vmem_limit_bytes=VMEM_LIMIT),
        name="finish",
    )(table, home, first_weight, first_mean, first_square, kept, far)


def on_device(
    features,
    roi_table,
    offsets,
    box_targets,
    first_weight,
    first_mean,
    first_square,
    second_weight,
    second_mean,
    second_square,
    out_weight,
    out_mean,
    out_square,
    biases,
    bias_mean,
    bias_square,
    n_dp,
    n_blk,
):
    place = lax.axis_index("blk")
    half = place // 2
    parity = place % 2
    roi_count = roi_table.shape[1]
    outw = out_weight.shape[1]
    rois = jnp.concatenate((roi_table.astype(jnp.float32), box_targets), axis=0)
    weight, all_rois = gather_quarter(first_weight, second_weight, rois, n_dp)
    valid_here = jnp.broadcast_to(jnp.sum(all_rois[7]), (8, HALF))
    if not by_groups(n_dp):
        valid_here = lax.psum(valid_here, "dp")
    predict = jnp.pad(out_weight.astype(jnp.bfloat16), ((0, 0), (0, HALF - outw)))
    bias = jnp.zeros((8, H), jnp.float32)
    bias = bias.at[0].set(biases[:H]).at[1].set(biases[H : 2 * H]).at[2, :outw].set(biases[2 * H :])

    table, targets, starts = sort_rois(all_rois[:8].astype(jnp.int32), all_rois[8:])
    lows = window_lows(offsets)
    row_sevens, col_sevens, rows_at, cols_at = sample_points(table, offsets, parity)
    apart = ((0, 0), (0, 64 - 7))
    points = jnp.concatenate((jnp.pad(row_sevens, apart), jnp.pad(col_sevens, apart)), axis=1)

    def by_group(values):
        grouped = values.reshape(-1, BATCH, SLOTS).transpose(0, 2, 1).reshape(-1, SLOTS * BATCH)
        return jnp.pad(grouped, ((0, 0), (0, LANES - SLOTS * BATCH)), constant_values=FAR)

    my_table = lax.dynamic_slice_in_dim(table, place * roi_count, roi_count, axis=1)
    my_targets = lax.dynamic_slice_in_dim(targets, place * roi_count, roi_count, axis=0)
    aux = jnp.concatenate(
        (
            my_table[6].astype(jnp.float32)[:, None],
            my_table[7].astype(jnp.float32)[:, None],
            jnp.zeros((roi_count, CLASSES - 2), jnp.float32),
            my_targets,
            jnp.zeros((roi_count, HALF - CLASSES - 4), jnp.float32),
        ),
        axis=1,
    )
    meta = jnp.stack((half, parity, lax.axis_index("dp") % 2))
    pooled = pool(features, meta, starts, lows, points)
    all_grad, second_wgrad, tail, ordered = middle(
        pooled, *weight, predict, bias, aux, valid_here, n_dp
    )
    second_part = lax.psum_scatter(second_wgrad, "dp", scatter_dimension=0, tiled=True)
    if by_groups(n_dp):
        here, there, later = weight_grad(pooled, all_grad, meta, n_dp)
        swapped = lax.ppermute(there, "dp", [(spot, spot ^ 1) for spot in range(n_dp)])
    cell_grads = spread(
        all_grad, ordered, starts, lows, by_group(rows_at), by_group(cols_at), features.shape[0]
    )
    if by_groups(n_dp):
        home, second_sum, tails, kept, far = reduce_home(
            here, swapped, later, tail, second_part, cell_grads, n_dp
        )
        first_new, first_mean_new, first_square_new, feature_grads = finish(
            home, kept, far, first_weight, first_mean, first_square, n_dp
        )
        tails = tails.reshape(n_blk, n_dp, -1, HALF)
        out_sum = tails[:, :, : -8].reshape(H, HALF)[:, :outw]
        bias_flat = tails[:, :, -8].reshape(-1)
    else:
        first_new, first_mean_new, first_square_new = adamw(
            first_weight, sum_apart(pooled, all_grad, n_blk), first_mean, first_square, rate_first
        )
        parts = lax.all_to_all(
            cell_grads.reshape(n_blk, -1, HALF), "blk", split_axis=0, concat_axis=0, tiled=True
        ).astype(jnp.float32)
        feature_grads = jnp.concatenate((parts[0] + parts[1], parts[2] + parts[3]), axis=1)
        second_sum = lax.psum_scatter(second_part, "blk", scatter_dimension=1, tiled=True)
        second_sum = second_sum.astype(jnp.float32)
        tails = lax.psum(tail, ("dp", "blk"))
        out_sum = tails[:, : H // n_blk].reshape(H, HALF)[:, :outw]
        bias_flat = tails[:, H // n_blk :].reshape(-1)
    bias_sum = bias_flat[: biases.shape[0]]
    total_loss = bias_flat[biases.shape[0]]

    second_new, second_mean_new, second_square_new = adamw(
        second_weight, second_sum, second_mean, second_square, rate_second
    )
    out_new, out_mean_new, out_square_new = adamw(
        out_weight, out_sum, out_mean, out_square, rate_out
    )
    bias_new, bias_mean_new, bias_square_new = adamw(
        biases, bias_sum, bias_mean, bias_square, rate_bias
    )
    return (
        feature_grads,
        total_loss,
        first_new,
        first_mean_new,
        first_square_new,
        second_new,
        second_mean_new,
        second_square_new,
        out_new,
        out_mean_new,
        out_square_new,
        bias_new,
        bias_mean_new,
        bias_square_new,
    )


def solution(mesh):
    in_specs = (
        P("dp", None),
        P(None, ("dp", "blk")),
        P(None, "dp"),
        P(None, ("dp", "blk")),
        P("dp", "blk"),
        P("dp", "blk"),
        P("dp", "blk"),
        P("dp", "blk"),
        P("dp", "blk"),
        P("dp", "blk"),
        P(),
        P(),
        P(),
        P(),
        P(),
        P(),
    )
    out_specs = (
        P(("dp", "blk"), None),
        P(),
        P("dp", "blk"),
        P("dp", "blk"),
        P("dp", "blk"),
        P("dp", "blk"),
        P("dp", "blk"),
        P("dp", "blk"),
        P(),
        P(),
        P(),
        P(),
        P(),
        P(),
    )
    return jax.shard_map(
        functools.partial(on_device, n_dp=mesh.shape["dp"], n_blk=mesh.shape["blk"]),
        mesh=mesh,
        in_specs=in_specs,
        out_specs=out_specs,
        check_vma=False,
    )
```
